32 devices in a mesh: cam: 8 (over z, x), row: 4 (over y, core).
Axes of the slice: x: 2, y: 2, z: 4, core: 2. Of those that a mesh axis runs over, the one named last changes fastest.
Arguments:
- features_in: bfloat16 [8, 16, 128, 128], P('cam', 'row'), may hold values from -6 to 6
- conv_weight: bfloat16 [3, 3, 128, 128], replicated, may hold values from -0.1875 to 0.1875
- q_weight: bfloat16 [128, 128], replicated, may hold values from -0.5 to 0.5
- k_weight: bfloat16 [128, 128], replicated, may hold values from -0.5 to 0.5
- v_weight: bfloat16 [128, 128], replicated, may hold values from -0.5 to 0.5
- partners: int32 [8, 2], replicated, may hold values from 0 to 7, as said below
- band_widths: int32 [8, 2], replicated, may hold values from 1 to 3, as said below
- bands: int32 [8, 16, 2, 3], P('cam', 'row'), may hold values from 0 to 15, as said below
- grad_attended: bfloat16 [8, 16, 128, 128], P('cam', 'row'), may hold values from -6 to 6
Outputs:
- attended: bfloat16 [8, 16, 128, 128], P('cam', 'row')
- grad_features: bfloat16 [8, 16, 128, 128], P('cam', 'row')
The draws below stay inside these ranges and needn't reach their ends.
Inputs may be any that keep to these rules, and one draw needn't show every extreme that they name: `partners`: view c is camera c // 1 of sample c % 1; partner 0 of view c is view c - 1 or c - 2 and partner 1 is view c + 1 or c + 2, modulo 8, so both are cameras of the same sample next or next but one in the cyclic order of its 8 cameras. `band_widths`: some view and partner have 3 live slots and some have 1. `bands`: entries are block numbers of the partner view; a block is one image row, so the block number is the image row; the 3 entries of a list are distinct and lie in image rows 4 * s - 2 to 4 * (s + 1) + 1, where s is the query block's image row // 4.
All inputs are finite; a program needn't handle non-finite values.
Results may differ from the reference program's by a relative error of at most 0.011.
Values may be sent and summed in bfloat16 or wider, within the bound.
No kernel may reach another device: no remote copies, remote signals or barrier semaphores. Data moves between devices by JAX's collectives and lax.ppermute only.
A program may use at most 64 MiB of HBM per device.

```python
import jax
import jax.numpy as jnp
from jax import lax

CHANNELS = 128
WIDTH = 128
BLOCK = 128
ROWS_DEV = 4
MARGIN = 2
BAND = 3
SAMPLES = 1
VIEWS = 8
HEIGHT = 16
QBLOCKS = 16


def draw_features_in(key, part):
    noise_key = jax.random.fold_in(key, 41)
    shape = (VIEWS, HEIGHT, WIDTH, CHANNELS)
    return jax.random.truncated_normal(noise_key, -6.0, 6.0, shape, jnp.float32).astype(jnp.bfloat16)


def draw_partners(key, part):
    gap_key = jax.random.fold_in(key, 11)
    gaps = jax.random.randint(gap_key, (VIEWS, 2), 1, 3)
    cameras = jnp.arange(VIEWS, dtype=jnp.int32)
    before_cam = jnp.mod(cameras - gaps[:, 0] * SAMPLES, VIEWS)
    after_cam = jnp.mod(cameras + gaps[:, 1] * SAMPLES, VIEWS)
    return jnp.stack([before_cam, after_cam], axis=1).astype(jnp.int32)


def draw_band_widths(key, part):
    width_key = jax.random.fold_in(key, 21)
    pick_key = jax.random.fold_in(key, 22)
    flat = jax.random.randint(width_key, (2 * VIEWS,), 1, BAND + 1)
    chosen = jax.random.randint(pick_key, (), 0, 2 * VIEWS)
    places = jnp.arange(2 * VIEWS, dtype=jnp.int32)
    flat = jnp.where(places == chosen, BAND, flat)
    flat = jnp.where(places == jnp.mod(chosen + 1, 2 * VIEWS), 1, flat)
    return flat.reshape(VIEWS, 2).astype(jnp.int32)


def draw_bands(key, part):
    step_key = jax.random.fold_in(key, 31)
    start_key = jax.random.fold_in(key, 32)
    per_row = WIDTH // BLOCK
    block_ids = jnp.arange(QBLOCKS, dtype=jnp.int32)
    slab = block_ids // per_row // ROWS_DEV
    low = jnp.maximum(slab * ROWS_DEV - MARGIN, 0) * per_row
    high = jnp.minimum((slab + 1) * ROWS_DEV + MARGIN, HEIGHT) * per_row
    stride = jnp.where(jax.random.randint(step_key, (VIEWS, QBLOCKS, 2), 0, 2) == 1, per_row, 1)
    room = high[None, :, None] - low[None, :, None] - (BAND - 1) * stride
    start = low[None, :, None] + jnp.mod(jax.random.randint(start_key, (VIEWS, QBLOCKS, 2), 0, 1048576), room)
    offsets = jnp.arange(BAND, dtype=jnp.int32)
    return (start[..., None] + stride[..., None] * offsets).astype(jnp.int32)


def block_scale(key, extent, cuts, low, top_value):
    level, own = 1.0, jax.random.fold_in(key, 6)
    for dim, blocks in cuts:
        heights = jnp.exp(jax.random.uniform(jax.random.fold_in(own, dim), (blocks,), jnp.float32, low / len(cuts), top_value / len(cuts)))
        level = level * jnp.repeat(heights, extent[dim] // blocks).reshape([-1 if axis == dim else 1 for axis in range(len(extent))])
    return level


def normal_values(rng, dims, spread, bound, cuts=(), kind=jnp.bfloat16):
    drawn = jax.random.normal(rng, dims, jnp.float32) * spread
    if len(cuts) > 0:
        drawn = block_scale(rng, dims, cuts, -0.22, 0.18) * drawn
    return jnp.clip(drawn, min=-bound, max=bound).astype(kind)


def setup_inputs(seed: int = 0) -> dict:
    arg_keys = jax.random.split(jax.random.key(seed), 10)
    features_in = draw_features_in(jax.random.fold_in(arg_keys[9], 71), 0)
    conv_weight = normal_values(arg_keys[1], (3, 3, CHANNELS, CHANNELS), (9 * CHANNELS) ** -0.5, 0.1875)
    q_weight = normal_values(arg_keys[2], (CHANNELS, CHANNELS), CHANNELS ** -0.5, 0.5)
    k_weight = normal_values(arg_keys[3], (CHANNELS, CHANNELS), CHANNELS ** -0.5, 0.5)
    v_weight = normal_values(arg_keys[4], (CHANNELS, CHANNELS), CHANNELS ** -0.5, 0.5)
    partners = draw_partners(jax.random.fold_in(arg_keys[9], 71), 0)
    band_widths = draw_band_widths(jax.random.fold_in(arg_keys[9], 71), 0)
    bands = draw_bands(jax.random.fold_in(arg_keys[9], 71), 0)
    grad_attended = normal_values(arg_keys[8], (VIEWS, HEIGHT, WIDTH, CHANNELS), 1.0, 6.0, ((0, 8), (1, 4)))
    return {"features_in": features_in, "conv_weight": conv_weight, "q_weight": q_weight, "k_weight": k_weight, "v_weight": v_weight, "partners": partners, "band_widths": band_widths, "bands": bands, "grad_attended": grad_attended}


def reference(features_in, conv_weight, q_weight, k_weight, v_weight, partners, band_widths, bands, grad_attended):
    channels = CHANNELS
    inverse_square_root = channels ** -0.5
    high = lax.Precision.HIGHEST

    def project(image):
        hidden = lax.conv_general_dilated(image[None].astype(jnp.float32), conv_weight.astype(jnp.float32), (1, 1), ((1, 1), (1, 1)), dimension_numbers=("NHWC", "HWIO", "NHWC"), precision=high)[0]
        hidden = hidden.astype(jnp.bfloat16).reshape(HEIGHT * WIDTH, channels)
        queries = jnp.dot(hidden, q_weight, preferred_element_type=jnp.float32).astype(jnp.bfloat16)
        key_rows = jnp.dot(hidden, k_weight, preferred_element_type=jnp.float32).astype(jnp.bfloat16)
        value_rows = jnp.dot(hidden, v_weight, preferred_element_type=jnp.float32).astype(jnp.bfloat16)
        return queries, key_rows, value_rows

    all_q, all_k, all_v = lax.map(project, features_in)
    key_blocks = all_k.reshape(VIEWS, QBLOCKS, BLOCK, channels)
    value_blocks = all_v.reshape(VIEWS, QBLOCKS, BLOCK, channels)
    slots = jnp.arange(BAND, dtype=jnp.int32)
    back_weight = jnp.concatenate([k_weight, v_weight], axis=1).astype(jnp.float32).T
    query_back = q_weight.astype(jnp.float32).T
    key_count = 2 * BAND * BLOCK

    def one_view(camera, carry):
        attended, grad_acc = carry
        pair_row = partners[camera]
        widths_here = band_widths[camera]
        lists = bands[camera]
        key_rows = jnp.concatenate([key_blocks[pair_row[0]][lists[:, 0]], key_blocks[pair_row[1]][lists[:, 1]]], axis=1)
        key_rows = key_rows.reshape(QBLOCKS, key_count, channels).astype(jnp.float32)
        value_rows = jnp.concatenate([value_blocks[pair_row[0]][lists[:, 0]], value_blocks[pair_row[1]][lists[:, 1]]], axis=1)
        value_rows = value_rows.reshape(QBLOCKS, key_count, channels).astype(jnp.float32)
        live = jnp.repeat(jnp.concatenate([slots < widths_here[0], slots < widths_here[1]]), BLOCK)
        query_block = all_q[camera].reshape(QBLOCKS, BLOCK, channels).astype(jnp.float32)
        score_matrix = jnp.einsum("apx,anx->apn", query_block, key_rows) * inverse_square_root
        expo = jnp.where(live, jnp.exp(score_matrix), 0.0)
        probs = expo / jnp.sum(expo, axis=2, keepdims=True)
        probabilities_halfwidth = lax.optimization_barrier(probs.astype(jnp.bfloat16)).astype(jnp.float32)
        output_rows = jnp.einsum("zld,zdi->zli", probabilities_halfwidth, value_rows)
        attended = attended.at[camera].set(output_rows.astype(jnp.bfloat16))
        incoming_gradient = grad_attended[camera].reshape(QBLOCKS, BLOCK, channels).astype(jnp.float32)
        probability_gradient = jnp.einsum("apx,anx->apn", incoming_gradient, value_rows)
        delta = jnp.sum(probs * probability_gradient, axis=2, keepdims=True)
        score_gradient = lax.optimization_barrier((probs * (probability_gradient - delta)).astype(jnp.bfloat16)).astype(jnp.float32)
        query_gradient = jnp.einsum("zld,zdi->zli", score_gradient, key_rows) * inverse_square_root
        key_gradient = jnp.einsum("wds,wdm->wsm", score_gradient, query_block) * inverse_square_root
        value_gradient = jnp.einsum("wds,wdm->wsm", probabilities_halfwidth, incoming_gradient)
        grad_own = jnp.dot(query_gradient.reshape(-1, channels), query_back, precision=high)
        grad_acc = grad_acc.at[camera].add(grad_own.reshape(QBLOCKS, BLOCK, channels))
        pieces = jnp.dot(jnp.concatenate([key_gradient, value_gradient], axis=2).reshape(-1, 2 * channels), back_weight, precision=high)
        pieces = pieces.reshape(QBLOCKS, 2, BAND, BLOCK, channels)
        grad_acc = grad_acc.at[pair_row[0], lists[:, 0]].add(pieces[:, 0])
        grad_acc = grad_acc.at[pair_row[1], lists[:, 1]].add(pieces[:, 1])
        return attended, grad_acc

    start_att = jnp.zeros((VIEWS, QBLOCKS, BLOCK, channels), jnp.bfloat16)
    start_grad = jnp.zeros((VIEWS, QBLOCKS, BLOCK, channels), jnp.float32)
    attended, grad_acc = lax.fori_loop(0, VIEWS, one_view, (start_att, start_grad))
    attended = attended.reshape(VIEWS, HEIGHT, WIDTH, channels)
    grad_features = grad_acc.astype(jnp.bfloat16).reshape(VIEWS, HEIGHT, WIDTH, channels)
    return attended, grad_features
```

```python
import functools

import jax
import jax.numpy as jnp
from jax import lax
from jax.experimental import pallas as pl
from jax.experimental.pallas import tpu as pltpu
from jax.sharding import PartitionSpec as P

MARGIN = 2
BAND = 3
LOG2E = 1.4426950408889634


def from_behind(value, axis, steps):
    count = lax.axis_size(axis)
    pairs = [(source, (source + steps) % count) for source in range(count)]
    return lax.ppermute(value, axis, pairs)


def passed_along(block, axis, distance):
    devices = range(lax.axis_size(axis))
    route = [(i - distance, i) for i in devices if i - distance in devices]
    return lax.ppermute(block, axis, route)


def dot_nn(a, b):
    return lax.dot_general(a, b, (((1,), (0,)), ((), ())), preferred_element_type=jnp.float32)


def dot_nt(a, b):
    return lax.dot_general(a, b, (((1,), (1,)), ((), ())), preferred_element_type=jnp.float32)


def conv_rows(ref, out_rows, width, taps):
    count = out_rows * width
    stacked = jnp.concatenate([ref[i * width : i * width + count, :] for i in range(3)], axis=1)
    parts = dot_nn(stacked, taps)
    channels = parts.shape[1] // 3
    left, middle, right = (parts[:, i * channels : (i + 1) * channels] for i in range(3))
    column = lax.broadcasted_iota(jnp.int32, (count, channels), 0) % width
    total = middle + jnp.where(column == 0, 0.0, pltpu.roll(left, 1, 0))
    total = total + jnp.where(column == width - 1, 0.0, pltpu.roll(right, count - 1, 0))
    return total.astype(jnp.bfloat16)


def attention_kernel(
    scalars,
    own,
    near_left,
    far_left,
    near_right,
    far_right,
    above,
    below,
    conv_weight,
    q_weight,
    k_weight,
    v_weight,
    cotangent,
    attended,
    top,
    bottom,
    center,
    grad_own,
    image,
    kv,
    kv_t,
    acc,
    pair,
):
    rows, width, channels = own.shape
    halo = MARGIN + 1
    win = rows + 2 * MARGIN
    scale = channels**-0.5
    taps = jnp.concatenate(
        [
            jnp.concatenate([conv_weight[i, j] for j in range(3)], axis=1)
            for i in range(3)
        ],
        axis=0,
    )
    wq, wk, wv = q_weight[...], k_weight[...], v_weight[...]
    wkv = jnp.concatenate([wk, wv], axis=1)
    wkv_t = wkv.T

    image[0:width, :] = above[2 * halo]
    image[width : (rows + 1) * width, :] = own[...].reshape(rows * width, channels)
    image[(rows + 1) * width : (rows + 2) * width, :] = below[2 * halo]
    hidden = conv_rows(image, rows, width, taps)
    queries = dot_nn(hidden, wq).astype(jnp.bfloat16)
    pair[...] = jnp.zeros_like(pair)
    for b in range(rows):
        pair[b, 0:width, 0:channels] = queries[b * width : (b + 1) * width, :]
        pair[b, width : 2 * width, channels : 2 * channels] = cotangent[b]

    acc[...] = jnp.zeros_like(acc)
    for side, (near, far) in enumerate(((near_left, far_left), (near_right, far_right))):
        image[0 : halo * width, :] = above[side * halo : (side + 1) * halo].reshape(-1, channels)
        chosen = jnp.where(scalars[side] == 1, near[...], far[...])
        image[halo * width : (halo + rows) * width, :] = chosen.reshape(rows * width, channels)
        image[(halo + rows) * width :, :] = below[side * halo : (side + 1) * halo].reshape(
            -1, channels
        )
        hidden = conv_rows(image, win, width, taps)
        kv[side] = (
            dot_nn(hidden, wkv).astype(jnp.bfloat16).reshape(win, width, 2 * channels)
        )
        turned = dot_nt(wkv_t, hidden).astype(jnp.bfloat16)
        for r in range(win):
            kv_t[side, r] = turned[:, r * width : (r + 1) * width]

    grad_q = []
    for b in range(rows):
        places = [
            (side, scalars[2 + (b * 2 + side) * BAND + s], scalars[2 + rows * 2 * BAND + side * BAND + s])
            for side in range(2)
            for s in range(BAND)
        ]
        keys = jnp.concatenate([kv[side, at] for side, at, _ in places], axis=0)
        both = dot_nt(keys, pair[b])
        scores, grad_probs = both[:, :width], both[:, width:]
        expo = jnp.exp2(scores * (scale * LOG2E))
        expo = jnp.concatenate(
            [
                jnp.where(live == 1, expo[i * width : (i + 1) * width], 0.0)
                for i, (_, _, live) in enumerate(places)
            ],
            axis=0,
        )
        probs = expo * (1.0 / jnp.sum(expo, axis=0, keepdims=True))
        probs_bf = probs.astype(jnp.bfloat16)
        delta = jnp.sum(probs * grad_probs, axis=0, keepdims=True)
        grad_scores = (probs * (grad_probs - delta)).astype(jnp.bfloat16)
        keys_t = jnp.concatenate([kv_t[side, at] for side, at, _ in places], axis=1)
        attended[b] = dot_nn(keys_t[channels:], probs_bf).T.astype(jnp.bfloat16)
        grad_q.append(dot_nn(keys_t[:channels], grad_scores))
        terms = dot_nn(jnp.concatenate([grad_scores, probs_bf], axis=1), pair[b])
        for i, (side, at, _) in enumerate(places):
            acc[side, at] += terms[i * width : (i + 1) * width]

    turned = dot_nn(wq, (jnp.concatenate(grad_q, axis=1) * scale).astype(jnp.bfloat16))
    for b in range(rows):
        grad_own[b] = turned[:, b * width : (b + 1) * width].T
    for side in range(2):
        grads = acc[side].reshape(win * width, 2 * channels)
        grads = jnp.concatenate([grads[:, :channels] * scale, grads[:, channels:]], axis=1)
        back = dot_nt(grads.astype(jnp.bfloat16), wkv).reshape(win, width, channels)
        top[side * MARGIN : (side + 1) * MARGIN] = back[:MARGIN].astype(jnp.bfloat16)
        center[side] = back[MARGIN : MARGIN + rows]
        bottom[side * MARGIN : (side + 1) * MARGIN] = back[MARGIN + rows :].astype(jnp.bfloat16)


def attention(scalars, *arrays):
    own = arrays[0]
    rows, width, channels = own.shape
    win = rows + 2 * MARGIN
    vmem = pl.BlockSpec(memory_space=pltpu.VMEM)
    shape = jax.ShapeDtypeStruct
    return pl.pallas_call(
        attention_kernel,
        out_shape=(
            shape((rows, width, channels), jnp.bfloat16),
            shape((2 * MARGIN, width, channels), jnp.bfloat16),
            shape((2 * MARGIN, width, channels), jnp.bfloat16),
            shape((2, rows, width, channels), jnp.float32),
            shape((rows, width, channels), jnp.float32),
        ),
        in_specs=[pl.BlockSpec(memory_space=pltpu.SMEM)] + [vmem] * len(arrays),
        out_specs=(vmem,) * 5,
        scratch_shapes=[
            pltpu.VMEM(((win + 2) * width, channels), jnp.bfloat16),
            pltpu.VMEM((2, win, width, 2 * channels), jnp.bfloat16),
            pltpu.VMEM((2, win, 2 * channels, width), jnp.bfloat16),
            pltpu.VMEM((2, win, width, 2 * channels), jnp.float32),
            pltpu.VMEM((rows, 2 * width, 2 * channels), jnp.bfloat16),
        ],
        compiler_params=pltpu.CompilerParams(vmem_limit_bytes=40 * 1024 * 1024),
        cost_estimate=pl.CostEstimate(
            flops=2_000_000_000, bytes_accessed=4_000_000, transcendentals=400_000
        ),
    )(scalars, *arrays)


def local(
    features_in,
    conv_weight,
    q_weight,
    k_weight,
    v_weight,
    partners,
    band_widths,
    bands,
    grad_attended,
):
    image = features_in[0]
    rows = image.shape[0]
    halo = MARGIN + 1
    views = lax.axis_size("cam")
    samples = views // min(16, views)
    camera = lax.axis_index("cam")
    slab = lax.axis_index("row")

    near_left = from_behind(image, "cam", samples)
    near_right = from_behind(image, "cam", -samples)
    far_left = from_behind(image, "cam", 2 * samples)
    far_right = from_behind(image, "cam", -2 * samples)

    def uses(step, side):
        other = jnp.mod(camera + step, views)
        return partners[other, side] == camera

    close_left = partners[camera, 0] == jnp.mod(camera - samples, views)
    close_right = partners[camera, 1] == jnp.mod(camera + samples, views)
    widths_here = lax.dynamic_index_in_dim(band_widths, camera, 0, keepdims=False)
    live = jnp.arange(BAND, dtype=jnp.int32)[None, :] < widths_here[:, None]
    places = jnp.clip(bands[0] - (slab * rows - MARGIN), 0, rows + 2 * MARGIN - 1)
    scalars = jnp.concatenate(
        [
            jnp.stack([close_left, close_right]).astype(jnp.int32),
            places.reshape(-1),
            live.reshape(-1).astype(jnp.int32),
        ]
    )

    left = jnp.where(close_left, near_left, far_left)
    right = jnp.where(close_right, near_right, far_right)
    above = passed_along(
        jnp.concatenate([left[rows - halo :], right[rows - halo :], image[rows - 1 :]]), "row", 1
    )
    below = passed_along(jnp.concatenate([left[:halo], right[:halo], image[:1]]), "row", -1)

    attended, top, bottom, center, grad_own = attention(
        scalars,
        image,
        near_left,
        far_left,
        near_right,
        far_right,
        above,
        below,
        conv_weight,
        q_weight,
        k_weight,
        v_weight,
        grad_attended[0],
    )

    from_above = passed_along(bottom, "row", 1).reshape(2, MARGIN, *image.shape[1:])
    from_below = passed_along(top, "row", -1).reshape(2, MARGIN, *image.shape[1:])
    zeros = jnp.zeros((2, rows - MARGIN, *image.shape[1:]), jnp.float32)
    total = (
        center
        + jnp.concatenate([from_above.astype(jnp.float32), zeros], axis=1)
        + jnp.concatenate([zeros, from_below.astype(jnp.float32)], axis=1)
    ).astype(jnp.bfloat16)
    summed = grad_own
    for side, sign in ((0, -1), (1, 1)):
        for distance in (1, 2):
            step = sign * distance * samples
            came = from_behind(total[side], "cam", step)
            summed = summed + jnp.where(uses(-step, side), came.astype(jnp.float32), 0.0)
    return (attended[None], summed.astype(jnp.bfloat16)[None])


def solution(mesh):
    placed = (
        P("cam", "row", None, None),
        P(),
        P(),
        P(),
        P(),
        P(),
        P(),
        P("cam", "row", None, None),
        P("cam", "row", None, None),
    )
    return jax.shard_map(
        local,
        mesh=mesh,
        in_specs=placed,
        out_specs=(P("cam", "row", None, None), P("cam", "row", None, None)),
        check_vma=False,
    )
```

```python
import functools

import jax
import jax.numpy as jnp
from jax import lax
from jax.experimental import pallas as pl
from jax.experimental.pallas import tpu as pltpu
from jax.sharding import PartitionSpec as P

MARGIN = 2
BAND = 3
LOG2E = 1.4426950408889634


def from_behind(value, axis, steps):
    count = lax.axis_size(axis)
    pairs = [(source, (source + steps) % count) for source in range(count)]
    return lax.ppermute(value, axis, pairs)


def passed_along(block, axis, distance):
    devices = range(lax.axis_size(axis))
    route = [(i - distance, i) for i in devices if i - distance in devices]
    return lax.ppermute(block, axis, route)


def dot_nn(a, b):
    return lax.dot_general(a, b, (((1,), (0,)), ((), ())), preferred_element_type=jnp.float32)


def dot_nt(a, b):
    return lax.dot_general(a, b, (((1,), (1,)), ((), ())), preferred_element_type=jnp.float32)


def conv_rows(ref, out_rows, width, taps):
    count = out_rows * width
    stacked = jnp.concatenate([ref[i * width : i * width + count, :] for i in range(3)], axis=1)
    parts = dot_nn(stacked, taps)
    channels = parts.shape[1] // 3
    left, middle, right = (parts[:, i * channels : (i + 1) * channels] for i in range(3))
    column = lax.broadcasted_iota(jnp.int32, (count, channels), 0) % width
    total = middle + jnp.where(column == 0, 0.0, pltpu.roll(left, 1, 0))
    total = total + jnp.where(column == width - 1, 0.0, pltpu.roll(right, count - 1, 0))
    return total.astype(jnp.bfloat16)


def attention_kernel(
    scalars,
    own,
    left,
    right,
    above,
    below,
    conv_weight,
    q_weight,
    k_weight,
    v_weight,
    cotangent,
    attended,
    top,
    bottom,
    center,
    grad_own,
    image,
    kv,
    kv_t,
    acc,
    pair,
):
    rows, width, channels = own.shape
    halo = MARGIN + 1
    win = rows + 2 * MARGIN
    scale = channels**-0.5
    taps = jnp.concatenate(
        [
            jnp.concatenate([conv_weight[i, j] for j in range(3)], axis=1)
            for i in range(3)
        ],
        axis=0,
    )
    wq, wk, wv = q_weight[...], k_weight[...], v_weight[...]
    wkv = jnp.concatenate([wk, wv], axis=1)
    wkv_t = wkv.T

    image[0:width, :] = above[2 * halo]
    image[width : (rows + 1) * width, :] = own[...].reshape(rows * width, channels)
    image[(rows + 1) * width : (rows + 2) * width, :] = below[2 * halo]
    hidden = conv_rows(image, rows, width, taps)
    queries = dot_nn(hidden, wq).astype(jnp.bfloat16)
    pair[...] = jnp.zeros_like(pair)
    for b in range(rows):
        pair[b, 0:width, 0:channels] = queries[b * width : (b + 1) * width, :]
        pair[b, width : 2 * width, channels : 2 * channels] = cotangent[b]

    acc[...] = jnp.zeros_like(acc)
    for side, slab in enumerate((left, right)):
        image[0 : halo * width, :] = above[side * halo : (side + 1) * halo].reshape(-1, channels)
        image[halo * width : (halo + rows) * width, :] = slab[...].reshape(rows * width, channels)
        image[(halo + rows) * width :, :] = below[side * halo : (side + 1) * halo].reshape(
            -1, channels
        )
        hidden = conv_rows(image, win, width, taps)
        kv[side] = (
            dot_nn(hidden, wkv).astype(jnp.bfloat16).reshape(win, width, 2 * channels)
        )
        turned = dot_nt(wkv_t, hidden).astype(jnp.bfloat16)
        for r in range(win):
            kv_t[side, r] = turned[:, r * width : (r + 1) * width]

    grad_q = []
    for b in range(rows):
        places = [
            (side, scalars[2 + (b * 2 + side) * BAND + s], scalars[2 + rows * 2 * BAND + side * BAND + s])
            for side in range(2)
            for s in range(BAND)
        ]
        keys = jnp.concatenate([kv[side, at] for side, at, _ in places], axis=0)
        both = dot_nt(keys, pair[b])
        scores, grad_probs = both[:, :width], both[:, width:]
        expo = jnp.exp2(scores * (scale * LOG2E))
        expo = jnp.concatenate(
            [
                jnp.where(live == 1, expo[i * width : (i + 1) * width], 0.0)
                for i, (_, _, live) in enumerate(places)
            ],
            axis=0,
        )
        probs = expo * (1.0 / jnp.sum(expo, axis=0, keepdims=True))
        probs_bf = probs.astype(jnp.bfloat16)
        delta = jnp.sum(probs * grad_probs, axis=0, keepdims=True)
        grad_scores = (probs * (grad_probs - delta)).astype(jnp.bfloat16)
        keys_t = jnp.concatenate([kv_t[side, at] for side, at, _ in places], axis=1)
        attended[b] = dot_nn(keys_t[channels:], probs_bf).T.astype(jnp.bfloat16)
        grad_q.append(dot_nn(keys_t[:channels], grad_scores))
        terms = dot_nn(jnp.concatenate([grad_scores, probs_bf], axis=1), pair[b])
        for i, (side, at, _) in enumerate(places):
            acc[side, at] += terms[i * width : (i + 1) * width]

    turned = dot_nn(wq, (jnp.concatenate(grad_q, axis=1) * scale).astype(jnp.bfloat16))
    for b in range(rows):
        grad_own[b] = turned[:, b * width : (b + 1) * width].T
    for side in range(2):
        grads = acc[side].reshape(win * width, 2 * channels)
        grads = jnp.concatenate([grads[:, :channels] * scale, grads[:, channels:]], axis=1)
        back = dot_nt(grads.astype(jnp.bfloat16), wkv).reshape(win, width, channels)
        top[side * MARGIN : (side + 1) * MARGIN] = back[:MARGIN].astype(jnp.bfloat16)
        center[side] = back[MARGIN : MARGIN + rows]
        bottom[side * MARGIN : (side + 1) * MARGIN] = back[MARGIN + rows :].astype(jnp.bfloat16)


def attention(scalars, *arrays):
    own = arrays[0]
    rows, width, channels = own.shape
    win = rows + 2 * MARGIN
    vmem = pl.BlockSpec(memory_space=pltpu.VMEM)
    shape = jax.ShapeDtypeStruct
    return pl.pallas_call(
        attention_kernel,
        out_shape=(
            shape((rows, width, channels), jnp.bfloat16),
            shape((2 * MARGIN, width, channels), jnp.bfloat16),
            shape((2 * MARGIN, width, channels), jnp.bfloat16),
            shape((2, rows, width, channels), jnp.float32),
            shape((rows, width, channels), jnp.float32),
        ),
        in_specs=[pl.BlockSpec(memory_space=pltpu.SMEM)] + [vmem] * len(arrays),
        out_specs=(vmem,) * 5,
        scratch_shapes=[
            pltpu.VMEM(((win + 2) * width, channels), jnp.bfloat16),
            pltpu.VMEM((2, win, width, 2 * channels), jnp.bfloat16),
            pltpu.VMEM((2, win, 2 * channels, width), jnp.bfloat16),
            pltpu.VMEM((2, win, width, 2 * channels), jnp.float32),
            pltpu.VMEM((rows, 2 * width, 2 * channels), jnp.bfloat16),
        ],
        compiler_params=pltpu.CompilerParams(vmem_limit_bytes=40 * 1024 * 1024),
        cost_estimate=pl.CostEstimate(
            flops=2_000_000_000, bytes_accessed=4_000_000, transcendentals=400_000
        ),
    )(scalars, *arrays)


def local(
    features_in,
    conv_weight,
    q_weight,
    k_weight,
    v_weight,
    partners,
    band_widths,
    bands,
    grad_attended,
):
    image = features_in[0]
    rows = image.shape[0]
    halo = MARGIN + 1
    views = lax.axis_size("cam")
    samples = views // min(16, views)
    camera = lax.axis_index("cam")
    slab = lax.axis_index("row")

    gathered = lax.all_gather(image, "cam")

    def uses(step, side):
        other = jnp.mod(camera + step, views)
        return partners[other, side] == camera

    chosen = lax.dynamic_index_in_dim(partners, camera, 0, keepdims=False)
    widths_here = lax.dynamic_index_in_dim(band_widths, camera, 0, keepdims=False)
    live = jnp.arange(BAND, dtype=jnp.int32)[None, :] < widths_here[:, None]
    places = jnp.clip(bands[0] - (slab * rows - MARGIN), 0, rows + 2 * MARGIN - 1)
    scalars = jnp.concatenate(
        [
            chosen,
            places.reshape(-1),
            live.reshape(-1).astype(jnp.int32),
        ]
    )

    left = lax.dynamic_index_in_dim(gathered, chosen[0], 0, keepdims=False)
    right = lax.dynamic_index_in_dim(gathered, chosen[1], 0, keepdims=False)
    above = passed_along(
        jnp.concatenate([left[rows - halo :], right[rows - halo :], image[rows - 1 :]]), "row", 1
    )
    below = passed_along(jnp.concatenate([left[:halo], right[:halo], image[:1]]), "row", -1)

    attended, top, bottom, center, grad_own = attention(
        scalars,
        image,
        left,
        right,
        above,
        below,
        conv_weight,
        q_weight,
        k_weight,
        v_weight,
        grad_attended[0],
    )

    from_above = passed_along(bottom, "row", 1).reshape(2, MARGIN, *image.shape[1:])
    from_below = passed_along(top, "row", -1).reshape(2, MARGIN, *image.shape[1:])
    zeros = jnp.zeros((2, rows - MARGIN, *image.shape[1:]), jnp.float32)
    total = (
        center
        + jnp.concatenate([from_above.astype(jnp.float32), zeros], axis=1)
        + jnp.concatenate([zeros, from_below.astype(jnp.float32)], axis=1)
    ).astype(jnp.bfloat16)
    summed = grad_own
    for side, sign in ((0, -1), (1, 1)):
        for distance in (1, 2):
            step = sign * distance * samples
            came = from_behind(total[side], "cam", step)
            summed = summed + jnp.where(uses(-step, side), came.astype(jnp.float32), 0.0)
    return (attended[None], summed.astype(jnp.bfloat16)[None])


def solution(mesh):
    placed = (
        P("cam", "row", None, None),
        P(),
        P(),
        P(),
        P(),
        P(),
        P(),
        P("cam", "row", None, None),
        P("cam", "row", None, None),
    )
    return jax.shard_map(
        local,
        mesh=mesh,
        in_specs=placed,
        out_specs=(P("cam", "row", None, None), P("cam", "row", None, None)),
        check_vma=False,
    )
```

```python
import functools

import jax
import jax.numpy as jnp
from jax import lax
from jax.experimental import pallas as pl
from jax.experimental.pallas import tpu as pltpu
from jax.sharding import PartitionSpec as P

MARGIN = 2
BAND = 3
LOG2E = 1.4426950408889634


def from_behind(value, axis, steps):
    count = lax.axis_size(axis)
    pairs = [(source, (source + steps) % count) for source in range(count)]
    return lax.ppermute(value, axis, pairs)


def swapped(to_next, to_previous, axis):
    count = lax.axis_size(axis)
    odd = lax.rem(lax.axis_index(axis), 2) == 1
    results = []
    for first in (1, 0):
        pairs = [(i, i + 1) for i in range(first, count - 1, 2)]
        pairs = pairs + [(j, i) for i, j in pairs]
        sends_up = odd if first == 1 else ~odd
        results.append(lax.ppermute(jnp.where(sends_up, to_next, to_previous), axis, pairs))
    between, within = results
    from_previous = jnp.where(odd, within, between)
    from_next = jnp.where(odd, between, within)
    return from_previous, from_next


def dot_nn(a, b):
    return lax.dot_general(a, b, (((1,), (0,)), ((), ())), preferred_element_type=jnp.float32)


def dot_nt(a, b):
    return lax.dot_general(a, b, (((1,), (1,)), ((), ())), preferred_element_type=jnp.float32)


def conv_rows(ref, out_rows, width, taps):
    count = out_rows * width
    stacked = jnp.concatenate([ref[i * width : i * width + count, :] for i in range(3)], axis=1)
    parts = dot_nn(stacked, taps)
    channels = parts.shape[1] // 3
    left, middle, right = (parts[:, i * channels : (i + 1) * channels] for i in range(3))
    column = lax.broadcasted_iota(jnp.int32, (count, channels), 0) % width
    total = middle + jnp.where(column == 0, 0.0, pltpu.roll(left, 1, 0))
    total = total + jnp.where(column == width - 1, 0.0, pltpu.roll(right, count - 1, 0))
    return total.astype(jnp.bfloat16)


def attention_kernel(
    scalars,
    own,
    near_left,
    far_left,
    near_right,
    far_right,
    above,
    below,
    conv_weight,
    q_weight,
    k_weight,
    v_weight,
    cotangent,
    attended,
    top,
    bottom,
    center,
    grad_own,
    image,
    kv,
    kv_t,
    acc,
    pair,
):
    rows, width, channels = own.shape
    halo = MARGIN + 1
    win = rows + 2 * MARGIN
    scale = channels**-0.5
    taps = jnp.concatenate(
        [
            jnp.concatenate([conv_weight[i, j] for j in range(3)], axis=1)
            for i in range(3)
        ],
        axis=0,
    )
    wq, wk, wv = q_weight[...], k_weight[...], v_weight[...]
    wkv = jnp.concatenate([wk, wv], axis=1)
    wkv_t = wkv.T

    image[0:width, :] = above[2 * halo]
    image[width : (rows + 1) * width, :] = own[...].reshape(rows * width, channels)
    image[(rows + 1) * width : (rows + 2) * width, :] = below[2 * halo]
    hidden = conv_rows(image, rows, width, taps)
    queries = dot_nn(hidden, wq).astype(jnp.bfloat16)
    pair[...] = jnp.zeros_like(pair)
    for b in range(rows):
        pair[b, 0:width, 0:channels] = queries[b * width : (b + 1) * width, :]
        pair[b, width : 2 * width, channels : 2 * channels] = cotangent[b]

    acc[...] = jnp.zeros_like(acc)
    for side, (near, far) in enumerate(((near_left, far_left), (near_right, far_right))):
        image[0 : halo * width, :] = above[side * halo : (side + 1) * halo].reshape(-1, channels)
        chosen = jnp.where(scalars[side] == 1, near[...], far[...])
        image[halo * width : (halo + rows) * width, :] = chosen.reshape(rows * width, channels)
        image[(halo + rows) * width :, :] = below[side * halo : (side + 1) * halo].reshape(
            -1, channels
        )
        hidden = conv_rows(image, win, width, taps)
        kv[side] = (
            dot_nn(hidden, wkv).astype(jnp.bfloat16).reshape(win, width, 2 * channels)
        )
        turned = dot_nt(wkv_t, hidden).astype(jnp.bfloat16)
        for r in range(win):
            kv_t[side, r] = turned[:, r * width : (r + 1) * width]

    grad_q = []
    for b in range(rows):
        places = [
            (side, scalars[2 + (b * 2 + side) * BAND + s], scalars[2 + rows * 2 * BAND + side * BAND + s])
            for side in range(2)
            for s in range(BAND)
        ]
        keys = jnp.concatenate([kv[side, at] for side, at, _ in places], axis=0)
        both = dot_nt(keys, pair[b])
        scores, grad_probs = both[:, :width], both[:, width:]
        expo = jnp.exp2(scores * (scale * LOG2E))
        expo = jnp.concatenate(
            [
                jnp.where(live == 1, expo[i * width : (i + 1) * width], 0.0)
                for i, (_, _, live) in enumerate(places)
            ],
            axis=0,
        )
        probs = expo * (1.0 / jnp.sum(expo, axis=0, keepdims=True))
        probs_bf = probs.astype(jnp.bfloat16)
        delta = jnp.sum(probs * grad_probs, axis=0, keepdims=True)
        grad_scores = (probs * (grad_probs - delta)).astype(jnp.bfloat16)
        keys_t = jnp.concatenate([kv_t[side, at] for side, at, _ in places], axis=1)
        attended[b] = dot_nn(keys_t[channels:], probs_bf).T.astype(jnp.bfloat16)
        grad_q.append(dot_nn(keys_t[:channels], grad_scores))
        terms = dot_nn(jnp.concatenate([grad_scores, probs_bf], axis=1), pair[b])
        for i, (side, at, _) in enumerate(places):
            acc[side, at] += terms[i * width : (i + 1) * width]

    turned = dot_nn(wq, (jnp.concatenate(grad_q, axis=1) * scale).astype(jnp.bfloat16))
    for b in range(rows):
        grad_own[b] = turned[:, b * width : (b + 1) * width].T
    for side in range(2):
        grads = acc[side].reshape(win * width, 2 * channels)
        grads = jnp.concatenate([grads[:, :channels] * scale, grads[:, channels:]], axis=1)
        back = dot_nt(grads.astype(jnp.bfloat16), wkv).reshape(win, width, channels)
        top[side * MARGIN : (side + 1) * MARGIN] = back[:MARGIN].astype(jnp.bfloat16)
        center[side] = back[MARGIN : MARGIN + rows]
        bottom[side * MARGIN : (side + 1) * MARGIN] = back[MARGIN + rows :].astype(jnp.bfloat16)


def attention(scalars, *arrays):
    own = arrays[0]
    rows, width, channels = own.shape
    win = rows + 2 * MARGIN
    vmem = pl.BlockSpec(memory_space=pltpu.VMEM)
    shape = jax.ShapeDtypeStruct
    return pl.pallas_call(
        attention_kernel,
        out_shape=(
            shape((rows, width, channels), jnp.bfloat16),
            shape((2 * MARGIN, width, channels), jnp.bfloat16),
            shape((2 * MARGIN, width, channels), jnp.bfloat16),
            shape((2, rows, width, channels), jnp.float32),
            shape((rows, width, channels), jnp.float32),
        ),
        in_specs=[pl.BlockSpec(memory_space=pltpu.SMEM)] + [vmem] * len(arrays),
        out_specs=(vmem,) * 5,
        scratch_shapes=[
            pltpu.VMEM(((win + 2) * width, channels), jnp.bfloat16),
            pltpu.VMEM((2, win, width, 2 * channels), jnp.bfloat16),
            pltpu.VMEM((2, win, 2 * channels, width), jnp.bfloat16),
            pltpu.VMEM((2, win, width, 2 * channels), jnp.float32),
            pltpu.VMEM((rows, 2 * width, 2 * channels), jnp.bfloat16),
        ],
        compiler_params=pltpu.CompilerParams(vmem_limit_bytes=40 * 1024 * 1024),
        cost_estimate=pl.CostEstimate(
            flops=2_000_000_000, bytes_accessed=4_000_000, transcendentals=400_000
        ),
    )(scalars, *arrays)


def local(
    features_in,
    conv_weight,
    q_weight,
    k_weight,
    v_weight,
    partners,
    band_widths,
    bands,
    grad_attended,
):
    image = features_in[0]
    rows = image.shape[0]
    halo = MARGIN + 1
    views = lax.axis_size("cam")
    samples = views // min(16, views)
    camera = lax.axis_index("cam")
    slab = lax.axis_index("row")

    near_left = from_behind(image, "cam", samples)
    near_right = from_behind(image, "cam", -samples)
    far_left = from_behind(image, "cam", 2 * samples)
    far_right = from_behind(image, "cam", -2 * samples)

    def uses(step, side):
        other = jnp.mod(camera + step, views)
        return partners[other, side] == camera

    close_left = partners[camera, 0] == jnp.mod(camera - samples, views)
    close_right = partners[camera, 1] == jnp.mod(camera + samples, views)
    widths_here = lax.dynamic_index_in_dim(band_widths, camera, 0, keepdims=False)
    live = jnp.arange(BAND, dtype=jnp.int32)[None, :] < widths_here[:, None]
    places = jnp.clip(bands[0] - (slab * rows - MARGIN), 0, rows + 2 * MARGIN - 1)
    scalars = jnp.concatenate(
        [
            jnp.stack([close_left, close_right]).astype(jnp.int32),
            places.reshape(-1),
            live.reshape(-1).astype(jnp.int32),
        ]
    )

    left = jnp.where(close_left, near_left, far_left)
    right = jnp.where(close_right, near_right, far_right)
    above, below = swapped(
        jnp.concatenate([left[rows - halo :], right[rows - halo :], image[rows - 1 :]]),
        jnp.concatenate([left[:halo], right[:halo], image[:1]]),
        "row",
    )

    attended, top, bottom, center, grad_own = attention(
        scalars,
        image,
        near_left,
        far_left,
        near_right,
        far_right,
        above,
        below,
        conv_weight,
        q_weight,
        k_weight,
        v_weight,
        grad_attended[0],
    )

    from_above, from_below = (
        part.reshape(2, MARGIN, *image.shape[1:]) for part in swapped(bottom, top, "row")
    )
    zeros = jnp.zeros((2, rows - MARGIN, *image.shape[1:]), jnp.float32)
    total = (
        center
        + jnp.concatenate([from_above.astype(jnp.float32), zeros], axis=1)
        + jnp.concatenate([zeros, from_below.astype(jnp.float32)], axis=1)
    ).astype(jnp.bfloat16)
    summed = grad_own
    for side, sign in ((0, -1), (1, 1)):
        for distance in (1, 2):
            step = sign * distance * samples
            came = from_behind(total[side], "cam", step)
            summed = summed + jnp.where(uses(-step, side), came.astype(jnp.float32), 0.0)
    return (attended[None], summed.astype(jnp.bfloat16)[None])


def solution(mesh):
    placed = (
        P("cam", "row", None, None),
        P(),
        P(),
        P(),
        P(),
        P(),
        P(),
        P("cam", "row", None, None),
        P("cam", "row", None, None),
    )
    return jax.shard_map(
        local,
        mesh=mesh,
        in_specs=placed,
        out_specs=(P("cam", "row", None, None), P("cam", "row", None, None)),
        check_vma=False,
    )
```

```python
import jax
import jax.numpy as jnp
from jax import lax
from jax.experimental import pallas as pl
from jax.experimental.pallas import tpu as pltpu
from jax.sharding import PartitionSpec as P

MARGIN = 2
BAND = 3
LOG2E = 1.4426950408889634


def from_behind(value, axis, steps):
    count = lax.axis_size(axis)
    pairs = [(source, (source + steps) % count) for source in range(count)]
    return lax.ppermute(value, axis, pairs)


def swapped(to_next, to_previous, axis):
    count = lax.axis_size(axis)
    odd = lax.rem(lax.axis_index(axis), 2) == 1
    results = []
    for first in (1, 0):
        pairs = [(i, i + 1) for i in range(first, count - 1, 2)]
        pairs = pairs + [(j, i) for i, j in pairs]
        sends_up = odd if first == 1 else ~odd
        results.append(lax.ppermute(jnp.where(sends_up, to_next, to_previous), axis, pairs))
    return results


def margins_of(odd, between, within):
    return jnp.where(odd, within, between), jnp.where(odd, between, within)


def dot_nn(a, b):
    return lax.dot_general(a, b, (((1,), (0,)), ((), ())), preferred_element_type=jnp.float32)


def dot_nt(a, b):
    return lax.dot_general(a, b, (((1,), (1,)), ((), ())), preferred_element_type=jnp.float32)


def stacked_taps(conv_weight):
    return jnp.concatenate(
        [jnp.concatenate([conv_weight[i, j] for j in range(3)], axis=1) for i in range(3)], axis=0
    )


def conv_rows(image, work, out_rows, width, taps):
    count = out_rows * width
    channels = taps.shape[1] // 3
    stacked = jnp.concatenate([image[i * width : i * width + count, :] for i in range(3)], axis=1)
    work[8 : 8 + count, :] = dot_nn(stacked, taps)
    none = jnp.zeros((1, channels), jnp.float32)
    for i in range(out_rows + 1):
        work[7 + i * width : 8 + i * width, :channels] = none
        work[8 + i * width : 9 + i * width, 2 * channels :] = none
    total = work[8 : 8 + count, channels : 2 * channels]
    total = total + work[7 : 7 + count, :channels]
    total = total + work[9 : 9 + count, 2 * channels :]
    return total.astype(jnp.bfloat16)


def side_keys(slab, odd, between, within, image, work, taps, wkv, kv, kv_t):
    rows, width, channels = slab.shape
    halo = MARGIN + 1
    win = rows + 2 * MARGIN
    above, below = margins_of(odd, between[0:halo], within[0:halo])
    image[0 : halo * width, :] = above.reshape(halo * width, channels)
    image[halo * width : (halo + rows) * width, :] = slab.reshape(rows * width, channels)
    image[(halo + rows) * width :, :] = below.reshape(halo * width, channels)
    hidden = conv_rows(image, work, win, width, taps)
    kv[...] = dot_nn(hidden, wkv).astype(jnp.bfloat16).reshape(win, width, 2 * channels)
    turned = dot_nt(wkv.T, hidden).astype(jnp.bfloat16)
    for r in range(win):
        kv_t[r] = turned[:, r * width : (r + 1) * width]


def places_of(scalars, rows, b, side):
    return [
        (
            scalars[2 + (b * 2 + side) * BAND + s],
            scalars[2 + rows * 2 * BAND + side * BAND + s] == 1,
        )
        for s in range(BAND)
    ]


def side_scores(places, kv, pair_b, width, channels):
    keys = jnp.concatenate([kv[at] for at, _ in places], axis=0)
    both = dot_nt(keys, pair_b)
    expo = jnp.exp2(both[:, :width] * (channels**-0.5 * LOG2E))
    expo = jnp.concatenate(
        [
            jnp.where(live, expo[i * width : (i + 1) * width], 0.0)
            for i, (_, live) in enumerate(places)
        ],
        axis=0,
    )
    return expo, both[:, width:]


def first_kernel(
    scalars,
    own,
    slab,
    within,
    between,
    conv_weight,
    q_weight,
    k_weight,
    v_weight,
    cotangent,
    pair,
    kv,
    kv_t,
    expo,
    grad_probs,
    image,
    work,
):
    rows, width, channels = own.shape
    halo = MARGIN + 1
    taps = stacked_taps(conv_weight)
    wkv = jnp.concatenate([k_weight[...], v_weight[...]], axis=1)

    odd = scalars[0] == 1
    above, below = margins_of(odd, between[halo], within[halo])
    image[0:width, :] = above
    image[width : (rows + 1) * width, :] = own[...].reshape(rows * width, channels)
    image[(rows + 1) * width : (rows + 2) * width, :] = below
    hidden = conv_rows(image, work, rows, width, taps)
    queries = dot_nn(hidden, q_weight[...]).astype(jnp.bfloat16)
    pair[...] = jnp.zeros_like(pair)
    for b in range(rows):
        pair[b, 0:width, 0:channels] = queries[b * width : (b + 1) * width, :]
        pair[b, width : 2 * width, channels : 2 * channels] = cotangent[b]

    side_keys(slab[...], odd, between, within, image, work, taps, wkv, kv, kv_t)
    for b in range(rows):
        expo[b], grad_probs[b] = side_scores(
            places_of(scalars, rows, b, 1), kv, pair[b], width, channels
        )


def second_kernel(
    scalars,
    near,
    far,
    within,
    between,
    conv_weight,
    q_weight,
    k_weight,
    v_weight,
    pair,
    first_kv_t,
    first_expo,
    first_grad_probs,
    attended,
    top,
    bottom,
    center,
    grad_own,
    image,
    work,
    kv,
    kv_t,
    acc,
):
    rows, width, channels = near.shape
    win = rows + 2 * MARGIN
    scale = channels**-0.5
    taps = stacked_taps(conv_weight)
    wkv = jnp.concatenate([k_weight[...], v_weight[...]], axis=1)
    acc[...] = jnp.zeros_like(acc)
    slab = jnp.where(scalars[1] == 1, near[...], far[...])
    side_keys(slab, scalars[0] == 1, between, within, image, work, taps, wkv, kv, kv_t)

    grad_q = []
    for b in range(rows):
        places = [places_of(scalars, rows, b, side) for side in range(2)]
        expo, grad_probs = side_scores(places[0], kv, pair[b], width, channels)
        expo = jnp.concatenate([expo, first_expo[b]], axis=0)
        grad_probs = jnp.concatenate([grad_probs, first_grad_probs[b]], axis=0)
        probs = expo * (1.0 / jnp.sum(expo, axis=0, keepdims=True))
        probs_bf = probs.astype(jnp.bfloat16)
        delta = jnp.sum(probs * grad_probs, axis=0, keepdims=True)
        grad_scores = (probs * (grad_probs - delta)).astype(jnp.bfloat16)
        keys_t = jnp.concatenate(
            [kv_t[at] for at, _ in places[0]] + [first_kv_t[at] for at, _ in places[1]], axis=1
        )
        attended[b] = dot_nn(keys_t[channels:], probs_bf).T.astype(jnp.bfloat16)
        grad_q.append(dot_nn(keys_t[:channels], grad_scores))
        terms = dot_nn(jnp.concatenate([grad_scores, probs_bf], axis=1), pair[b])
        for side in range(2):
            for s, (at, _) in enumerate(places[side]):
                i = side * BAND + s
                acc[side, at] += terms[i * width : (i + 1) * width]

    turned = dot_nn(q_weight[...], (jnp.concatenate(grad_q, axis=1) * scale).astype(jnp.bfloat16))
    for b in range(rows):
        grad_own[b] = turned[:, b * width : (b + 1) * width].T
    for side in range(2):
        grads = acc[side].reshape(win * width, 2 * channels)
        grads = jnp.concatenate([grads[:, :channels] * scale, grads[:, channels:]], axis=1)
        back = dot_nt(grads.astype(jnp.bfloat16), wkv).reshape(win, width, channels)
        top[side * MARGIN : (side + 1) * MARGIN] = back[:MARGIN].astype(jnp.bfloat16)
        center[side] = back[MARGIN : MARGIN + rows]
        bottom[side * MARGIN : (side + 1) * MARGIN] = back[MARGIN + rows :].astype(jnp.bfloat16)


def slab_kernel(scalars, center, within, between, left, right):
    rows, width, channels = left.shape
    above, below = margins_of(scalars[0] == 1, between[...], within[...])
    for side, out in enumerate((left, right)):
        for r in range(rows):
            total = center[side, r]
            if r < MARGIN:
                total = total + above[side * MARGIN + r].astype(jnp.float32)
            if r >= rows - MARGIN:
                total = total + below[side * MARGIN + r - rows + MARGIN].astype(jnp.float32)
            out[r] = total.astype(jnp.bfloat16)


def on_device(kernel, out_shape, scratch, flops, *arrays):
    vmem = pl.BlockSpec(memory_space=pltpu.VMEM)
    return pl.pallas_call(
        kernel,
        out_shape=tuple(jax.ShapeDtypeStruct(*one) for one in out_shape),
        in_specs=[pl.BlockSpec(memory_space=pltpu.SMEM)] + [vmem] * (len(arrays) - 1),
        out_specs=(vmem,) * len(out_shape),
        scratch_shapes=[pltpu.VMEM(*one) for one in scratch],
        compiler_params=pltpu.CompilerParams(vmem_limit_bytes=32 * 1024 * 1024),
        cost_estimate=pl.CostEstimate(
            flops=flops, bytes_accessed=flops // 1000, transcendentals=0
        ),
    )(*arrays)


def local(
    features_in,
    conv_weight,
    q_weight,
    k_weight,
    v_weight,
    partners,
    band_widths,
    bands,
    grad_attended,
):
    image = features_in[0]
    rows = image.shape[0]
    halo = MARGIN + 1
    views = lax.axis_size("cam")
    samples = views // min(16, views)
    camera = lax.axis_index("cam")
    slab = lax.axis_index("row")

    near_left = from_behind(image, "cam", samples)
    near_right = from_behind(image, "cam", -samples)
    far_left = from_behind(image, "cam", 2 * samples)
    far_right = from_behind(image, "cam", -2 * samples)

    def uses(step, side):
        other = jnp.mod(camera + step, views)
        return partners[other, side] == camera

    close_left = partners[camera, 0] == jnp.mod(camera - samples, views)
    close_right = partners[camera, 1] == jnp.mod(camera + samples, views)
    widths_here = lax.dynamic_index_in_dim(band_widths, camera, 0, keepdims=False)
    live = jnp.arange(BAND, dtype=jnp.int32)[None, :] < widths_here[:, None]
    places = jnp.clip(bands[0] - (slab * rows - MARGIN), 0, rows + 2 * MARGIN - 1)
    scalars = jnp.concatenate(
        [
            jnp.mod(slab, 2).reshape(1),
            close_left.astype(jnp.int32).reshape(1),
            places.reshape(-1),
            live.reshape(-1).astype(jnp.int32),
        ]
    )

    right = jnp.where(close_right, near_right, far_right)
    between, within = swapped(
        jnp.concatenate([right[rows - halo :], image[rows - 1 :]]),
        jnp.concatenate([right[:halo], image[:1]]),
        "row",
    )
    width, channels = image.shape[1:]
    win = rows + 2 * MARGIN
    half, full = jnp.bfloat16, jnp.float32
    conv_scratch = [
        (((win + 2) * width, channels), half),
        ((win * width + 16, 3 * channels), full),
    ]
    pair, _, first_kv_t, first_expo, first_grad_probs = on_device(
        first_kernel,
        [
            ((rows, 2 * width, 2 * channels), half),
            ((win, width, 2 * channels), half),
            ((win, 2 * channels, width), half),
            ((rows, BAND * width, width), full),
            ((rows, BAND * width, width), full),
        ],
        conv_scratch,
        1_000_000,
        scalars,
        image,
        right,
        within,
        between,
        conv_weight,
        q_weight,
        k_weight,
        v_weight,
        grad_attended[0],
    )
    close_left, _ = lax.optimization_barrier((close_left, right))
    left = jnp.where(close_left, near_left, far_left)
    between, within = swapped(left[rows - halo :], left[:halo], "row")
    attended, top, bottom, center, grad_own = on_device(
        second_kernel,
        [
            ((rows, width, channels), half),
            ((2 * MARGIN, width, channels), half),
            ((2 * MARGIN, width, channels), half),
            ((2, rows, width, channels), full),
            ((rows, width, channels), full),
        ],
        conv_scratch
        + [
            ((win, width, 2 * channels), half),
            ((win, 2 * channels, width), half),
            ((2, win, width, 2 * channels), full),
        ],
        1_500_000_000,
        scalars,
        near_left,
        far_left,
        within,
        between,
        conv_weight,
        q_weight,
        k_weight,
        v_weight,
        pair,
        first_kv_t,
        first_expo,
        first_grad_probs,
    )

    between, within = swapped(bottom, top, "row")
    total = on_device(
        slab_kernel,
        [(image.shape, half)] * 2,
        [],
        1_000_000,
        scalars,
        center,
        within,
        between,
    )
    summed = grad_own
    for side, sign in ((0, -1), (1, 1)):
        for distance in (1, 2):
            step = sign * distance * samples
            came = from_behind(total[side], "cam", step)
            summed = summed + jnp.where(uses(-step, side), came.astype(jnp.float32), 0.0)
    return (attended[None], summed.astype(jnp.bfloat16)[None])


def solution(mesh):
    placed = (
        P("cam", "row", None, None),
        P(),
        P(),
        P(),
        P(),
        P(),
        P(),
        P("cam", "row", None, None),
        P("cam", "row", None, None),
    )
    return jax.shard_map(
        local,
        mesh=mesh,
        in_specs=placed,
        out_specs=(P("cam", "row", None, None), P("cam", "row", None, None)),
        check_vma=False,
    )
```

```python
import jax
import jax.numpy as jnp
from jax import lax
from jax.experimental import pallas as pl
from jax.experimental.pallas import tpu as pltpu
from jax.sharding import PartitionSpec as P

MARGIN = 2
BAND = 3
LOG2E = 1.4426950408889634


def swapped(to_next, to_previous, axis):
    count = lax.axis_size(axis)
    odd = lax.rem(lax.axis_index(axis), 2) == 1
    results = []
    for first in (1, 0):
        pairs = [(i, i + 1) for i in range(first, count - 1, 2)]
        pairs = pairs + [(j, i) for i, j in pairs]
        sends_up = odd if first == 1 else ~odd
        results.append(lax.ppermute(jnp.where(sends_up, to_next, to_previous), axis, pairs))
    return results


def margins_of(odd, between, within):
    return jnp.where(odd, within, between), jnp.where(odd, between, within)


def dot_nn(a, b):
    return lax.dot_general(a, b, (((1,), (0,)), ((), ())), preferred_element_type=jnp.float32)


def dot_nt(a, b):
    return lax.dot_general(a, b, (((1,), (1,)), ((), ())), preferred_element_type=jnp.float32)


def stacked_taps(conv_weight):
    return jnp.concatenate(
        [jnp.concatenate([conv_weight[i, j] for j in range(3)], axis=1) for i in range(3)], axis=0
    )


def conv_rows(image, work, out_rows, width, taps):
    count = out_rows * width
    channels = taps.shape[1] // 3
    stacked = jnp.concatenate([image[i * width : i * width + count, :] for i in range(3)], axis=1)
    work[8 : 8 + count, :] = dot_nn(stacked, taps)
    none = jnp.zeros((1, channels), jnp.float32)
    for i in range(out_rows + 1):
        work[7 + i * width : 8 + i * width, :channels] = none
        work[8 + i * width : 9 + i * width, 2 * channels :] = none
    total = work[8 : 8 + count, channels : 2 * channels]
    total = total + work[7 : 7 + count, :channels]
    total = total + work[9 : 9 + count, 2 * channels :]
    return total.astype(jnp.bfloat16)


def side_keys(slab, odd, between, within, image, work, taps, wkv, kv, kv_t):
    rows, width, channels = slab.shape
    halo = MARGIN + 1
    win = rows + 2 * MARGIN
    above, below = margins_of(odd, between[0:halo], within[0:halo])
    image[0 : halo * width, :] = above.reshape(halo * width, channels)
    image[halo * width : (halo + rows) * width, :] = slab.reshape(rows * width, channels)
    image[(halo + rows) * width :, :] = below.reshape(halo * width, channels)
    hidden = conv_rows(image, work, win, width, taps)
    kv[...] = dot_nn(hidden, wkv).astype(jnp.bfloat16).reshape(win, width, 2 * channels)
    turned = dot_nt(wkv.T, hidden).astype(jnp.bfloat16)
    for r in range(win):
        kv_t[r] = turned[:, r * width : (r + 1) * width]


def places_of(scalars, rows, b, side):
    return [
        (
            scalars[1 + (b * 2 + side) * BAND + s],
            scalars[1 + rows * 2 * BAND + side * BAND + s] == 1,
        )
        for s in range(BAND)
    ]


def side_scores(places, kv, pair_b, width, channels):
    keys = jnp.concatenate([kv[at] for at, _ in places], axis=0)
    both = dot_nt(keys, pair_b)
    expo = jnp.exp2(both[:, :width] * (channels**-0.5 * LOG2E))
    expo = jnp.concatenate(
        [
            jnp.where(live, expo[i * width : (i + 1) * width], 0.0)
            for i, (_, live) in enumerate(places)
        ],
        axis=0,
    )
    return expo, both[:, width:]


def first_kernel(
    scalars,
    own,
    slab,
    within,
    between,
    conv_weight,
    q_weight,
    k_weight,
    v_weight,
    cotangent,
    pair,
    kv_t,
    expo,
    grad_probs,
    image,
    work,
    kv,
):
    rows, width, channels = own.shape
    halo = MARGIN + 1
    taps = stacked_taps(conv_weight)
    wkv = jnp.concatenate([k_weight[...], v_weight[...]], axis=1)

    odd = scalars[0] == 1
    above, below = margins_of(odd, between[halo], within[halo])
    image[0:width, :] = above
    image[width : (rows + 1) * width, :] = own[...].reshape(rows * width, channels)
    image[(rows + 1) * width : (rows + 2) * width, :] = below
    hidden = conv_rows(image, work, rows, width, taps)
    queries = dot_nn(hidden, q_weight[...]).astype(jnp.bfloat16)
    pair[...] = jnp.zeros_like(pair)
    for b in range(rows):
        pair[b, 0:width, 0:channels] = queries[b * width : (b + 1) * width, :]
        pair[b, width : 2 * width, channels : 2 * channels] = cotangent[b]

    side_keys(slab[...], odd, between, within, image, work, taps, wkv, kv, kv_t)
    for b in range(rows):
        expo[b], grad_probs[b] = side_scores(
            places_of(scalars, rows, b, 1), kv, pair[b], width, channels
        )


def second_kernel(
    scalars,
    pair,
    slab,
    within,
    between,
    conv_weight,
    q_weight,
    k_weight,
    v_weight,
    first_kv_t,
    first_expo,
    first_grad_probs,
    attended,
    top,
    bottom,
    center,
    grad_own,
    image,
    work,
    kv,
    kv_t,
    acc,
):
    rows, width, channels = slab.shape
    win = rows + 2 * MARGIN
    scale = channels**-0.5
    taps = stacked_taps(conv_weight)
    wkv = jnp.concatenate([k_weight[...], v_weight[...]], axis=1)
    acc[...] = jnp.zeros_like(acc)
    side_keys(slab[...], scalars[0] == 1, between, within, image, work, taps, wkv, kv, kv_t)

    grad_q = []
    for b in range(rows):
        places = [places_of(scalars, rows, b, side) for side in range(2)]
        expo, grad_probs = side_scores(places[0], kv, pair[b], width, channels)
        expo = jnp.concatenate([expo, first_expo[b]], axis=0)
        grad_probs = jnp.concatenate([grad_probs, first_grad_probs[b]], axis=0)
        probs = expo * (1.0 / jnp.sum(expo, axis=0, keepdims=True))
        probs_bf = probs.astype(jnp.bfloat16)
        delta = jnp.sum(probs * grad_probs, axis=0, keepdims=True)
        grad_scores = (probs * (grad_probs - delta)).astype(jnp.bfloat16)
        keys_t = jnp.concatenate(
            [kv_t[at] for at, _ in places[0]] + [first_kv_t[at] for at, _ in places[1]], axis=1
        )
        attended[b] = dot_nn(keys_t[channels:], probs_bf).T.astype(jnp.bfloat16)
        grad_q.append(dot_nn(keys_t[:channels], grad_scores))
        terms = dot_nn(jnp.concatenate([grad_scores, probs_bf], axis=1), pair[b])
        for side in range(2):
            for s, (at, _) in enumerate(places[side]):
                i = side * BAND + s
                acc[side, at] += terms[i * width : (i + 1) * width]

    turned = dot_nn(q_weight[...], (jnp.concatenate(grad_q, axis=1) * scale).astype(jnp.bfloat16))
    for b in range(rows):
        grad_own[b] = turned[:, b * width : (b + 1) * width].T
    for side in range(2):
        grads = acc[side].reshape(win * width, 2 * channels)
        grads = jnp.concatenate([grads[:, :channels] * scale, grads[:, channels:]], axis=1)
        back = dot_nt(grads.astype(jnp.bfloat16), wkv).reshape(win, width, channels)
        top[side * MARGIN : (side + 1) * MARGIN] = back[:MARGIN].astype(jnp.bfloat16)
        center[side] = back[MARGIN : MARGIN + rows]
        bottom[side * MARGIN : (side + 1) * MARGIN] = back[MARGIN + rows :].astype(jnp.bfloat16)


def slab_kernel(scalars, center, within, between, left, right):
    rows, width, channels = left.shape
    above, below = margins_of(scalars[0] == 1, between[...], within[...])
    for side, out in enumerate((left, right)):
        for r in range(rows):
            total = center[side, r]
            if r < MARGIN:
                total = total + above[side * MARGIN + r].astype(jnp.float32)
            if r >= rows - MARGIN:
                total = total + below[side * MARGIN + r - rows + MARGIN].astype(jnp.float32)
            out[r] = total.astype(jnp.bfloat16)


def on_device(kernel, out_shape, scratch, flops, *arrays):
    vmem = pl.BlockSpec(memory_space=pltpu.VMEM)
    return pl.pallas_call(
        kernel,
        out_shape=tuple(jax.ShapeDtypeStruct(*one) for one in out_shape),
        in_specs=[pl.BlockSpec(memory_space=pltpu.SMEM)] + [vmem] * (len(arrays) - 1),
        out_specs=(vmem,) * len(out_shape),
        scratch_shapes=[pltpu.VMEM(*one) for one in scratch],
        compiler_params=pltpu.CompilerParams(vmem_limit_bytes=32 * 1024 * 1024),
        cost_estimate=pl.CostEstimate(
            flops=flops, bytes_accessed=flops // 1000, transcendentals=0
        ),
    )(*arrays)


def local(
    features_in,
    conv_weight,
    q_weight,
    k_weight,
    v_weight,
    partners,
    band_widths,
    bands,
    grad_attended,
):
    image = features_in[0]
    rows = image.shape[0]
    halo = MARGIN + 1
    views = lax.axis_size("cam")
    samples = views // min(16, views)
    camera = lax.axis_index("cam")
    slab = lax.axis_index("row")

    ring = views // samples
    odd_place = lax.rem(lax.div(camera, samples), 2) == 1
    sign = jnp.where(odd_place, -1, 1)

    def routed(value, evens, odds):
        pairs = []
        for c in range(views):
            step = odds if (c // samples) % 2 else evens
            pairs.append((c, (c // samples + step) % ring * samples + c % samples))
        return lax.ppermute(value, "cam", pairs)

    def is_near(steps, first):
        other = jnp.mod(camera + steps * samples, views)
        side = jnp.where(odd_place, 1 - first, first)
        gap = jnp.where(side == 1, samples, -samples)
        return partners[other, side] == jnp.mod(other + gap, views)

    first_near = is_near(0, 1)
    second_near_on = is_near(2 * sign, 0)
    first_near_back = is_near(-2 * sign, 1)

    pair_slab = routed(image, 1, -1)
    far_slab = routed(image, -2, 2)
    passed_on = jnp.where(second_near_on, pair_slab, image)
    second_slab = routed(passed_on, 2, -2)
    far_slab, _ = lax.optimization_barrier((far_slab, passed_on))
    first_slab = jnp.where(~first_near, far_slab, pair_slab)

    widths_here = lax.dynamic_index_in_dim(band_widths, camera, 0, keepdims=False)
    live = jnp.arange(BAND, dtype=jnp.int32)[None, :] < widths_here[:, None]
    places = jnp.clip(bands[0] - (slab * rows - MARGIN), 0, rows + 2 * MARGIN - 1)
    live = jnp.where(odd_place, live[::-1], live)
    places = jnp.where(odd_place, places[:, ::-1], places)
    scalars = jnp.concatenate(
        [
            jnp.mod(slab, 2).reshape(1),
            places.reshape(-1),
            live.reshape(-1).astype(jnp.int32),
        ]
    )

    between, within = swapped(
        jnp.concatenate([first_slab[rows - halo :], image[rows - 1 :]]),
        jnp.concatenate([first_slab[:halo], image[:1]]),
        "row",
    )
    width, channels = image.shape[1:]
    win = rows + 2 * MARGIN
    half, full = jnp.bfloat16, jnp.float32
    conv_scratch = [
        (((win + 2) * width, channels), half),
        ((win * width + 16, 3 * channels), full),
    ]
    pair, first_kv_t, first_expo, first_grad_probs = on_device(
        first_kernel,
        [
            ((rows, 2 * width, 2 * channels), half),
            ((win, 2 * channels, width), half),
            ((rows, BAND * width, width), full),
            ((rows, BAND * width, width), full),
        ],
        conv_scratch + [((win, width, 2 * channels), half)],
        1_000_000,
        scalars,
        image,
        first_slab,
        within,
        between,
        conv_weight,
        q_weight,
        k_weight,
        v_weight,
        grad_attended[0],
    )
    between, within = swapped(second_slab[rows - halo :], second_slab[:halo], "row")
    attended, top, bottom, center, grad_own = on_device(
        second_kernel,
        [
            ((rows, width, channels), half),
            ((2 * MARGIN, width, channels), half),
            ((2 * MARGIN, width, channels), half),
            ((2, rows, width, channels), full),
            ((rows, width, channels), full),
        ],
        conv_scratch
        + [
            ((win, width, 2 * channels), half),
            ((win, 2 * channels, width), half),
            ((2, win, width, 2 * channels), full),
        ],
        1_500_000_000,
        scalars,
        pair,
        second_slab,
        within,
        between,
        conv_weight,
        q_weight,
        k_weight,
        v_weight,
        first_kv_t,
        first_expo,
        first_grad_probs,
    )

    between, within = swapped(bottom, top, "row")
    second, first = on_device(
        slab_kernel,
        [(image.shape, half)] * 2,
        [],
        1_000_000,
        scalars,
        center,
        within,
        between,
    )
    from_second = routed(second, -2, 2).astype(full)
    from_first = routed(first, 2, -2).astype(full)
    for_pair = jnp.where(first_near, first.astype(full), 0.0) + jnp.where(
        second_near_on, from_second, 0.0
    )
    from_pair = routed(for_pair.astype(half), 1, -1).astype(full)
    summed = grad_own + from_pair
    summed = summed + jnp.where(second_near_on, 0.0, from_second)
    summed = summed + jnp.where(first_near_back, 0.0, from_first)
    return (attended[None], summed.astype(half)[None])


def solution(mesh):
    placed = (
        P("cam", "row", None, None),
        P(),
        P(),
        P(),
        P(),
        P(),
        P(),
        P("cam", "row", None, None),
        P("cam", "row", None, None),
    )
    return jax.shard_map(
        local,
        mesh=mesh,
        in_specs=placed,
        out_specs=(P("cam", "row", None, None), P("cam", "row", None, None)),
        check_vma=False,
    )
```

```python
import functools

import jax
import jax.numpy as jnp
from jax import lax
from jax.experimental import pallas as pl
from jax.experimental.pallas import tpu as pltpu
from jax.sharding import PartitionSpec as P

MARGIN = 2
BAND = 3
LOG2E = 1.4426950408889634
FLAGS = 4


def swap_parts(for_between, for_within, axis):
    count = lax.axis_size(axis)
    results = []
    for first, part in ((1, for_between), (0, for_within)):
        pairs = [(i, i + 1) for i in range(first, count - 1, 2)]
        results.append(lax.ppermute(part, axis, pairs + [(j, i) for i, j in pairs]))
    return results


def swapped(to_next, to_previous, axis):
    odd = lax.rem(lax.axis_index(axis), 2) == 1
    for_between = jnp.where(odd, to_next, to_previous)
    for_within = jnp.where(odd, to_previous, to_next)
    return swap_parts(for_between, for_within, axis)


def margins_of(odd, between, within):
    return jnp.where(odd, within, between), jnp.where(odd, between, within)


def dot_nn(a, b):
    return lax.dot_general(a, b, (((1,), (0,)), ((), ())), preferred_element_type=jnp.float32)


def dot_nt(a, b):
    return lax.dot_general(a, b, (((1,), (1,)), ((), ())), preferred_element_type=jnp.float32)


def stacked_taps(conv_weight):
    return jnp.concatenate(
        [jnp.concatenate([conv_weight[i, j] for j in range(3)], axis=1) for i in range(3)], axis=0
    )


def conv_rows(image, work, out_rows, width, taps):
    count = out_rows * width
    channels = taps.shape[1] // 3
    stacked = jnp.concatenate([image[i * width : i * width + count, :] for i in range(3)], axis=1)
    work[8 : 8 + count, :] = dot_nn(stacked, taps)
    none = jnp.zeros((1, channels), jnp.float32)
    for i in range(out_rows + 1):
        work[7 + i * width : 8 + i * width, :channels] = none
        work[8 + i * width : 9 + i * width, 2 * channels :] = none
    total = work[8 : 8 + count, channels : 2 * channels]
    total = total + work[7 : 7 + count, :channels]
    total = total + work[9 : 9 + count, 2 * channels :]
    return total.astype(jnp.bfloat16)


def side_keys(slab, odd, between, within, image, work, taps, wkv, kv, kv_t):
    rows, width, channels = slab.shape
    halo = MARGIN + 1
    win = rows + 2 * MARGIN
    above, below = margins_of(odd, between[0:halo], within[0:halo])
    image[0 : halo * width, :] = above.reshape(halo * width, channels)
    image[halo * width : (halo + rows) * width, :] = slab.reshape(rows * width, channels)
    image[(halo + rows) * width :, :] = below.reshape(halo * width, channels)
    hidden = conv_rows(image, work, win, width, taps)
    kv[...] = dot_nn(hidden, wkv).astype(jnp.bfloat16).reshape(win, width, 2 * channels)
    turned = dot_nt(wkv.T, hidden).astype(jnp.bfloat16)
    for r in range(win):
        kv_t[r] = turned[:, r * width : (r + 1) * width]


def places_of(scalars, rows, b, side):
    return [
        (
            scalars[FLAGS + (b * 2 + side) * BAND + s],
            scalars[FLAGS + rows * 2 * BAND + side * BAND + s] == 1,
        )
        for s in range(BAND)
    ]


def side_scores(places, kv, pair_b, width, channels):
    keys = jnp.concatenate([kv[at] for at, _ in places], axis=0)
    both = dot_nt(keys, pair_b)
    expo = jnp.exp2(both[:, :width] * (channels**-0.5 * LOG2E))
    expo = jnp.concatenate(
        [
            jnp.where(live, expo[i * width : (i + 1) * width], 0.0)
            for i, (_, live) in enumerate(places)
        ],
        axis=0,
    )
    return expo, both[:, width:]


def first_kernel(
    scalars,
    own,
    slab,
    within,
    between,
    conv_weight,
    q_weight,
    k_weight,
    v_weight,
    cotangent,
    pair,
    kv_t,
    expo,
    grad_probs,
    image,
    work,
    kv,
):
    rows, width, channels = own.shape
    halo = MARGIN + 1
    taps = stacked_taps(conv_weight)
    wkv = jnp.concatenate([k_weight[...], v_weight[...]], axis=1)

    odd = scalars[0] == 1
    above, below = margins_of(odd, between[halo], within[halo])
    image[0:width, :] = above
    image[width : (rows + 1) * width, :] = own[...].reshape(rows * width, channels)
    image[(rows + 1) * width : (rows + 2) * width, :] = below
    hidden = conv_rows(image, work, rows, width, taps)
    queries = dot_nn(hidden, q_weight[...]).astype(jnp.bfloat16)
    pair[...] = jnp.zeros_like(pair)
    for b in range(rows):
        pair[b, 0:width, 0:channels] = queries[b * width : (b + 1) * width, :]
        pair[b, width : 2 * width, channels : 2 * channels] = cotangent[b]

    side_keys(slab[...], odd, between, within, image, work, taps, wkv, kv, kv_t)
    for b in range(rows):
        expo[b], grad_probs[b] = side_scores(
            places_of(scalars, rows, b, 1), kv, pair[b], width, channels
        )


def second_kernel(
    scalars,
    pair,
    slab,
    within,
    between,
    conv_weight,
    k_weight,
    v_weight,
    first_expo,
    first_grad_probs,
    top,
    bottom,
    acc,
    probs_out,
    grad_scores_out,
    kv_t,
    image,
    work,
    kv,
):
    rows, width, channels = slab.shape
    taps = stacked_taps(conv_weight)
    wkv = jnp.concatenate([k_weight[...], v_weight[...]], axis=1)
    acc[...] = jnp.zeros_like(acc)
    side_keys(slab[...], scalars[0] == 1, between, within, image, work, taps, wkv, kv, kv_t)

    for b in range(rows):
        places = [places_of(scalars, rows, b, side) for side in range(2)]
        expo, grad_probs = side_scores(places[0], kv, pair[b], width, channels)
        expo = jnp.concatenate([expo, first_expo[b]], axis=0)
        grad_probs = jnp.concatenate([grad_probs, first_grad_probs[b]], axis=0)
        probs = expo * (1.0 / jnp.sum(expo, axis=0, keepdims=True))
        probs_bf = probs.astype(jnp.bfloat16)
        delta = jnp.sum(probs * grad_probs, axis=0, keepdims=True)
        grad_scores = (probs * (grad_probs - delta)).astype(jnp.bfloat16)
        probs_out[b] = probs_bf
        grad_scores_out[b] = grad_scores
        terms = dot_nn(jnp.concatenate([grad_scores, probs_bf], axis=1), pair[b])
        for side in range(2):
            for s, (at, _) in enumerate(places[side]):
                i = side * BAND + s
                acc[side, at] += terms[i * width : (i + 1) * width]

    for side in range(2):
        span = slice(side * MARGIN, (side + 1) * MARGIN)
        top[span] = back_projected(acc[side, :MARGIN], wkv).astype(jnp.bfloat16)
        bottom[span] = back_projected(acc[side, MARGIN + rows :], wkv).astype(jnp.bfloat16)


def back_projected(grads, wkv):
    rows, width, both = grads.shape
    channels = both // 2
    grads = grads.reshape(rows * width, both)
    grads = jnp.concatenate(
        [grads[:, :channels] * channels**-0.5, grads[:, channels:]], axis=1
    )
    return dot_nt(grads.astype(jnp.bfloat16), wkv).reshape(rows, width, channels)


def third_kernel(
    scalars,
    acc,
    probs,
    grad_scores,
    kv_t,
    first_kv_t,
    q_weight,
    k_weight,
    v_weight,
    attended,
    center,
    grad_own,
):
    rows, width, channels = attended.shape
    wkv = jnp.concatenate([k_weight[...], v_weight[...]], axis=1)
    for side in range(2):
        center[side] = back_projected(acc[side, MARGIN : MARGIN + rows], wkv)
    grad_q = []
    for b in range(rows):
        places = [places_of(scalars, rows, b, side) for side in range(2)]
        keys_t = jnp.concatenate(
            [kv_t[at] for at, _ in places[0]] + [first_kv_t[at] for at, _ in places[1]], axis=1
        )
        attended[b] = dot_nn(keys_t[channels:], probs[b]).T.astype(jnp.bfloat16)
        grad_q.append(dot_nn(keys_t[:channels], grad_scores[b]))
    grad_q = jnp.concatenate(grad_q, axis=1) * channels**-0.5
    turned = dot_nn(q_weight[...], grad_q.astype(jnp.bfloat16))
    for b in range(rows):
        grad_own[b] = turned[:, b * width : (b + 1) * width].T


def scalar_kernel(views, samples, where, partners, band_widths, bands, scalars):
    camera, slab = where[0], where[1]
    rows = bands.shape[2]
    odd = lax.rem(lax.div(camera, samples), 2)

    def is_near(steps, first):
        other = lax.rem(camera + steps * samples + views, views)
        side = jnp.where(odd == 1, 1 - first, first)
        gap = jnp.where(side == 1, samples, views - samples)
        return (partners[side, other] == lax.rem(other + gap, views)).astype(jnp.int32)

    on = jnp.where(odd == 1, -2, 2)
    scalars[0] = lax.rem(slab, 2)
    scalars[1] = is_near(0, 1)
    scalars[2] = is_near(on, 0)
    scalars[3] = is_near(-on, 1)
    top = slab * rows - MARGIN
    last = rows + 2 * MARGIN - 1
    for first in range(2):
        side = jnp.where(odd == 1, 1 - first, first)
        for s in range(BAND):
            for b in range(rows):
                at = jnp.clip(bands[s, side, b] - top, 0, last)
                scalars[FLAGS + (b * 2 + first) * BAND + s] = at
            live = (s < band_widths[side, camera]).astype(jnp.int32)
            scalars[FLAGS + rows * 2 * BAND + first * BAND + s] = live


def pass_kernel(scalars, pair_slab, own, passed_on):
    passed_on[...] = jnp.where(scalars[2] == 1, pair_slab[...], own[...])


def first_slab_kernel(scalars, far_slab, pair_slab, own, first_slab, for_within, for_between):
    rows = own.shape[0]
    halo = MARGIN + 1
    odd = scalars[0] == 1
    chosen = jnp.where(scalars[1] == 1, pair_slab[...], far_slab[...])
    first_slab[...] = chosen
    to_next, to_previous = chosen[rows - halo :], chosen[:halo]
    for_within[:halo] = jnp.where(odd, to_previous, to_next)
    for_between[:halo] = jnp.where(odd, to_next, to_previous)
    for_within[halo] = jnp.where(odd, own[0], own[rows - 1])
    for_between[halo] = jnp.where(odd, own[rows - 1], own[0])


def pair_kernel(scalars, first, from_second, for_pair):
    own = jnp.where(scalars[1] == 1, first[...].astype(jnp.float32), 0.0)
    relayed = jnp.where(scalars[2] == 1, from_second[...].astype(jnp.float32), 0.0)
    for_pair[...] = (own + relayed).astype(jnp.bfloat16)


def sum_kernel(scalars, grad_own, from_second, from_first, from_pair, grad_features):
    total = grad_own[...] + from_pair[...].astype(jnp.float32)
    total = total + jnp.where(scalars[2] == 1, 0.0, from_second[...].astype(jnp.float32))
    total = total + jnp.where(scalars[3] == 1, 0.0, from_first[...].astype(jnp.float32))
    grad_features[...] = total.astype(jnp.bfloat16)


def slab_kernel(scalars, center, within, between, left, right):
    rows, width, channels = left.shape
    above, below = margins_of(scalars[0] == 1, between[...], within[...])
    for side, out in enumerate((left, right)):
        for r in range(rows):
            total = center[side, r]
            if r < MARGIN:
                total = total + above[side * MARGIN + r].astype(jnp.float32)
            if r >= rows - MARGIN:
                total = total + below[side * MARGIN + r - rows + MARGIN].astype(jnp.float32)
            out[r] = total.astype(jnp.bfloat16)


def on_device(kernel, out_shape, scratch, flops, *arrays):
    smem = pl.BlockSpec(memory_space=pltpu.SMEM)
    vmem = pl.BlockSpec(memory_space=pltpu.VMEM)
    return pl.pallas_call(
        kernel,
        out_shape=tuple(jax.ShapeDtypeStruct(*one) for one in out_shape),
        in_specs=[smem if one.dtype == jnp.int32 else vmem for one in arrays],
        out_specs=tuple(smem if one[1] == jnp.int32 else vmem for one in out_shape),
        scratch_shapes=[pltpu.VMEM(*one) for one in scratch],
        compiler_params=pltpu.CompilerParams(vmem_limit_bytes=32 * 1024 * 1024),
        cost_estimate=pl.CostEstimate(
            flops=flops, bytes_accessed=flops // 1000, transcendentals=0
        ),
    )(*arrays)


def local(
    features_in,
    conv_weight,
    q_weight,
    k_weight,
    v_weight,
    partners,
    band_widths,
    bands,
    grad_attended,
):
    image = features_in[0]
    rows, width, channels = image.shape
    halo = MARGIN + 1
    win = rows + 2 * MARGIN
    half, full = jnp.bfloat16, jnp.float32
    views = lax.axis_size("cam")
    samples = views // min(16, views)
    ring = views // samples

    def routed(value, evens, odds):
        pairs = []
        for c in range(views):
            step = odds if (c // samples) % 2 else evens
            pairs.append((c, (c // samples + step) % ring * samples + c % samples))
        return lax.ppermute(value, "cam", pairs)

    pair_slab = routed(image, 1, -1)
    far_slab = routed(image, -2, 2)
    where = jnp.stack([lax.axis_index("cam"), lax.axis_index("row")]).astype(jnp.int32)
    (scalars,) = on_device(
        functools.partial(scalar_kernel, views, samples),
        [((FLAGS + (rows + 1) * 2 * BAND,), jnp.int32)],
        [],
        1_000_000,
        where,
        partners.T,
        band_widths.T,
        bands[0].transpose(2, 1, 0),
    )
    (passed_on,) = on_device(
        pass_kernel, [(image.shape, half)], [], 1_000_000, scalars, pair_slab, image
    )
    second_slab = routed(passed_on, 2, -2)
    far_slab, _ = lax.optimization_barrier((far_slab, passed_on))
    edge = ((halo + 1, width, channels), half)
    first_slab, for_within, for_between = on_device(
        first_slab_kernel,
        [(image.shape, half), edge, edge],
        [],
        1_000_000,
        scalars,
        far_slab,
        pair_slab,
        image,
    )
    between, within = swap_parts(for_between, for_within, "row")

    conv_scratch = [
        (((win + 2) * width, channels), half),
        ((win * width + 16, 3 * channels), full),
        ((win, width, 2 * channels), half),
    ]
    pair, first_kv_t, first_expo, first_grad_probs = on_device(
        first_kernel,
        [
            ((rows, 2 * width, 2 * channels), half),
            ((win, 2 * channels, width), half),
            ((rows, BAND * width, width), full),
            ((rows, BAND * width, width), full),
        ],
        conv_scratch,
        1_000_000,
        scalars,
        image,
        first_slab,
        within,
        between,
        conv_weight,
        q_weight,
        k_weight,
        v_weight,
        grad_attended[0],
    )
    between, within = swapped(second_slab[rows - halo :], second_slab[:halo], "row")
    margins = ((2 * MARGIN, width, channels), half)
    weights = ((rows, 2 * BAND * width, width), half)
    top, bottom, acc, probs, grad_scores, kv_t = on_device(
        second_kernel,
        [
            margins,
            margins,
            ((2, win, width, 2 * channels), full),
            weights,
            weights,
            ((win, 2 * channels, width), half),
        ],
        conv_scratch,
        1_500_000_000,
        scalars,
        pair,
        second_slab,
        within,
        between,
        conv_weight,
        k_weight,
        v_weight,
        first_expo,
        first_grad_probs,
    )
    between, within = swapped(bottom, top, "row")
    attended, center, grad_own = on_device(
        third_kernel,
        [
            (image.shape, half),
            ((2, rows, width, channels), full),
            (image.shape, full),
        ],
        [],
        1_000_000,
        scalars,
        acc,
        probs,
        grad_scores,
        kv_t,
        first_kv_t,
        q_weight,
        k_weight,
        v_weight,
    )
    second, first = on_device(
        slab_kernel,
        [(image.shape, half)] * 2,
        [],
        1_000_000,
        scalars,
        center,
        within,
        between,
    )
    from_second = routed(second, -2, 2)
    from_first = routed(first, 2, -2)
    (for_pair,) = on_device(
        pair_kernel, [(image.shape, half)], [], 1_000_000, scalars, first, from_second
    )
    from_pair = routed(for_pair, 1, -1)
    (grad_features,) = on_device(
        sum_kernel,
        [(image.shape, half)],
        [],
        1_000_000,
        scalars,
        grad_own,
        from_second,
        from_first,
        from_pair,
    )
    return (attended[None], grad_features[None])


def solution(mesh):
    placed = (
        P("cam", "row", None, None),
        P(),
        P(),
        P(),
        P(),
        P(),
        P(),
        P("cam", "row", None, None),
        P("cam", "row", None, None),
    )
    return jax.shard_map(
        local,
        mesh=mesh,
        in_specs=placed,
        out_specs=(P("cam", "row", None, None), P("cam", "row", None, None)),
        check_vma=False,
    )
```

```python
import jax
import jax.numpy as jnp
from jax import lax
from jax.experimental import pallas as pl
from jax.experimental.pallas import tpu as pltpu
from jax.sharding import PartitionSpec as P

MARGIN = 2
BAND = 3
LOG2E = 1.4426950408889634


def swap_parts(for_between, for_within, axis):
    count = lax.axis_size(axis)
    results = []
    for first, part in ((1, for_between), (0, for_within)):
        pairs = [(i, i + 1) for i in range(first, count - 1, 2)]
        results.append(lax.ppermute(part, axis, pairs + [(j, i) for i, j in pairs]))
    return results


def parity_split(to_next, to_previous, odd):
    return jnp.where(odd, to_next, to_previous), jnp.where(odd, to_previous, to_next)


def margins_of(odd, between, within):
    return jnp.where(odd, within, between), jnp.where(odd, between, within)


def dot_nn(a, b):
    return lax.dot_general(a, b, (((1,), (0,)), ((), ())), preferred_element_type=jnp.float32)


def dot_nt(a, b):
    return lax.dot_general(a, b, (((1,), (1,)), ((), ())), preferred_element_type=jnp.float32)


def stacked_taps(conv_weight):
    return jnp.concatenate(
        [jnp.concatenate([conv_weight[i, j] for j in range(3)], axis=1) for i in range(3)], axis=0
    )


def conv_rows(image, work, out_rows, width, taps):
    count = out_rows * width
    channels = taps.shape[1] // 3
    stacked = jnp.concatenate([image[i * width : i * width + count, :] for i in range(3)], axis=1)
    work[8 : 8 + count, :] = dot_nn(stacked, taps)
    none = jnp.zeros((1, channels), jnp.float32)
    for i in range(out_rows + 1):
        work[7 + i * width : 8 + i * width, :channels] = none
        work[8 + i * width : 9 + i * width, 2 * channels :] = none
    total = work[8 : 8 + count, channels : 2 * channels]
    total = total + work[7 : 7 + count, :channels]
    total = total + work[9 : 9 + count, 2 * channels :]
    return total.astype(jnp.bfloat16)


def side_keys(slab, odd, between, within, image, work, taps, wkv, kv, kv_t):
    rows, width, channels = slab.shape
    halo = MARGIN + 1
    win = rows + 2 * MARGIN
    above, below = margins_of(odd, between[0:halo], within[0:halo])
    image[0 : halo * width, :] = above.reshape(halo * width, channels)
    image[halo * width : (halo + rows) * width, :] = slab.reshape(rows * width, channels)
    image[(halo + rows) * width :, :] = below.reshape(halo * width, channels)
    hidden = conv_rows(image, work, win, width, taps)
    kv[...] = dot_nn(hidden, wkv).astype(jnp.bfloat16).reshape(win, width, 2 * channels)
    turned = dot_nt(wkv.T, hidden).astype(jnp.bfloat16)
    for r in range(win):
        kv_t[r] = turned[:, r * width : (r + 1) * width]


def places_of(scalars, rows, b, side):
    return [
        (
            scalars[1 + (b * 2 + side) * BAND + s],
            scalars[1 + rows * 2 * BAND + side * BAND + s] == 1,
        )
        for s in range(BAND)
    ]


def side_scores(places, kv, pair_b, width, channels):
    keys = jnp.concatenate([kv[at] for at, _ in places], axis=0)
    both = dot_nt(keys, pair_b)
    expo = jnp.exp2(both[:, :width] * (channels**-0.5 * LOG2E))
    expo = jnp.concatenate(
        [
            jnp.where(live, expo[i * width : (i + 1) * width], 0.0)
            for i, (_, live) in enumerate(places)
        ],
        axis=0,
    )
    return expo, both[:, width:]


def first_kernel(
    scalars,
    own,
    slab,
    within,
    between,
    conv_weight,
    q_weight,
    k_weight,
    v_weight,
    cotangent,
    pair,
    kv_t,
    expo,
    grad_probs,
    image,
    work,
    kv,
):
    rows, width, channels = own.shape
    halo = MARGIN + 1
    taps = stacked_taps(conv_weight)
    wkv = jnp.concatenate([k_weight[...], v_weight[...]], axis=1)

    odd = scalars[0] == 1
    above, below = margins_of(odd, between[halo], within[halo])
    image[0:width, :] = above
    image[width : (rows + 1) * width, :] = own[...].reshape(rows * width, channels)
    image[(rows + 1) * width : (rows + 2) * width, :] = below
    hidden = conv_rows(image, work, rows, width, taps)
    queries = dot_nn(hidden, q_weight[...]).astype(jnp.bfloat16)
    pair[...] = jnp.zeros_like(pair)
    for b in range(rows):
        pair[b, 0:width, 0:channels] = queries[b * width : (b + 1) * width, :]
        pair[b, width : 2 * width, channels : 2 * channels] = cotangent[b]

    side_keys(slab[...], odd, between, within, image, work, taps, wkv, kv, kv_t)
    for b in range(rows):
        expo[b], grad_probs[b] = side_scores(
            places_of(scalars, rows, b, 1), kv, pair[b], width, channels
        )


def second_kernel(
    scalars,
    pair,
    slab,
    within,
    between,
    conv_weight,
    k_weight,
    v_weight,
    first_expo,
    first_grad_probs,
    top,
    bottom,
    acc,
    probs_out,
    grad_scores_out,
    kv_t,
    image,
    work,
    kv,
):
    rows, width, channels = slab.shape
    taps = stacked_taps(conv_weight)
    wkv = jnp.concatenate([k_weight[...], v_weight[...]], axis=1)
    acc[...] = jnp.zeros_like(acc)
    side_keys(slab[...], scalars[0] == 1, between, within, image, work, taps, wkv, kv, kv_t)

    for b in range(rows):
        places = [places_of(scalars, rows, b, side) for side in range(2)]
        expo, grad_probs = side_scores(places[0], kv, pair[b], width, channels)
        expo = jnp.concatenate([expo, first_expo[b]], axis=0)
        grad_probs = jnp.concatenate([grad_probs, first_grad_probs[b]], axis=0)
        probs = expo * (1.0 / jnp.sum(expo, axis=0, keepdims=True))
        probs_bf = probs.astype(jnp.bfloat16)
        delta = jnp.sum(probs * grad_probs, axis=0, keepdims=True)
        grad_scores = (probs * (grad_probs - delta)).astype(jnp.bfloat16)
        probs_out[b] = probs_bf
        grad_scores_out[b] = grad_scores
        terms = dot_nn(jnp.concatenate([grad_scores, probs_bf], axis=1), pair[b])
        for side in range(2):
            for s, (at, _) in enumerate(places[side]):
                i = side * BAND + s
                acc[side, at] += terms[i * width : (i + 1) * width]

    for side in range(2):
        span = slice(side * MARGIN, (side + 1) * MARGIN)
        top[span] = back_projected(acc[side, :MARGIN], wkv).astype(jnp.bfloat16)
        bottom[span] = back_projected(acc[side, MARGIN + rows :], wkv).astype(jnp.bfloat16)


def back_projected(grads, wkv):
    rows, width, both = grads.shape
    channels = both // 2
    grads = grads.reshape(rows * width, both)
    grads = jnp.concatenate(
        [grads[:, :channels] * channels**-0.5, grads[:, channels:]], axis=1
    )
    return dot_nt(grads.astype(jnp.bfloat16), wkv).reshape(rows, width, channels)


def third_kernel(
    scalars,
    acc,
    probs,
    grad_scores,
    kv_t,
    first_kv_t,
    q_weight,
    k_weight,
    v_weight,
    attended,
    center,
    grad_own,
):
    rows, width, channels = attended.shape
    wkv = jnp.concatenate([k_weight[...], v_weight[...]], axis=1)
    for side in range(2):
        center[side] = back_projected(acc[side, MARGIN : MARGIN + rows], wkv)
    grad_q = []
    for b in range(rows):
        places = [places_of(scalars, rows, b, side) for side in range(2)]
        keys_t = jnp.concatenate(
            [kv_t[at] for at, _ in places[0]] + [first_kv_t[at] for at, _ in places[1]], axis=1
        )
        attended[b] = dot_nn(keys_t[channels:], probs[b]).T.astype(jnp.bfloat16)
        grad_q.append(dot_nn(keys_t[:channels], grad_scores[b]))
    grad_q = jnp.concatenate(grad_q, axis=1) * channels**-0.5
    turned = dot_nn(q_weight[...], grad_q.astype(jnp.bfloat16))
    for b in range(rows):
        grad_own[b] = turned[:, b * width : (b + 1) * width].T


def on_device(kernel, out_shape, scratch, flops, *arrays):
    smem = pl.BlockSpec(memory_space=pltpu.SMEM)
    vmem = pl.BlockSpec(memory_space=pltpu.VMEM)
    return pl.pallas_call(
        kernel,
        out_shape=tuple(jax.ShapeDtypeStruct(*one) for one in out_shape),
        in_specs=[smem if one.dtype == jnp.int32 else vmem for one in arrays],
        out_specs=tuple(smem if one[1] == jnp.int32 else vmem for one in out_shape),
        scratch_shapes=[pltpu.VMEM(*one) for one in scratch],
        compiler_params=pltpu.CompilerParams(vmem_limit_bytes=32 * 1024 * 1024),
        cost_estimate=pl.CostEstimate(
            flops=flops, bytes_accessed=flops // 1000, transcendentals=0
        ),
    )(*arrays)


def local(
    features_in,
    conv_weight,
    q_weight,
    k_weight,
    v_weight,
    partners,
    band_widths,
    bands,
    grad_attended,
):
    image = features_in[0]
    rows, width, channels = image.shape
    halo = MARGIN + 1
    win = rows + 2 * MARGIN
    half, full = jnp.bfloat16, jnp.float32
    views = lax.axis_size("cam")
    samples = views // min(16, views)
    ring = views // samples

    def routed(value, evens, odds):
        pairs = []
        for c in range(views):
            step = odds if (c // samples) % 2 else evens
            pairs.append((c, (c // samples + step) % ring * samples + c % samples))
        return lax.ppermute(value, "cam", pairs)

    camera = lax.axis_index("cam")
    slab = lax.axis_index("row")
    odd_place = lax.rem(lax.div(camera, samples), 2) == 1
    odd_row = lax.rem(slab, 2) == 1
    on = jnp.where(odd_place, -2, 2)

    def is_near(steps, first):
        other = lax.rem(camera + steps * samples + views, views)
        side = jnp.where(odd_place, 1 - first, first)
        gap = jnp.where(side == 1, samples, views - samples)
        return partners[other, side] == lax.rem(other + gap, views)

    first_near = is_near(0, 1)
    second_near_on = is_near(on, 0)
    first_near_back = is_near(-on, 1)
    pair_slab = routed(image, 1, -1)
    far_slab = routed(image, -2, 2)
    passed_on = jnp.where(second_near_on, pair_slab, image)
    second_slab = routed(passed_on, 2, -2)
    far_slab, _ = lax.optimization_barrier((far_slab, passed_on))
    first_slab = jnp.where(~first_near, far_slab, pair_slab)
    to_next = jnp.concatenate([first_slab[rows - halo :], image[rows - 1 :]])
    to_previous = jnp.concatenate([first_slab[:halo], image[:1]])
    for_between, for_within = parity_split(to_next, to_previous, odd_row)
    between, within = swap_parts(for_between, for_within, "row")
    bands, band_widths, _ = lax.optimization_barrier((bands, band_widths, for_between))

    widths_here = lax.dynamic_index_in_dim(band_widths, camera, 0, keepdims=False)
    live = jnp.arange(BAND, dtype=jnp.int32)[None, :] < widths_here[:, None]
    places = jnp.clip(bands[0] - (slab * rows - MARGIN), 0, win - 1)
    live = jnp.where(odd_place, live[::-1], live)
    places = jnp.where(odd_place, places[:, ::-1], places)
    scalars = jnp.concatenate(
        [
            odd_row.astype(jnp.int32).reshape(1),
            places.reshape(-1),
            live.reshape(-1).astype(jnp.int32),
        ]
    )

    conv_scratch = [
        (((win + 2) * width, channels), half),
        ((win * width + 16, 3 * channels), full),
        ((win, width, 2 * channels), half),
    ]
    pair, first_kv_t, first_expo, first_grad_probs = on_device(
        first_kernel,
        [
            ((rows, 2 * width, 2 * channels), half),
            ((win, 2 * channels, width), half),
            ((rows, BAND * width, width), full),
            ((rows, BAND * width, width), full),
        ],
        conv_scratch,
        1_000_000,
        scalars,
        image,
        first_slab,
        within,
        between,
        conv_weight,
        q_weight,
        k_weight,
        v_weight,
        grad_attended[0],
    )
    between, within = swap_parts(
        *parity_split(second_slab[rows - halo :], second_slab[:halo], odd_row), "row"
    )
    margins = ((2 * MARGIN, width, channels), half)
    weights = ((rows, 2 * BAND * width, width), half)
    top, bottom, acc, probs, grad_scores, kv_t = on_device(
        second_kernel,
        [
            margins,
            margins,
            ((2, win, width, 2 * channels), full),
            weights,
            weights,
            ((win, 2 * channels, width), half),
        ],
        conv_scratch,
        1_500_000_000,
        scalars,
        pair,
        second_slab,
        within,
        between,
        conv_weight,
        k_weight,
        v_weight,
        first_expo,
        first_grad_probs,
    )
    between, within = swap_parts(*parity_split(bottom, top, odd_row), "row")
    attended, center, grad_own = on_device(
        third_kernel,
        [
            (image.shape, half),
            ((2, rows, width, channels), full),
            (image.shape, full),
        ],
        [],
        1_000_000,
        scalars,
        acc,
        probs,
        grad_scores,
        kv_t,
        first_kv_t,
        q_weight,
        k_weight,
        v_weight,
    )
    from_above, from_below = (
        part.reshape(2, MARGIN, width, channels).astype(full)
        for part in margins_of(~odd_row, within, between)
    )
    zeros = jnp.zeros((2, rows - MARGIN, width, channels), full)
    total = center + jnp.concatenate([from_above, zeros], axis=1)
    total = total + jnp.concatenate([zeros, from_below], axis=1)
    second, first = total[0].astype(half), total[1].astype(half)
    from_second = routed(second, -2, 2)
    from_first = routed(first, 2, -2)
    for_pair = jnp.where(first_near, first.astype(full), 0.0) + jnp.where(
        second_near_on, from_second.astype(full), 0.0
    )
    from_pair = routed(for_pair.astype(half), 1, -1)
    summed = grad_own + from_pair.astype(full)
    summed = summed + jnp.where(second_near_on, 0.0, from_second.astype(full))
    summed = summed + jnp.where(first_near_back, 0.0, from_first.astype(full))
    return (attended[None], summed.astype(half)[None])


def solution(mesh):
    placed = (
        P("cam", "row", None, None),
        P(),
        P(),
        P(),
        P(),
        P(),
        P(),
        P("cam", "row", None, None),
        P("cam", "row", None, None),
    )
    return jax.shard_map(
        local,
        mesh=mesh,
        in_specs=placed,
        out_specs=(P("cam", "row", None, None), P("cam", "row", None, None)),
        check_vma=False,
    )
```

```python
import jax
import jax.numpy as jnp
from jax import lax
from jax.experimental import pallas as pl
from jax.experimental.pallas import tpu as pltpu
from jax.sharding import PartitionSpec as P

MARGIN = 2
BAND = 3
LOG2E = 1.4426950408889634


def swap_parts(for_between, for_within, axis):
    count = lax.axis_size(axis)
    results = []
    for first, part in ((1, for_between), (0, for_within)):
        pairs = [(i, i + 1) for i in range(first, count - 1, 2)]
        results.append(lax.ppermute(part, axis, pairs + [(j, i) for i, j in pairs]))
    return results


def parity_split(to_next, to_previous, odd):
    return jnp.where(odd, to_next, to_previous), jnp.where(odd, to_previous, to_next)


def margins_of(odd, between, within):
    return jnp.where(odd, within, between), jnp.where(odd, between, within)


def dot_nn(a, b):
    return lax.dot_general(a, b, (((1,), (0,)), ((), ())), preferred_element_type=jnp.float32)


def dot_nt(a, b):
    return lax.dot_general(a, b, (((1,), (1,)), ((), ())), preferred_element_type=jnp.float32)


def stacked_taps(conv_weight):
    return jnp.concatenate(
        [jnp.concatenate([conv_weight[i, j] for j in range(3)], axis=1) for i in range(3)], axis=0
    )


def conv_rows(image, work, out_rows, width, taps):
    count = out_rows * width
    channels = taps.shape[1] // 3
    stacked = jnp.concatenate([image[i * width : i * width + count, :] for i in range(3)], axis=1)
    work[8 : 8 + count, :] = dot_nn(stacked, taps)
    none = jnp.zeros((1, channels), jnp.float32)
    for i in range(out_rows + 1):
        work[7 + i * width : 8 + i * width, :channels] = none
        work[8 + i * width : 9 + i * width, 2 * channels :] = none
    total = work[8 : 8 + count, channels : 2 * channels]
    total = total + work[7 : 7 + count, :channels]
    total = total + work[9 : 9 + count, 2 * channels :]
    return total.astype(jnp.bfloat16)


def side_keys(slab, odd, between, within, image, work, taps, wkv, kv, kv_t):
    rows, width, channels = slab.shape
    halo = MARGIN + 1
    win = rows + 2 * MARGIN
    above, below = margins_of(odd, between[0:halo], within[0:halo])
    image[0 : halo * width, :] = above.reshape(halo * width, channels)
    image[halo * width : (halo + rows) * width, :] = slab.reshape(rows * width, channels)
    image[(halo + rows) * width :, :] = below.reshape(halo * width, channels)
    hidden = conv_rows(image, work, win, width, taps)
    kv[...] = dot_nn(hidden, wkv).astype(jnp.bfloat16).reshape(win, width, 2 * channels)
    turned = dot_nt(wkv.T, hidden).astype(jnp.bfloat16)
    for r in range(win):
        kv_t[r] = turned[:, r * width : (r + 1) * width]


def places_of(scalars, rows, b, side):
    return [
        (
            scalars[1 + (b * 2 + side) * BAND + s],
            scalars[1 + rows * 2 * BAND + side * BAND + s] == 1,
        )
        for s in range(BAND)
    ]


def side_scores(places, kv, pair_b, width, channels):
    keys = jnp.concatenate([kv[at] for at, _ in places], axis=0)
    both = dot_nt(keys, pair_b)
    expo = jnp.exp2(both[:, :width] * (channels**-0.5 * LOG2E))
    expo = jnp.concatenate(
        [
            jnp.where(live, expo[i * width : (i + 1) * width], 0.0)
            for i, (_, live) in enumerate(places)
        ],
        axis=0,
    )
    return expo, both[:, width:]


def first_kernel(
    scalars,
    own,
    slab,
    within,
    between,
    conv_weight,
    q_weight,
    k_weight,
    v_weight,
    cotangent,
    pair,
    kv_t,
    expo,
    grad_probs,
    image,
    work,
    kv,
):
    rows, width, channels = own.shape
    halo = MARGIN + 1
    taps = stacked_taps(conv_weight)
    wkv = jnp.concatenate([k_weight[...], v_weight[...]], axis=1)

    odd = scalars[0] == 1
    above, below = margins_of(odd, between[halo], within[halo])
    image[0:width, :] = above
    image[width : (rows + 1) * width, :] = own[...].reshape(rows * width, channels)
    image[(rows + 1) * width : (rows + 2) * width, :] = below
    hidden = conv_rows(image, work, rows, width, taps)
    queries = dot_nn(hidden, q_weight[...]).astype(jnp.bfloat16)
    pair[...] = jnp.zeros_like(pair)
    for b in range(rows):
        pair[b, 0:width, 0:channels] = queries[b * width : (b + 1) * width, :]
        pair[b, width : 2 * width, channels : 2 * channels] = cotangent[b]

    side_keys(slab[...], odd, between, within, image, work, taps, wkv, kv, kv_t)
    for b in range(rows):
        expo[b], grad_probs[b] = side_scores(
            places_of(scalars, rows, b, 1), kv, pair[b], width, channels
        )


def second_kernel(
    scalars,
    pair,
    slab,
    within,
    between,
    conv_weight,
    k_weight,
    v_weight,
    first_expo,
    first_grad_probs,
    top,
    bottom,
    acc,
    probs_out,
    grad_scores_out,
    kv_t,
    image,
    work,
    kv,
):
    rows, width, channels = slab.shape
    taps = stacked_taps(conv_weight)
    wkv = jnp.concatenate([k_weight[...], v_weight[...]], axis=1)
    acc[...] = jnp.zeros_like(acc)
    side_keys(slab[...], scalars[0] == 1, between, within, image, work, taps, wkv, kv, kv_t)

    for b in range(rows):
        places = [places_of(scalars, rows, b, side) for side in range(2)]
        expo, grad_probs = side_scores(places[0], kv, pair[b], width, channels)
        expo = jnp.concatenate([expo, first_expo[b]], axis=0)
        grad_probs = jnp.concatenate([grad_probs, first_grad_probs[b]], axis=0)
        probs = expo * (1.0 / jnp.sum(expo, axis=0, keepdims=True))
        probs_bf = probs.astype(jnp.bfloat16)
        delta = jnp.sum(probs * grad_probs, axis=0, keepdims=True)
        grad_scores = (probs * (grad_probs - delta)).astype(jnp.bfloat16)
        probs_out[b] = probs_bf
        grad_scores_out[b] = grad_scores
        terms = dot_nn(jnp.concatenate([grad_scores, probs_bf], axis=1), pair[b])
        for side in range(2):
            for s, (at, _) in enumerate(places[side]):
                i = side * BAND + s
                acc[side, at] += terms[i * width : (i + 1) * width]

    for side in range(2):
        span = slice(side * MARGIN, (side + 1) * MARGIN)
        top[span] = back_projected(acc[side, :MARGIN], wkv).astype(jnp.bfloat16)
        bottom[span] = back_projected(acc[side, MARGIN + rows :], wkv).astype(jnp.bfloat16)


def back_projected(grads, wkv):
    rows, width, both = grads.shape
    channels = both // 2
    grads = grads.reshape(rows * width, both)
    grads = jnp.concatenate(
        [grads[:, :channels] * channels**-0.5, grads[:, channels:]], axis=1
    )
    return dot_nt(grads.astype(jnp.bfloat16), wkv).reshape(rows, width, channels)


def third_kernel(
    scalars,
    acc,
    probs,
    grad_scores,
    kv_t,
    first_kv_t,
    q_weight,
    k_weight,
    v_weight,
    attended,
    center,
    grad_own,
):
    rows, width, channels = attended.shape
    wkv = jnp.concatenate([k_weight[...], v_weight[...]], axis=1)
    for side in range(2):
        center[side] = back_projected(acc[side, MARGIN : MARGIN + rows], wkv)
    grad_q = []
    for b in range(rows):
        places = [places_of(scalars, rows, b, side) for side in range(2)]
        keys_t = jnp.concatenate(
            [kv_t[at] for at, _ in places[0]] + [first_kv_t[at] for at, _ in places[1]], axis=1
        )
        attended[b] = dot_nn(keys_t[channels:], probs[b]).T.astype(jnp.bfloat16)
        grad_q.append(dot_nn(keys_t[:channels], grad_scores[b]))
    grad_q = jnp.concatenate(grad_q, axis=1) * channels**-0.5
    turned = dot_nn(q_weight[...], grad_q.astype(jnp.bfloat16))
    for b in range(rows):
        grad_own[b] = turned[:, b * width : (b + 1) * width].T


def on_device(kernel, out_shape, scratch, flops, *arrays):
    smem = pl.BlockSpec(memory_space=pltpu.SMEM)
    vmem = pl.BlockSpec(memory_space=pltpu.VMEM)
    return pl.pallas_call(
        kernel,
        out_shape=tuple(jax.ShapeDtypeStruct(*one) for one in out_shape),
        in_specs=[smem if one.dtype == jnp.int32 else vmem for one in arrays],
        out_specs=tuple(smem if one[1] == jnp.int32 else vmem for one in out_shape),
        scratch_shapes=[pltpu.VMEM(*one) for one in scratch],
        compiler_params=pltpu.CompilerParams(vmem_limit_bytes=14 * 1024 * 1024),
        cost_estimate=pl.CostEstimate(
            flops=flops, bytes_accessed=flops // 1000, transcendentals=0
        ),
    )(*arrays)


def local(
    features_in,
    conv_weight,
    q_weight,
    k_weight,
    v_weight,
    partners,
    band_widths,
    bands,
    grad_attended,
):
    image = features_in[0]
    rows, width, channels = image.shape
    halo = MARGIN + 1
    win = rows + 2 * MARGIN
    half, full = jnp.bfloat16, jnp.float32
    views = lax.axis_size("cam")
    samples = views // min(16, views)
    ring = views // samples

    def routed(value, evens, odds):
        pairs = []
        for c in range(views):
            step = odds if (c // samples) % 2 else evens
            pairs.append((c, (c // samples + step) % ring * samples + c % samples))
        return lax.ppermute(value, "cam", pairs)

    camera = lax.axis_index("cam")
    slab = lax.axis_index("row")
    odd_place = lax.rem(lax.div(camera, samples), 2) == 1
    odd_row = lax.rem(slab, 2) == 1
    on = jnp.where(odd_place, -2, 2)

    def is_near(steps, first):
        other = lax.rem(camera + steps * samples + views, views)
        side = jnp.where(odd_place, 1 - first, first)
        gap = jnp.where(side == 1, samples, views - samples)
        return partners[other, side] == lax.rem(other + gap, views)

    first_near = is_near(0, 1)
    second_near_on = is_near(on, 0)
    first_near_back = is_near(-on, 1)
    pair_slab = routed(image, 1, -1)
    far_slab = routed(image, -2, 2)
    passed_on = jnp.where(second_near_on, pair_slab, image)
    second_slab = routed(passed_on, 2, -2)
    far_slab, _ = lax.optimization_barrier((far_slab, passed_on))
    first_slab = jnp.where(~first_near, far_slab, pair_slab)
    to_next = jnp.concatenate([first_slab[rows - halo :], image[rows - 1 :]])
    to_previous = jnp.concatenate([first_slab[:halo], image[:1]])
    for_between, for_within = parity_split(to_next, to_previous, odd_row)
    between, within = swap_parts(for_between, for_within, "row")
    bands, band_widths, _ = lax.optimization_barrier((bands, band_widths, for_between))

    widths_here = lax.dynamic_index_in_dim(band_widths, camera, 0, keepdims=False)
    live = jnp.arange(BAND, dtype=jnp.int32)[None, :] < widths_here[:, None]
    places = jnp.clip(bands[0] - (slab * rows - MARGIN), 0, win - 1)
    live = jnp.where(odd_place, live[::-1], live)
    places = jnp.where(odd_place, places[:, ::-1], places)
    scalars = jnp.concatenate(
        [
            odd_row.astype(jnp.int32).reshape(1),
            places.reshape(-1),
            live.reshape(-1).astype(jnp.int32),
        ]
    )

    conv_scratch = [
        (((win + 2) * width, channels), half),
        ((win * width + 16, 3 * channels), full),
        ((win, width, 2 * channels), half),
    ]
    pair, first_kv_t, first_expo, first_grad_probs = on_device(
        first_kernel,
        [
            ((rows, 2 * width, 2 * channels), half),
            ((win, 2 * channels, width), half),
            ((rows, BAND * width, width), full),
            ((rows, BAND * width, width), full),
        ],
        conv_scratch,
        1_000_000,
        scalars,
        image,
        first_slab,
        within,
        between,
        conv_weight,
        q_weight,
        k_weight,
        v_weight,
        grad_attended[0],
    )
    between, within = swap_parts(
        *parity_split(second_slab[rows - halo :], second_slab[:halo], odd_row), "row"
    )
    margins = ((2 * MARGIN, width, channels), half)
    weights = ((rows, 2 * BAND * width, width), half)
    top, bottom, acc, probs, grad_scores, kv_t = on_device(
        second_kernel,
        [
            margins,
            margins,
            ((2, win, width, 2 * channels), full),
            weights,
            weights,
            ((win, 2 * channels, width), half),
        ],
        conv_scratch,
        1_500_000_000,
        scalars,
        pair,
        second_slab,
        within,
        between,
        conv_weight,
        k_weight,
        v_weight,
        first_expo,
        first_grad_probs,
    )
    between, within = swap_parts(*parity_split(bottom, top, odd_row), "row")
    attended, center, grad_own = on_device(
        third_kernel,
        [
            (image.shape, half),
            ((2, rows, width, channels), full),
            (image.shape, full),
        ],
        [],
        1_000_000,
        scalars,
        acc,
        probs,
        grad_scores,
        kv_t,
        first_kv_t,
        q_weight,
        k_weight,
        v_weight,
    )
    from_above, from_below = (
        part.reshape(2, MARGIN, width, channels).astype(full)
        for part in margins_of(~odd_row, within, between)
    )
    zeros = jnp.zeros((2, rows - MARGIN, width, channels), full)
    total = center + jnp.concatenate([from_above, zeros], axis=1)
    total = total + jnp.concatenate([zeros, from_below], axis=1)
    second, first = total[0].astype(half), total[1].astype(half)
    from_second = routed(second, -2, 2)
    from_first = routed(first, 2, -2)
    for_pair = jnp.where(first_near, first.astype(full), 0.0) + jnp.where(
        second_near_on, from_second.astype(full), 0.0
    )
    from_pair = routed(for_pair.astype(half), 1, -1)
    summed = grad_own + from_pair.astype(full)
    summed = summed + jnp.where(second_near_on, 0.0, from_second.astype(full))
    summed = summed + jnp.where(first_near_back, 0.0, from_first.astype(full))
    return (attended[None], summed.astype(half)[None])


def solution(mesh):
    placed = (
        P("cam", "row", None, None),
        P(),
        P(),
        P(),
        P(),
        P(),
        P(),
        P("cam", "row", None, None),
        P("cam", "row", None, None),
    )
    return jax.shard_map(
        local,
        mesh=mesh,
        in_specs=placed,
        out_specs=(P("cam", "row", None, None), P("cam", "row", None, None)),
        check_vma=False,
    )
```

```python
import jax
import jax.numpy as jnp
from jax import lax
from jax.experimental import pallas as pl
from jax.experimental.pallas import tpu as pltpu
from jax.sharding import PartitionSpec as P

MARGIN = 2
BAND = 3
LOG2E = 1.4426950408889634


def swap_parts(for_between, for_within, axis):
    count = lax.axis_size(axis)
    results = []
    for first, part in ((1, for_between), (0, for_within)):
        pairs = [(i, i + 1) for i in range(first, count - 1, 2)]
        results.append(lax.ppermute(part, axis, pairs + [(j, i) for i, j in pairs]))
    return results


def parity_split(to_next, to_previous, odd):
    return jnp.where(odd, to_next, to_previous), jnp.where(odd, to_previous, to_next)


def margins_of(odd, between, within):
    return jnp.where(odd, within, between), jnp.where(odd, between, within)


def dot_nn(a, b):
    return lax.dot_general(a, b, (((1,), (0,)), ((), ())), preferred_element_type=jnp.float32)


def dot_nt(a, b):
    return lax.dot_general(a, b, (((1,), (1,)), ((), ())), preferred_element_type=jnp.float32)


def stacked_taps(conv_weight):
    return jnp.concatenate(
        [jnp.concatenate([conv_weight[i, j] for j in range(3)], axis=1) for i in range(3)], axis=0
    )


def conv_rows(image, work, out_rows, width, taps):
    count = out_rows * width
    channels = taps.shape[1] // 3
    stacked = jnp.concatenate([image[i * width : i * width + count, :] for i in range(3)], axis=1)
    work[8 : 8 + count, :] = dot_nn(stacked, taps)
    none = jnp.zeros((1, channels), jnp.float32)
    for i in range(out_rows + 1):
        work[7 + i * width : 8 + i * width, :channels] = none
        work[8 + i * width : 9 + i * width, 2 * channels :] = none
    total = work[8 : 8 + count, channels : 2 * channels]
    total = total + work[7 : 7 + count, :channels]
    total = total + work[9 : 9 + count, 2 * channels :]
    return total.astype(jnp.bfloat16)


def side_keys(slab, odd, between, within, image, work, taps, wkv, kv, kv_t):
    rows, width, channels = slab.shape
    halo = MARGIN + 1
    win = rows + 2 * MARGIN
    above, below = margins_of(odd, between[0:halo], within[0:halo])
    image[0 : halo * width, :] = above.reshape(halo * width, channels)
    image[halo * width : (halo + rows) * width, :] = slab.reshape(rows * width, channels)
    image[(halo + rows) * width :, :] = below.reshape(halo * width, channels)
    hidden = conv_rows(image, work, win, width, taps)
    kv[...] = dot_nn(hidden, wkv).astype(jnp.bfloat16).reshape(win, width, 2 * channels)
    turned = dot_nt(wkv.T, hidden).astype(jnp.bfloat16)
    for r in range(win):
        kv_t[r] = turned[:, r * width : (r + 1) * width]


def places_of(scalars, rows, b, side):
    return [
        (
            scalars[1 + (b * 2 + side) * BAND + s],
            scalars[1 + rows * 2 * BAND + side * BAND + s] == 1,
        )
        for s in range(BAND)
    ]


def side_scores(places, kv, pair_b, width, channels):
    keys = jnp.concatenate([kv[at] for at, _ in places], axis=0)
    both = dot_nt(keys, pair_b)
    expo = jnp.exp2(both[:, :width] * (channels**-0.5 * LOG2E))
    expo = jnp.concatenate(
        [
            jnp.where(live, expo[i * width : (i + 1) * width], 0.0)
            for i, (_, live) in enumerate(places)
        ],
        axis=0,
    )
    return expo, both[:, width:]


def squared(queries_b, cotangent_b, square):
    width, channels = queries_b.shape
    square[...] = jnp.zeros_like(square)
    square[:width, :channels] = queries_b
    square[width:, channels:] = cotangent_b


def first_kernel(
    scalars,
    own,
    slab,
    within,
    between,
    conv_weight,
    q_weight,
    k_weight,
    v_weight,
    cotangent,
    queries,
    kv_t,
    expo,
    grad_probs,
    taps,
    wkv,
    image,
    work,
    kv,
    square,
):
    rows, width, channels = own.shape
    halo = MARGIN + 1
    odd = scalars[0] == 1
    taps[...] = stacked_taps(conv_weight)
    wkv[...] = jnp.concatenate([k_weight[...], v_weight[...]], axis=1)

    above, below = margins_of(odd, between[halo], within[halo])
    image[0:width, :] = above
    image[width : (rows + 1) * width, :] = own[...].reshape(rows * width, channels)
    image[(rows + 1) * width : (rows + 2) * width, :] = below
    hidden = conv_rows(image, work, rows, width, taps[...])
    queries[...] = (
        dot_nn(hidden, q_weight[...]).astype(jnp.bfloat16).reshape(rows, width, channels)
    )

    side_keys(slab[...], odd, between, within, image, work, taps[...], wkv[...], kv, kv_t)
    for b in range(rows):
        squared(queries[b], cotangent[b], square.at[b])
        expo[b], grad_probs[b] = side_scores(
            places_of(scalars, rows, b, 1), kv, square[b], width, channels
        )


def second_kernel(
    scalars,
    queries,
    cotangent,
    slab,
    within,
    between,
    taps,
    wkv,
    first_expo,
    first_grad_probs,
    for_within,
    for_between,
    middle,
    probs_out,
    grad_scores_out,
    kv_t,
    image,
    work,
    kv,
    square,
    acc,
):
    rows, width, channels = slab.shape
    odd = scalars[0] == 1
    acc[...] = jnp.zeros_like(acc)
    side_keys(slab[...], odd, between, within, image, work, taps[...], wkv[...], kv, kv_t)

    for b in range(rows):
        squared(queries[b], cotangent[b], square.at[b])
        places = [places_of(scalars, rows, b, side) for side in range(2)]
        expo, grad_probs = side_scores(places[0], kv, square[b], width, channels)
        expo = jnp.concatenate([expo, first_expo[b]], axis=0)
        grad_probs = jnp.concatenate([grad_probs, first_grad_probs[b]], axis=0)
        probs = expo * (1.0 / jnp.sum(expo, axis=0, keepdims=True))
        probs_bf = probs.astype(jnp.bfloat16)
        delta = jnp.sum(probs * grad_probs, axis=0, keepdims=True)
        grad_scores = (probs * (grad_probs - delta)).astype(jnp.bfloat16)
        probs_out[b] = probs_bf
        grad_scores_out[b] = grad_scores
        terms = dot_nn(jnp.concatenate([grad_scores, probs_bf], axis=1), square[b])
        for side in range(2):
            for s, (at, _) in enumerate(places[side]):
                i = side * BAND + s
                acc[side, at] += terms[i * width : (i + 1) * width]

    for side in range(2):
        span = slice(side * MARGIN, (side + 1) * MARGIN)
        top = back_projected(scaled(acc[side, :MARGIN]), wkv[...])
        bottom = back_projected(scaled(acc[side, MARGIN + rows :]), wkv[...])
        for_within[span] = jnp.where(odd, top, bottom).astype(jnp.bfloat16)
        for_between[span] = jnp.where(odd, bottom, top).astype(jnp.bfloat16)
        middle[side] = scaled(acc[side, MARGIN : MARGIN + rows])


def scaled(grads):
    channels = grads.shape[2] // 2
    return jnp.concatenate(
        [grads[:, :, :channels] * channels**-0.5, grads[:, :, channels:]], axis=2
    ).astype(jnp.bfloat16)


def back_projected(grads, wkv):
    rows, width, both = grads.shape
    return dot_nt(grads.reshape(rows * width, both), wkv).reshape(rows, width, both // 2)


def third_kernel(
    scalars,
    middle,
    probs,
    grad_scores,
    kv_t,
    first_kv_t,
    q_weight,
    wkv,
    attended,
    center,
    grad_own,
):
    rows, width, channels = attended.shape
    for side in range(2):
        center[side] = back_projected(middle[side], wkv[...])
    grad_q = []
    for b in range(rows):
        places = [places_of(scalars, rows, b, side) for side in range(2)]
        keys_t = jnp.concatenate(
            [kv_t[at] for at, _ in places[0]] + [first_kv_t[at] for at, _ in places[1]], axis=1
        )
        attended[b] = dot_nn(keys_t[channels:], probs[b]).T.astype(jnp.bfloat16)
        grad_q.append(dot_nn(keys_t[:channels], grad_scores[b]))
    grad_q = jnp.concatenate(grad_q, axis=1) * channels**-0.5
    turned = dot_nn(q_weight[...], grad_q.astype(jnp.bfloat16))
    for b in range(rows):
        grad_own[b] = turned[:, b * width : (b + 1) * width].T


def on_device(kernel, out_shape, scratch, flops, *arrays):
    smem = pl.BlockSpec(memory_space=pltpu.SMEM)
    vmem = pl.BlockSpec(memory_space=pltpu.VMEM)
    return pl.pallas_call(
        kernel,
        out_shape=tuple(jax.ShapeDtypeStruct(*one) for one in out_shape),
        in_specs=[smem if one.dtype == jnp.int32 else vmem for one in arrays],
        out_specs=tuple(smem if one[1] == jnp.int32 else vmem for one in out_shape),
        scratch_shapes=[pltpu.VMEM(*one) for one in scratch],
        compiler_params=pltpu.CompilerParams(vmem_limit_bytes=14 * 1024 * 1024),
        cost_estimate=pl.CostEstimate(
            flops=flops, bytes_accessed=flops // 1000, transcendentals=0
        ),
    )(*arrays)


def local(
    features_in,
    conv_weight,
    q_weight,
    k_weight,
    v_weight,
    partners,
    band_widths,
    bands,
    grad_attended,
):
    image = features_in[0]
    rows, width, channels = image.shape
    halo = MARGIN + 1
    win = rows + 2 * MARGIN
    half, full = jnp.bfloat16, jnp.float32
    views = lax.axis_size("cam")
    samples = views // min(16, views)
    ring = views // samples

    def routed(value, evens, odds):
        pairs = []
        for c in range(views):
            step = odds if (c // samples) % 2 else evens
            pairs.append((c, (c // samples + step) % ring * samples + c % samples))
        return lax.ppermute(value, "cam", pairs)

    camera = lax.axis_index("cam")
    slab = lax.axis_index("row")
    odd_place = lax.rem(lax.div(camera, samples), 2) == 1
    odd_row = lax.rem(slab, 2) == 1
    on = jnp.where(odd_place, -2, 2)

    def is_near(steps, first):
        other = lax.rem(camera + steps * samples + views, views)
        side = jnp.where(odd_place, 1 - first, first)
        gap = jnp.where(side == 1, samples, views - samples)
        return partners[other, side] == lax.rem(other + gap, views)

    first_near = is_near(0, 1)
    second_near_on = is_near(on, 0)
    first_near_back = is_near(-on, 1)
    pair_slab = routed(image, 1, -1)
    far_slab = routed(image, -2, 2)
    passed_on = jnp.where(second_near_on, pair_slab, image)
    second_slab = routed(passed_on, 2, -2)
    far_slab, _ = lax.optimization_barrier((far_slab, passed_on))
    first_slab = jnp.where(~first_near, far_slab, pair_slab)
    to_next = jnp.concatenate([first_slab[rows - halo :], image[rows - 1 :]])
    to_previous = jnp.concatenate([first_slab[:halo], image[:1]])
    for_between, for_within = parity_split(to_next, to_previous, odd_row)
    between, within = swap_parts(for_between, for_within, "row")
    bands, band_widths, _ = lax.optimization_barrier((bands, band_widths, for_between))

    widths_here = lax.dynamic_index_in_dim(band_widths, camera, 0, keepdims=False)
    live = jnp.arange(BAND, dtype=jnp.int32)[None, :] < widths_here[:, None]
    places = jnp.clip(bands[0] - (slab * rows - MARGIN), 0, win - 1)
    live = jnp.where(odd_place, live[::-1], live)
    places = jnp.where(odd_place, places[:, ::-1], places)
    scalars = jnp.concatenate(
        [
            odd_row.astype(jnp.int32).reshape(1),
            places.reshape(-1),
            live.reshape(-1).astype(jnp.int32),
        ]
    )

    conv_scratch = [
        (((win + 2) * width, channels), half),
        ((win * width + 16, 3 * channels), full),
        ((win, width, 2 * channels), half),
        ((rows, 2 * width, 2 * channels), half),
    ]
    queries, first_kv_t, first_expo, first_grad_probs, taps, wkv = on_device(
        first_kernel,
        [
            (image.shape, half),
            ((win, 2 * channels, width), half),
            ((rows, BAND * width, width), full),
            ((rows, BAND * width, width), full),
            ((3 * channels, 3 * channels), half),
            ((channels, 2 * channels), half),
        ],
        conv_scratch,
        1_000_000,
        scalars,
        image,
        first_slab,
        within,
        between,
        conv_weight,
        q_weight,
        k_weight,
        v_weight,
        grad_attended[0],
    )
    between, within = swap_parts(
        *parity_split(second_slab[rows - halo :], second_slab[:halo], odd_row), "row"
    )
    margins = ((2 * MARGIN, width, channels), half)
    weights = ((rows, 2 * BAND * width, width), half)
    for_within, for_between, middle, probs, grad_scores, kv_t = on_device(
        second_kernel,
        [
            margins,
            margins,
            ((2, rows, width, 2 * channels), half),
            weights,
            weights,
            ((win, 2 * channels, width), half),
        ],
        conv_scratch + [((2, win, width, 2 * channels), full)],
        1_500_000_000,
        scalars,
        queries,
        grad_attended[0],
        second_slab,
        within,
        between,
        taps,
        wkv,
        first_expo,
        first_grad_probs,
    )
    between, within = swap_parts(for_between, for_within, "row")
    attended, center, grad_own = on_device(
        third_kernel,
        [
            (image.shape, half),
            ((2, rows, width, channels), full),
            (image.shape, full),
        ],
        [],
        1_000_000,
        scalars,
        middle,
        probs,
        grad_scores,
        kv_t,
        first_kv_t,
        q_weight,
        wkv,
    )
    from_above, from_below = (
        part.reshape(2, MARGIN, width, channels).astype(full)
        for part in margins_of(~odd_row, within, between)
    )
    zeros = jnp.zeros((2, rows - MARGIN, width, channels), full)
    total = center + jnp.concatenate([from_above, zeros], axis=1)
    total = total + jnp.concatenate([zeros, from_below], axis=1)
    second, first = total[0].astype(half), total[1].astype(half)
    from_second = routed(second, -2, 2)
    from_first = routed(first, 2, -2)
    for_pair = jnp.where(first_near, first.astype(full), 0.0) + jnp.where(
        second_near_on, from_second.astype(full), 0.0
    )
    from_pair = routed(for_pair.astype(half), 1, -1)
    summed = grad_own + from_pair.astype(full)
    summed = summed + jnp.where(second_near_on, 0.0, from_second.astype(full))
    summed = summed + jnp.where(first_near_back, 0.0, from_first.astype(full))
    return (attended[None], summed.astype(half)[None])


def solution(mesh):
    placed = (
        P("cam", "row", None, None),
        P(),
        P(),
        P(),
        P(),
        P(),
        P(),
        P("cam", "row", None, None),
        P("cam", "row", None, None),
    )
    return jax.shard_map(
        local,
        mesh=mesh,
        in_specs=placed,
        out_specs=(P("cam", "row", None, None), P("cam", "row", None, None)),
        check_vma=False,
    )
```

```python
import jax
import jax.numpy as jnp
from jax import lax
from jax.experimental import pallas as pl
from jax.experimental.pallas import tpu as pltpu
from jax.sharding import PartitionSpec as P

MARGIN = 2
BAND = 3
LOG2E = 1.4426950408889634


def swap_parts(for_between, for_within, axis):
    count = lax.axis_size(axis)
    results = []
    for first, part in ((1, for_between), (0, for_within)):
        pairs = [(i, i + 1) for i in range(first, count - 1, 2)]
        results.append(lax.ppermute(part, axis, pairs + [(j, i) for i, j in pairs]))
    return results


def parity_split(to_next, to_previous, odd):
    return jnp.where(odd, to_next, to_previous), jnp.where(odd, to_previous, to_next)


def margins_of(odd, between, within):
    return jnp.where(odd, within, between), jnp.where(odd, between, within)


def dot_nn(a, b):
    return lax.dot_general(a, b, (((1,), (0,)), ((), ())), preferred_element_type=jnp.float32)


def dot_nt(a, b):
    return lax.dot_general(a, b, (((1,), (1,)), ((), ())), preferred_element_type=jnp.float32)


def stacked_taps(conv_weight):
    return jnp.concatenate(
        [jnp.concatenate([conv_weight[i, j] for j in range(3)], axis=1) for i in range(3)], axis=0
    )


def conv_rows(image, work, out_rows, width, taps):
    count = out_rows * width
    channels = taps.shape[1] // 3
    stacked = jnp.concatenate([image[i * width : i * width + count, :] for i in range(3)], axis=1)
    work[8 : 8 + count, :] = dot_nn(stacked, taps)
    none = jnp.zeros((1, channels), jnp.float32)
    for i in range(out_rows + 1):
        work[7 + i * width : 8 + i * width, :channels] = none
        work[8 + i * width : 9 + i * width, 2 * channels :] = none
    total = work[8 : 8 + count, channels : 2 * channels]
    total = total + work[7 : 7 + count, :channels]
    total = total + work[9 : 9 + count, 2 * channels :]
    return total.astype(jnp.bfloat16)


def side_keys(slab, odd, between, within, image, work, taps, wkv, kv, kv_t):
    rows, width, channels = slab.shape
    halo = MARGIN + 1
    win = rows + 2 * MARGIN
    above, below = margins_of(odd, between[0:halo], within[0:halo])
    image[0 : halo * width, :] = above.reshape(halo * width, channels)
    image[halo * width : (halo + rows) * width, :] = slab.reshape(rows * width, channels)
    image[(halo + rows) * width :, :] = below.reshape(halo * width, channels)
    hidden = conv_rows(image, work, win, width, taps)
    kv[...] = dot_nn(hidden, wkv).astype(jnp.bfloat16).reshape(win, width, 2 * channels)
    turned = dot_nt(wkv.T, hidden).astype(jnp.bfloat16)
    for r in range(win):
        kv_t[r] = turned[:, r * width : (r + 1) * width]


def places_of(scalars, rows, b, side):
    return [
        (
            scalars[1 + (b * 2 + side) * BAND + s],
            scalars[1 + rows * 2 * BAND + side * BAND + s] == 1,
        )
        for s in range(BAND)
    ]


def side_scores(places, kv, pair_b, width, channels):
    keys = jnp.concatenate([kv[at] for at, _ in places], axis=0)
    both = dot_nt(keys, pair_b)
    expo = jnp.exp2(both[:, :width] * (channels**-0.5 * LOG2E))
    expo = jnp.concatenate(
        [
            jnp.where(live, expo[i * width : (i + 1) * width], 0.0)
            for i, (_, live) in enumerate(places)
        ],
        axis=0,
    )
    return expo, both[:, width:]


def squared(queries_b, cotangent_b, square):
    width, channels = queries_b.shape
    square[...] = jnp.zeros_like(square)
    square[:width, :channels] = queries_b
    square[width:, channels:] = cotangent_b


def first_kernel(
    scalars,
    own,
    slab,
    within,
    between,
    conv_weight,
    q_weight,
    k_weight,
    v_weight,
    cotangent,
    queries,
    kv_t,
    expo,
    grad_probs,
    taps,
    wkv,
    image,
    work,
    kv,
    square,
):
    rows, width, channels = own.shape
    halo = MARGIN + 1
    odd = scalars[0] == 1
    taps[...] = stacked_taps(conv_weight)
    wkv[...] = jnp.concatenate([k_weight[...], v_weight[...]], axis=1)

    above, below = margins_of(odd, between[halo], within[halo])
    image[0:width, :] = above
    image[width : (rows + 1) * width, :] = own[...].reshape(rows * width, channels)
    image[(rows + 1) * width : (rows + 2) * width, :] = below
    hidden = conv_rows(image, work, rows, width, taps[...])
    queries[...] = (
        dot_nn(hidden, q_weight[...]).astype(jnp.bfloat16).reshape(rows, width, channels)
    )

    side_keys(slab[...], odd, between, within, image, work, taps[...], wkv[...], kv, kv_t)
    for b in range(rows):
        squared(queries[b], cotangent[b], square.at[b])
        expo[b], grad_probs[b] = side_scores(
            places_of(scalars, rows, b, 1), kv, square[b], width, channels
        )


def second_kernel(
    scalars,
    queries,
    cotangent,
    slab,
    within,
    between,
    taps,
    wkv,
    first_expo,
    first_grad_probs,
    for_within,
    for_between,
    middle,
    probs_out,
    grad_scores_out,
    kv_t,
    image,
    work,
    kv,
    square,
    acc,
):
    rows, width, channels = slab.shape
    odd = scalars[0] == 1
    acc[...] = jnp.zeros_like(acc)
    side_keys(slab[...], odd, between, within, image, work, taps[...], wkv[...], kv, kv_t)

    for b in range(rows):
        squared(queries[b], cotangent[b], square.at[b])
        places = [places_of(scalars, rows, b, side) for side in range(2)]
        expo, grad_probs = side_scores(places[0], kv, square[b], width, channels)
        expo = jnp.concatenate([expo, first_expo[b]], axis=0)
        grad_probs = jnp.concatenate([grad_probs, first_grad_probs[b]], axis=0)
        probs = expo * (1.0 / jnp.sum(expo, axis=0, keepdims=True))
        probs_bf = probs.astype(jnp.bfloat16)
        delta = jnp.sum(probs * grad_probs, axis=0, keepdims=True)
        grad_scores = (probs * (grad_probs - delta)).astype(jnp.bfloat16)
        probs_out[b] = probs_bf
        grad_scores_out[b] = grad_scores
        terms = dot_nn(jnp.concatenate([grad_scores, probs_bf], axis=1), square[b])
        for side in range(2):
            for s, (at, _) in enumerate(places[side]):
                i = side * BAND + s
                acc[side, at] += terms[i * width : (i + 1) * width]

    for side in range(2):
        span = slice(side * MARGIN, (side + 1) * MARGIN)
        top = back_projected(scaled(acc[side, :MARGIN]), wkv[...])
        bottom = back_projected(scaled(acc[side, MARGIN + rows :]), wkv[...])
        for_within[span] = jnp.where(odd, top, bottom).astype(jnp.bfloat16)
        for_between[span] = jnp.where(odd, bottom, top).astype(jnp.bfloat16)
        middle[side] = scaled(acc[side, MARGIN : MARGIN + rows])


def scaled(grads):
    channels = grads.shape[2] // 2
    return jnp.concatenate(
        [grads[:, :, :channels] * channels**-0.5, grads[:, :, channels:]], axis=2
    ).astype(jnp.bfloat16)


def back_projected(grads, wkv):
    rows, width, both = grads.shape
    return dot_nt(grads.reshape(rows * width, both), wkv).reshape(rows, width, both // 2)


def third_kernel(
    scalars,
    middle,
    probs,
    grad_scores,
    kv_t,
    first_kv_t,
    q_weight,
    wkv,
    attended,
    center,
    grad_own,
):
    rows, width, channels = attended.shape
    for side in range(2):
        center[side] = back_projected(middle[side], wkv[...])
    grad_q = []
    for b in range(rows):
        places = [places_of(scalars, rows, b, side) for side in range(2)]
        keys_t = jnp.concatenate(
            [kv_t[at] for at, _ in places[0]] + [first_kv_t[at] for at, _ in places[1]], axis=1
        )
        attended[b] = dot_nn(keys_t[channels:], probs[b]).T.astype(jnp.bfloat16)
        grad_q.append(dot_nn(keys_t[:channels], grad_scores[b]))
    grad_q = jnp.concatenate(grad_q, axis=1) * channels**-0.5
    turned = dot_nn(q_weight[...], grad_q.astype(jnp.bfloat16))
    for b in range(rows):
        grad_own[b] = turned[:, b * width : (b + 1) * width].T


def on_device(kernel, out_shape, scratch, flops, *arrays):
    smem = pl.BlockSpec(memory_space=pltpu.SMEM)
    vmem = pl.BlockSpec(memory_space=pltpu.VMEM)
    return pl.pallas_call(
        kernel,
        out_shape=tuple(jax.ShapeDtypeStruct(*one) for one in out_shape),
        in_specs=[smem if one.dtype == jnp.int32 else vmem for one in arrays],
        out_specs=tuple(smem if one[1] == jnp.int32 else vmem for one in out_shape),
        scratch_shapes=[pltpu.VMEM(*one) for one in scratch],
        compiler_params=pltpu.CompilerParams(vmem_limit_bytes=14 * 1024 * 1024),
        cost_estimate=pl.CostEstimate(
            flops=flops, bytes_accessed=flops // 1000, transcendentals=0
        ),
    )(*arrays)


def local(
    features_in,
    conv_weight,
    q_weight,
    k_weight,
    v_weight,
    partners,
    band_widths,
    bands,
    grad_attended,
):
    image = features_in[0]
    rows, width, channels = image.shape
    halo = MARGIN + 1
    win = rows + 2 * MARGIN
    half, full = jnp.bfloat16, jnp.float32
    views = lax.axis_size("cam")
    samples = views // min(16, views)
    ring = views // samples

    def routed(value, evens, odds):
        pairs = []
        for c in range(views):
            step = odds if (c // samples) % 2 else evens
            pairs.append((c, (c // samples + step) % ring * samples + c % samples))
        return lax.ppermute(value, "cam", pairs)

    camera = lax.axis_index("cam")
    slab = lax.axis_index("row")
    odd_place = (camera if samples == 1 else lax.div(camera, samples)) & 1
    odd_row = (slab & 1) == 1
    even_row = (slab & 1) == 0
    on = (2 - 4 * odd_place) * samples
    to_pair = (1 - 2 * odd_place) * samples

    def around(place):
        return place & (views - 1) if views & (views - 1) == 0 else lax.rem(place + views, views)

    def is_near(other, side, gap):
        partner = lax.dynamic_slice(
            partners, (other, side), (1, 1), allow_negative_indices=False
        )
        return partner[0, 0] == around(other + gap)

    second_near_on = is_near(around(camera + on), odd_place, -to_pair)
    first_near = is_near(camera, odd_place ^ 1, to_pair)
    first_near_back = is_near(around(camera - on), odd_place ^ 1, to_pair)
    pair_slab = routed(image, 1, -1)
    far_slab = routed(image, -2, 2)
    passed_on = jnp.where(second_near_on, pair_slab, image)
    second_slab = routed(passed_on, 2, -2)
    far_slab, image, _ = lax.optimization_barrier((far_slab, image, passed_on))
    first_slab = jnp.where(~first_near, far_slab, pair_slab)
    to_next = jnp.concatenate([first_slab[rows - halo :], image[rows - 1 :]])
    to_previous = jnp.concatenate([first_slab[:halo], image[:1]])
    for_between, for_within = parity_split(to_next, to_previous, odd_row)
    between, within = swap_parts(for_between, for_within, "row")
    bands, band_widths, even_row, second_near, first_near, first_near_back, _ = (
        lax.optimization_barrier(
            (
                bands,
                band_widths,
                even_row,
                second_near_on,
                first_near,
                first_near_back,
                for_between,
            )
        )
    )

    widths_here = lax.dynamic_slice(
        band_widths, (camera, 0), (1, 2), allow_negative_indices=False
    )[0]
    live = jnp.arange(BAND, dtype=jnp.int32)[None, :] < widths_here[:, None]
    places = jnp.clip(bands[0] - (slab * rows - MARGIN), 0, win - 1)
    live = jnp.where(odd_place == 1, live[::-1], live)
    places = jnp.where(odd_place == 1, places[:, ::-1], places)
    scalars = jnp.concatenate(
        [
            odd_row.astype(jnp.int32).reshape(1),
            places.reshape(-1),
            live.reshape(-1).astype(jnp.int32),
        ]
    )

    conv_scratch = [
        (((win + 2) * width, channels), half),
        ((win * width + 16, 3 * channels), full),
        ((win, width, 2 * channels), half),
        ((rows, 2 * width, 2 * channels), half),
    ]
    queries, first_kv_t, first_expo, first_grad_probs, taps, wkv = on_device(
        first_kernel,
        [
            (image.shape, half),
            ((win, 2 * channels, width), half),
            ((rows, BAND * width, width), full),
            ((rows, BAND * width, width), full),
            ((3 * channels, 3 * channels), half),
            ((channels, 2 * channels), half),
        ],
        conv_scratch,
        1_000_000,
        scalars,
        image,
        first_slab,
        within,
        between,
        conv_weight,
        q_weight,
        k_weight,
        v_weight,
        grad_attended[0],
    )
    between, within = swap_parts(
        *parity_split(second_slab[rows - halo :], second_slab[:halo], odd_row), "row"
    )
    margins = ((2 * MARGIN, width, channels), half)
    weights = ((rows, 2 * BAND * width, width), half)
    for_within, for_between, middle, probs, grad_scores, kv_t = on_device(
        second_kernel,
        [
            margins,
            margins,
            ((2, rows, width, 2 * channels), half),
            weights,
            weights,
            ((win, 2 * channels, width), half),
        ],
        conv_scratch + [((2, win, width, 2 * channels), full)],
        1_500_000_000,
        scalars,
        queries,
        grad_attended[0],
        second_slab,
        within,
        between,
        taps,
        wkv,
        first_expo,
        first_grad_probs,
    )
    between, within = swap_parts(for_between, for_within, "row")
    attended, center, grad_own = on_device(
        third_kernel,
        [
            (image.shape, half),
            ((2, rows, width, channels), full),
            (image.shape, full),
        ],
        [],
        1_000_000,
        scalars,
        middle,
        probs,
        grad_scores,
        kv_t,
        first_kv_t,
        q_weight,
        wkv,
    )
    from_above, from_below = (
        part.reshape(2, MARGIN, width, channels).astype(full)
        for part in margins_of(even_row, within, between)
    )
    zeros = jnp.zeros((2, rows - MARGIN, width, channels), full)
    total = center + jnp.concatenate([from_above, zeros], axis=1)
    total = total + jnp.concatenate([zeros, from_below], axis=1)
    second, first = total[0].astype(half), total[1].astype(half)
    from_second = routed(second, -2, 2)
    from_first = routed(first, 2, -2)
    for_pair = jnp.where(first_near, first.astype(full), 0.0) + jnp.where(
        second_near, from_second.astype(full), 0.0
    )
    from_pair = routed(for_pair.astype(half), 1, -1)
    summed = grad_own + from_pair.astype(full)
    summed = summed + jnp.where(second_near, 0.0, from_second.astype(full))
    summed = summed + jnp.where(first_near_back, 0.0, from_first.astype(full))
    return (attended[None], summed.astype(half)[None])


def solution(mesh):
    placed = (
        P("cam", "row", None, None),
        P(),
        P(),
        P(),
        P(),
        P(),
        P(),
        P("cam", "row", None, None),
        P("cam", "row", None, None),
    )
    return jax.shard_map(
        local,
        mesh=mesh,
        in_specs=placed,
        out_specs=(P("cam", "row", None, None), P("cam", "row", None, None)),
        check_vma=False,
    )
```

```python
import jax
import jax.numpy as jnp
import numpy as np
from jax import lax
from jax.experimental import pallas as pl
from jax.experimental.pallas import tpu as pltpu
from jax.sharding import PartitionSpec as P

MARGIN = 2
BAND = 3
LOG2E = 1.4426950408889634


def swap_within(value):
    pairs = [(i, i + 1) for i in range(0, lax.axis_size("row") - 1, 2)]
    return lax.ppermute(value, "row", pairs + [(j, i) for i, j in pairs])


def swap_between(value):
    pairs = [(i, i + 1) for i in range(1, lax.axis_size("row") - 1, 2)]
    return lax.ppermute(value, "row", pairs + [(j, i) for i, j in pairs])


def parity_split(to_next, to_previous, odd):
    return jnp.where(odd, to_next, to_previous), jnp.where(odd, to_previous, to_next)


def margins_of(odd, between, within):
    return jnp.where(odd, within, between), jnp.where(odd, between, within)


def dot_nn(a, b):
    return lax.dot_general(a, b, (((1,), (0,)), ((), ())), preferred_element_type=jnp.float32)


def dot_nt(a, b):
    return lax.dot_general(a, b, (((1,), (1,)), ((), ())), preferred_element_type=jnp.float32)


def stacked_taps(conv_weight):
    return jnp.concatenate(
        [jnp.concatenate([conv_weight[i, j] for j in range(3)], axis=1) for i in range(3)], axis=0
    )


def conv_rows(image, work, out_rows, width, taps):
    count = out_rows * width
    channels = taps.shape[1] // 3
    stacked = jnp.concatenate([image[i * width : i * width + count, :] for i in range(3)], axis=1)
    work[8 : 8 + count, :] = dot_nn(stacked, taps)
    none = jnp.zeros((1, channels), jnp.float32)
    for i in range(out_rows + 1):
        work[7 + i * width : 8 + i * width, :channels] = none
        work[8 + i * width : 9 + i * width, 2 * channels :] = none
    total = work[8 : 8 + count, channels : 2 * channels]
    total = total + work[7 : 7 + count, :channels]
    total = total + work[9 : 9 + count, 2 * channels :]
    return total.astype(jnp.bfloat16)


def side_keys(slab, odd, between, within, image, work, taps, wkv, kv, kv_t):
    rows, width, channels = slab.shape
    halo = MARGIN + 1
    win = rows + 2 * MARGIN
    above, below = margins_of(odd, between[0:halo], within[0:halo])
    image[0 : halo * width, :] = above.reshape(halo * width, channels)
    image[halo * width : (halo + rows) * width, :] = slab.reshape(rows * width, channels)
    image[(halo + rows) * width :, :] = below.reshape(halo * width, channels)
    hidden = conv_rows(image, work, win, width, taps)
    kv[...] = dot_nn(hidden, wkv).astype(jnp.bfloat16).reshape(win, width, 2 * channels)
    turned = dot_nt(wkv.T, hidden).astype(jnp.bfloat16)
    for r in range(win):
        kv_t[r] = turned[:, r * width : (r + 1) * width]


def places_of(scalars, rows, b, side):
    return [
        (
            scalars[1 + (b * 2 + side) * BAND + s],
            scalars[1 + rows * 2 * BAND + side * BAND + s] == 1,
        )
        for s in range(BAND)
    ]


def side_scores(places, kv, pair_b, width, channels):
    keys = jnp.concatenate([kv[at] for at, _ in places], axis=0)
    both = dot_nt(keys, pair_b)
    expo = jnp.exp2(both[:, :width] * (channels**-0.5 * LOG2E))
    expo = jnp.concatenate(
        [
            jnp.where(live, expo[i * width : (i + 1) * width], 0.0)
            for i, (_, live) in enumerate(places)
        ],
        axis=0,
    )
    return expo, both[:, width:]


def squared(queries_b, cotangent_b, square):
    width, channels = queries_b.shape
    square[...] = jnp.zeros_like(square)
    square[:width, :channels] = queries_b
    square[width:, channels:] = cotangent_b


def first_kernel(
    scalars,
    own,
    slab,
    within,
    between,
    conv_weight,
    q_weight,
    k_weight,
    v_weight,
    cotangent,
    queries,
    kv_t,
    expo,
    grad_probs,
    taps,
    wkv,
    image,
    work,
    kv,
    square,
):
    rows, width, channels = own.shape
    halo = MARGIN + 1
    odd = scalars[0] == 1
    taps[...] = stacked_taps(conv_weight)
    wkv[...] = jnp.concatenate([k_weight[...], v_weight[...]], axis=1)

    above, below = margins_of(odd, between[halo], within[halo])
    image[0:width, :] = above
    image[width : (rows + 1) * width, :] = own[...].reshape(rows * width, channels)
    image[(rows + 1) * width : (rows + 2) * width, :] = below
    hidden = conv_rows(image, work, rows, width, taps[...])
    queries[...] = (
        dot_nn(hidden, q_weight[...]).astype(jnp.bfloat16).reshape(rows, width, channels)
    )

    side_keys(slab[...], odd, between, within, image, work, taps[...], wkv[...], kv, kv_t)
    for b in range(rows):
        squared(queries[b], cotangent[b], square.at[b])
        expo[b], grad_probs[b] = side_scores(
            places_of(scalars, rows, b, 1), kv, square[b], width, channels
        )


def second_kernel(
    scalars,
    queries,
    cotangent,
    slab,
    within,
    between,
    taps,
    wkv,
    first_expo,
    first_grad_probs,
    for_within,
    second_for_between,
    first_for_between,
    center,
    probs_out,
    grad_scores_out,
    kv_t,
    image,
    work,
    kv,
    square,
    acc,
):
    rows, width, channels = slab.shape
    odd = scalars[0] == 1
    acc[...] = jnp.zeros_like(acc)
    side_keys(slab[...], odd, between, within, image, work, taps[...], wkv[...], kv, kv_t)

    for b in range(rows):
        squared(queries[b], cotangent[b], square.at[b])
        places = [places_of(scalars, rows, b, side) for side in range(2)]
        expo, grad_probs = side_scores(places[0], kv, square[b], width, channels)
        expo = jnp.concatenate([expo, first_expo[b]], axis=0)
        grad_probs = jnp.concatenate([grad_probs, first_grad_probs[b]], axis=0)
        probs = expo * (1.0 / jnp.sum(expo, axis=0, keepdims=True))
        probs_bf = probs.astype(jnp.bfloat16)
        delta = jnp.sum(probs * grad_probs, axis=0, keepdims=True)
        grad_scores = (probs * (grad_probs - delta)).astype(jnp.bfloat16)
        probs_out[b] = probs_bf
        grad_scores_out[b] = grad_scores
        terms = dot_nn(jnp.concatenate([grad_scores, probs_bf], axis=1), square[b])
        for side in range(2):
            for s, (at, _) in enumerate(places[side]):
                i = side * BAND + s
                acc[side, at] += terms[i * width : (i + 1) * width]

    for side, for_between in enumerate((second_for_between, first_for_between)):
        back = back_projected(acc[side], wkv[...])
        top, bottom = back[:MARGIN], back[MARGIN + rows :]
        span = slice(side * MARGIN, (side + 1) * MARGIN)
        for_within[span] = jnp.where(odd, top, bottom).astype(jnp.bfloat16)
        for_between[...] = jnp.where(odd, bottom, top).astype(jnp.bfloat16)
        center[side] = back[MARGIN : MARGIN + rows]


def back_projected(grads, wkv):
    rows, width, both = grads.shape
    channels = both // 2
    grads = jnp.concatenate(
        [grads[:, :, :channels] * channels**-0.5, grads[:, :, channels:]], axis=2
    ).astype(jnp.bfloat16)
    return dot_nt(grads.reshape(rows * width, both), wkv).reshape(rows, width, channels)


def third_kernel(
    scalars,
    probs,
    grad_scores,
    kv_t,
    first_kv_t,
    q_weight,
    attended,
    grad_own,
):
    rows, width, channels = attended.shape
    grad_q = []
    for b in range(rows):
        places = [places_of(scalars, rows, b, side) for side in range(2)]
        keys_t = jnp.concatenate(
            [kv_t[at] for at, _ in places[0]] + [first_kv_t[at] for at, _ in places[1]], axis=1
        )
        attended[b] = dot_nn(keys_t[channels:], probs[b]).T.astype(jnp.bfloat16)
        grad_q.append(dot_nn(keys_t[:channels], grad_scores[b]))
    grad_q = jnp.concatenate(grad_q, axis=1) * channels**-0.5
    turned = dot_nn(q_weight[...], grad_q.astype(jnp.bfloat16))
    for b in range(rows):
        grad_own[b] = turned[:, b * width : (b + 1) * width].T


def on_device(kernel, out_shape, scratch, flops, *arrays):
    smem = pl.BlockSpec(memory_space=pltpu.SMEM)
    vmem = pl.BlockSpec(memory_space=pltpu.VMEM)
    return pl.pallas_call(
        kernel,
        out_shape=tuple(jax.ShapeDtypeStruct(*one) for one in out_shape),
        in_specs=[smem if one.dtype == jnp.int32 else vmem for one in arrays],
        out_specs=tuple(smem if one[1] == jnp.int32 else vmem for one in out_shape),
        scratch_shapes=[pltpu.VMEM(*one) for one in scratch],
        compiler_params=pltpu.CompilerParams(vmem_limit_bytes=14 * 1024 * 1024),
        cost_estimate=pl.CostEstimate(
            flops=flops, bytes_accessed=flops // 1000, transcendentals=0
        ),
    )(*arrays)


def local(
    features_in,
    conv_weight,
    q_weight,
    k_weight,
    v_weight,
    partners,
    band_widths,
    bands,
    grad_attended,
):
    image = features_in[0]
    rows, width, channels = image.shape
    halo = MARGIN + 1
    win = rows + 2 * MARGIN
    half, full = jnp.bfloat16, jnp.float32
    views = lax.axis_size("cam")
    samples = views // min(16, views)
    ring = views // samples
    count = lax.axis_size("row")

    def routed(value, evens, odds):
        pairs = []
        for c in range(views):
            step = odds if (c // samples) % 2 else evens
            pairs.append((c, (c // samples + step) % ring * samples + c % samples))
        return lax.ppermute(value, "cam", pairs)

    camera = lax.axis_index("cam")
    slab = lax.axis_index("row")
    odd_place = (camera if samples == 1 else lax.div(camera, samples)) & 1
    odd_row = (slab & 1) == 1
    even_row = (slab & 1) == 0
    on = (2 - 4 * odd_place) * samples

    def around(place):
        return place & (views - 1) if views & (views - 1) == 0 else lax.rem(place + views, views)

    near_partner = np.arange(views)[:, None] + samples * np.array([[-1, 1]])
    near = (partners == np.mod(near_partner, views).astype(np.int32)).astype(full)
    near = jnp.broadcast_to(near.reshape(2 * views, 1), (2 * views, channels))
    near = lax.optimization_barrier(near)

    def is_near(other, side):
        place = (2 * other + side, jnp.int32(0))
        row = lax.dynamic_slice(near, place, (1, channels), allow_negative_indices=False)
        return row[None] > 0.5

    def across(value, evens, odds):
        pairs = []
        for c in range(views):
            step = odds if (c // samples) % 2 else evens
            to = (c // samples + step) % ring * samples + c % samples
            for r in range(1, count - 1, 2):
                pairs += [(c * count + r, to * count + r + 1), (c * count + r + 1, to * count + r)]
        return lax.ppermute(value, ("cam", "row"), pairs)

    second_near = is_near(around(camera + on), odd_place)
    first_near = is_near(camera, odd_place ^ 1)
    first_near_back = is_near(around(camera - on), odd_place ^ 1)
    pair_slab = routed(image, 1, -1)
    far_slab = routed(image, -2, 2)
    passed_on = jnp.where(second_near, pair_slab, image)
    second_slab = routed(passed_on, 2, -2)
    second_between = across(
        jnp.where(odd_row, passed_on[rows - halo :], passed_on[:halo]), 2, -2
    )
    far_slab, _ = lax.optimization_barrier((far_slab, passed_on))
    first_slab = jnp.where(~first_near, far_slab, pair_slab)
    to_next = jnp.concatenate([first_slab[rows - halo :], image[rows - 1 :]])
    to_previous = jnp.concatenate([first_slab[:halo], image[:1]])
    for_between, for_within = parity_split(to_next, to_previous, odd_row)
    between, within = swap_between(for_between), swap_within(for_within)
    bands, band_widths, even_row, _ = lax.optimization_barrier(
        (bands, band_widths, even_row, for_between)
    )

    widths_here = lax.dynamic_slice(
        band_widths, (camera, 0), (1, 2), allow_negative_indices=False
    )[0]
    live = jnp.arange(BAND, dtype=jnp.int32)[None, :] < widths_here[:, None]
    places = jnp.clip(bands[0] - (slab * rows - MARGIN), 0, win - 1)
    live = jnp.where(odd_place == 1, live[::-1], live)
    places = jnp.where(odd_place == 1, places[:, ::-1], places)
    scalars = jnp.concatenate(
        [
            odd_row.astype(jnp.int32).reshape(1),
            places.reshape(-1),
            live.reshape(-1).astype(jnp.int32),
        ]
    )

    conv_scratch = [
        (((win + 2) * width, channels), half),
        ((win * width + 16, 3 * channels), full),
        ((win, width, 2 * channels), half),
        ((rows, 2 * width, 2 * channels), half),
    ]
    queries, first_kv_t, first_expo, first_grad_probs, taps, wkv = on_device(
        first_kernel,
        [
            (image.shape, half),
            ((win, 2 * channels, width), half),
            ((rows, BAND * width, width), full),
            ((rows, BAND * width, width), full),
            ((3 * channels, 3 * channels), half),
            ((channels, 2 * channels), half),
        ],
        conv_scratch,
        1_000_000,
        scalars,
        image,
        first_slab,
        within,
        between,
        conv_weight,
        q_weight,
        k_weight,
        v_weight,
        grad_attended[0],
    )
    second_within = swap_within(
        jnp.where(odd_row, second_slab[:halo], second_slab[rows - halo :])
    )
    margins = ((MARGIN, width, channels), half)
    weights = ((rows, 2 * BAND * width, width), half)
    for_within, second_for_between, first_for_between, center, probs, grad_scores, kv_t = on_device(
        second_kernel,
        [
            ((2 * MARGIN, width, channels), half),
            margins,
            margins,
            ((2, rows, width, channels), full),
            weights,
            weights,
            ((win, 2 * channels, width), half),
        ],
        conv_scratch + [((2, win, width, 2 * channels), full)],
        1_500_000_000,
        scalars,
        queries,
        grad_attended[0],
        second_slab,
        second_within,
        second_between,
        taps,
        wkv,
        first_expo,
        first_grad_probs,
    )
    within = swap_within(for_within)
    second_between = across(second_for_between, -2, 2)

    def spread(part, onto_first):
        part = part.astype(full)
        none = jnp.zeros((rows - 2 * MARGIN, width, channels), full)
        return jnp.concatenate(
            [jnp.where(onto_first, part, 0.0), none, jnp.where(onto_first, 0.0, part)], axis=0
        )

    second = (center[0] + spread(within[:MARGIN], odd_row)).astype(half)
    from_second = routed(second, -2, 2)
    first_for_between, _ = lax.optimization_barrier((first_for_between, second))
    first_between = swap_between(first_for_between)
    attended, grad_own = on_device(
        third_kernel,
        [(image.shape, half), (image.shape, full)],
        [],
        1_000_000,
        scalars,
        probs,
        grad_scores,
        kv_t,
        first_kv_t,
        q_weight,
    )
    first = center[1] + spread(within[MARGIN:], odd_row) + spread(first_between, even_row)
    first = first.astype(half)
    from_first = routed(first, 2, -2)
    from_second, second_between, _ = lax.optimization_barrier(
        (from_second, second_between, first)
    )
    from_second = from_second.astype(full) + spread(second_between, even_row)
    for_pair = jnp.where(first_near, first.astype(full), 0.0) + jnp.where(
        second_near, from_second, 0.0
    )
    from_pair = routed(for_pair.astype(half), 1, -1)
    summed = grad_own + from_pair.astype(full)
    summed = summed + jnp.where(second_near, 0.0, from_second)
    summed = summed + jnp.where(first_near_back, 0.0, from_first.astype(full))
    return (attended[None], summed.astype(half)[None])


def solution(mesh):
    placed = (
        P("cam", "row", None, None),
        P(),
        P(),
        P(),
        P(),
        P(),
        P(),
        P("cam", "row", None, None),
        P("cam", "row", None, None),
    )
    return jax.shard_map(
        local,
        mesh=mesh,
        in_specs=placed,
        out_specs=(P("cam", "row", None, None), P("cam", "row", None, None)),
        check_vma=False,
    )
```

```python
import jax
import jax.numpy as jnp
import numpy as np
from jax import lax
from jax.experimental import pallas as pl
from jax.experimental.pallas import tpu as pltpu
from jax.sharding import PartitionSpec as P

MARGIN = 2
BAND = 3
LOG2E = 1.4426950408889634


def swap_within(value):
    pairs = [(i, i + 1) for i in range(0, lax.axis_size("row") - 1, 2)]
    return lax.ppermute(value, "row", pairs + [(j, i) for i, j in pairs])


def swap_between(value):
    pairs = [(i, i + 1) for i in range(1, lax.axis_size("row") - 1, 2)]
    return lax.ppermute(value, "row", pairs + [(j, i) for i, j in pairs])


def parity_split(to_next, to_previous, odd):
    return jnp.where(odd, to_next, to_previous), jnp.where(odd, to_previous, to_next)


def margins_of(odd, between, within):
    return jnp.where(odd, within, between), jnp.where(odd, between, within)


def dot_nn(a, b):
    return lax.dot_general(a, b, (((1,), (0,)), ((), ())), preferred_element_type=jnp.float32)


def dot_nt(a, b):
    return lax.dot_general(a, b, (((1,), (1,)), ((), ())), preferred_element_type=jnp.float32)


def stacked_taps(conv_weight):
    return jnp.concatenate(
        [jnp.concatenate([conv_weight[i, j] for j in range(3)], axis=1) for i in range(3)], axis=0
    )


def conv_rows(image, work, out_rows, width, taps):
    count = out_rows * width
    channels = taps.shape[1] // 3
    stacked = jnp.concatenate([image[i * width : i * width + count, :] for i in range(3)], axis=1)
    work[8 : 8 + count, :] = dot_nn(stacked, taps)
    none = jnp.zeros((1, channels), jnp.float32)
    for i in range(out_rows + 1):
        work[7 + i * width : 8 + i * width, :channels] = none
        work[8 + i * width : 9 + i * width, 2 * channels :] = none
    total = work[8 : 8 + count, channels : 2 * channels]
    total = total + work[7 : 7 + count, :channels]
    total = total + work[9 : 9 + count, 2 * channels :]
    return total.astype(jnp.bfloat16)


def side_keys(slab, odd, between, within, image, work, taps, wkv, kv, kv_t):
    rows, width, channels = slab.shape
    halo = MARGIN + 1
    win = rows + 2 * MARGIN
    above, below = margins_of(odd, between[0:halo], within[0:halo])
    image[0 : halo * width, :] = above.reshape(halo * width, channels)
    image[halo * width : (halo + rows) * width, :] = slab.reshape(rows * width, channels)
    image[(halo + rows) * width :, :] = below.reshape(halo * width, channels)
    hidden = conv_rows(image, work, win, width, taps)
    kv[...] = dot_nn(hidden, wkv).astype(jnp.bfloat16).reshape(win, width, 2 * channels)
    turned = dot_nt(wkv.T, hidden).astype(jnp.bfloat16)
    for r in range(win):
        kv_t[r] = turned[:, r * width : (r + 1) * width]


def places_of(scalars, rows, b, side):
    return [
        (
            scalars[1 + (b * 2 + side) * BAND + s],
            scalars[1 + rows * 2 * BAND + side * BAND + s] == 1,
        )
        for s in range(BAND)
    ]


def side_scores(places, kv, pair_b, width, channels):
    keys = jnp.concatenate([kv[at] for at, _ in places], axis=0)
    both = dot_nt(keys, pair_b)
    expo = jnp.exp2(both[:, :width] * (channels**-0.5 * LOG2E))
    expo = jnp.concatenate(
        [
            jnp.where(live, expo[i * width : (i + 1) * width], 0.0)
            for i, (_, live) in enumerate(places)
        ],
        axis=0,
    )
    return expo, both[:, width:]


def squared(queries_b, cotangent_b, square):
    width, channels = queries_b.shape
    square[...] = jnp.zeros_like(square)
    square[:width, :channels] = queries_b
    square[width:, channels:] = cotangent_b


def first_kernel(
    scalars,
    own,
    slab,
    within,
    between,
    conv_weight,
    q_weight,
    k_weight,
    v_weight,
    cotangent,
    queries,
    kv_t,
    expo,
    grad_probs,
    taps,
    wkv,
    image,
    work,
    kv,
    square,
):
    rows, width, channels = own.shape
    halo = MARGIN + 1
    odd = scalars[0] == 1
    taps[...] = stacked_taps(conv_weight)
    wkv[...] = jnp.concatenate([k_weight[...], v_weight[...]], axis=1)

    above, below = margins_of(odd, between[halo], within[halo])
    image[0:width, :] = above
    image[width : (rows + 1) * width, :] = own[...].reshape(rows * width, channels)
    image[(rows + 1) * width : (rows + 2) * width, :] = below
    hidden = conv_rows(image, work, rows, width, taps[...])
    queries[...] = (
        dot_nn(hidden, q_weight[...]).astype(jnp.bfloat16).reshape(rows, width, channels)
    )

    side_keys(slab[...], odd, between, within, image, work, taps[...], wkv[...], kv, kv_t)
    for b in range(rows):
        squared(queries[b], cotangent[b], square.at[b])
        expo[b], grad_probs[b] = side_scores(
            places_of(scalars, rows, b, 1), kv, square[b], width, channels
        )


def second_kernel(
    scalars,
    queries,
    cotangent,
    slab,
    within,
    between,
    taps,
    wkv,
    first_expo,
    first_grad_probs,
    for_within,
    second_edges,
    first_edges,
    center,
    probs_out,
    grad_scores_out,
    kv_t,
    image,
    work,
    kv,
    square,
    acc,
):
    rows, width, channels = slab.shape
    odd = scalars[0] == 1
    acc[...] = jnp.zeros_like(acc)
    side_keys(slab[...], odd, between, within, image, work, taps[...], wkv[...], kv, kv_t)

    for b in range(rows):
        squared(queries[b], cotangent[b], square.at[b])
        places = [places_of(scalars, rows, b, side) for side in range(2)]
        expo, grad_probs = side_scores(places[0], kv, square[b], width, channels)
        expo = jnp.concatenate([expo, first_expo[b]], axis=0)
        grad_probs = jnp.concatenate([grad_probs, first_grad_probs[b]], axis=0)
        probs = expo * (1.0 / jnp.sum(expo, axis=0, keepdims=True))
        probs_bf = probs.astype(jnp.bfloat16)
        delta = jnp.sum(probs * grad_probs, axis=0, keepdims=True)
        grad_scores = (probs * (grad_probs - delta)).astype(jnp.bfloat16)
        probs_out[b] = probs_bf
        grad_scores_out[b] = grad_scores
        terms = dot_nn(jnp.concatenate([grad_scores, probs_bf], axis=1), square[b])
        for side in range(2):
            for s, (at, _) in enumerate(places[side]):
                i = side * BAND + s
                acc[side, at] += terms[i * width : (i + 1) * width]

    for side, edges in enumerate((second_edges, first_edges)):
        back = back_projected(acc[side], wkv[...])
        top, bottom = back[:MARGIN], back[MARGIN + rows :]
        span = slice(side * MARGIN, (side + 1) * MARGIN)
        for_within[span] = jnp.where(odd, top, bottom).astype(jnp.bfloat16)
        edges[:MARGIN] = top.astype(jnp.bfloat16)
        edges[MARGIN:] = bottom.astype(jnp.bfloat16)
        center[side] = back[MARGIN : MARGIN + rows]


def back_projected(grads, wkv):
    rows, width, both = grads.shape
    channels = both // 2
    grads = jnp.concatenate(
        [grads[:, :, :channels] * channels**-0.5, grads[:, :, channels:]], axis=2
    ).astype(jnp.bfloat16)
    return dot_nt(grads.reshape(rows * width, both), wkv).reshape(rows, width, channels)


def third_kernel(
    scalars,
    probs,
    grad_scores,
    kv_t,
    first_kv_t,
    q_weight,
    attended,
    grad_own,
):
    rows, width, channels = attended.shape
    grad_q = []
    for b in range(rows):
        places = [places_of(scalars, rows, b, side) for side in range(2)]
        keys_t = jnp.concatenate(
            [kv_t[at] for at, _ in places[0]] + [first_kv_t[at] for at, _ in places[1]], axis=1
        )
        attended[b] = dot_nn(keys_t[channels:], probs[b]).T.astype(jnp.bfloat16)
        grad_q.append(dot_nn(keys_t[:channels], grad_scores[b]))
    grad_q = jnp.concatenate(grad_q, axis=1) * channels**-0.5
    turned = dot_nn(q_weight[...], grad_q.astype(jnp.bfloat16))
    for b in range(rows):
        grad_own[b] = turned[:, b * width : (b + 1) * width].T


def on_device(kernel, out_shape, scratch, flops, *arrays):
    smem = pl.BlockSpec(memory_space=pltpu.SMEM)
    vmem = pl.BlockSpec(memory_space=pltpu.VMEM)
    return pl.pallas_call(
        kernel,
        out_shape=tuple(jax.ShapeDtypeStruct(*one) for one in out_shape),
        in_specs=[smem if one.dtype == jnp.int32 else vmem for one in arrays],
        out_specs=tuple(smem if one[1] == jnp.int32 else vmem for one in out_shape),
        scratch_shapes=[pltpu.VMEM(*one) for one in scratch],
        compiler_params=pltpu.CompilerParams(vmem_limit_bytes=14 * 1024 * 1024),
        cost_estimate=pl.CostEstimate(
            flops=flops, bytes_accessed=flops // 1000, transcendentals=0
        ),
    )(*arrays)


def local(
    features_in,
    conv_weight,
    q_weight,
    k_weight,
    v_weight,
    partners,
    band_widths,
    bands,
    grad_attended,
):
    image = features_in[0]
    rows, width, channels = image.shape
    halo = MARGIN + 1
    win = rows + 2 * MARGIN
    half, full = jnp.bfloat16, jnp.float32
    views = lax.axis_size("cam")
    samples = views // min(16, views)
    ring = views // samples
    count = lax.axis_size("row")

    def routed(value, evens, odds):
        pairs = []
        for c in range(views):
            step = odds if (c // samples) % 2 else evens
            pairs.append((c, (c // samples + step) % ring * samples + c % samples))
        return lax.ppermute(value, "cam", pairs)

    camera = lax.axis_index("cam")
    slab = lax.axis_index("row")
    odd_place = (camera if samples == 1 else lax.div(camera, samples)) & 1
    odd_row = (slab & 1) == 1
    even_row = (slab & 1) == 0
    on = (2 - 4 * odd_place) * samples

    def around(place):
        return place & (views - 1) if views & (views - 1) == 0 else lax.rem(place + views, views)

    near_partner = np.arange(views)[:, None] + samples * np.array([[-1, 1]])
    near = (partners == np.mod(near_partner, views).astype(np.int32)).astype(full)
    near = jnp.broadcast_to(near.reshape(2 * views, 1), (2 * views, channels))
    near = lax.optimization_barrier(near)

    def is_near(other, side):
        place = (2 * other + side, jnp.int32(0))
        row = lax.dynamic_slice(near, place, (1, channels), allow_negative_indices=False)
        return row[None] > 0.5

    def across(value, evens, odds):
        pairs = []
        for c in range(views):
            step = odds if (c // samples) % 2 else evens
            to = (c // samples + step) % ring * samples + c % samples
            for r in range(1, count - 1, 2):
                pairs += [(c * count + r, to * count + r + 1), (c * count + r + 1, to * count + r)]
        return lax.ppermute(value, ("cam", "row"), pairs)

    second_near = is_near(around(camera + on), odd_place)
    first_near = is_near(camera, odd_place ^ 1)
    first_near_back = is_near(around(camera - on), odd_place ^ 1)
    pair_slab = routed(image, 1, -1)
    far_slab = routed(image, -2, 2)
    passed_on = jnp.where(second_near, pair_slab, image)
    second_slab = routed(passed_on, 2, -2)
    second_between = across(
        jnp.where(odd_row, passed_on[rows - halo :], passed_on[:halo]), 2, -2
    )
    far_slab, _ = lax.optimization_barrier((far_slab, passed_on))
    first_slab = jnp.where(~first_near, far_slab, pair_slab)
    to_next = jnp.concatenate([first_slab[rows - halo :], image[rows - 1 :]])
    to_previous = jnp.concatenate([first_slab[:halo], image[:1]])
    for_between, for_within = parity_split(to_next, to_previous, odd_row)
    between, within = swap_between(for_between), swap_within(for_within)
    bands, band_widths, even_row, _ = lax.optimization_barrier(
        (bands, band_widths, even_row, for_between)
    )

    widths_here = lax.dynamic_slice(
        band_widths, (camera, 0), (1, 2), allow_negative_indices=False
    )[0]
    live = jnp.arange(BAND, dtype=jnp.int32)[None, :] < widths_here[:, None]
    places = jnp.clip(bands[0] - (slab * rows - MARGIN), 0, win - 1)
    live = jnp.where(odd_place == 1, live[::-1], live)
    places = jnp.where(odd_place == 1, places[:, ::-1], places)
    scalars = jnp.concatenate(
        [
            odd_row.astype(jnp.int32).reshape(1),
            places.reshape(-1),
            live.reshape(-1).astype(jnp.int32),
        ]
    )

    conv_scratch = [
        (((win + 2) * width, channels), half),
        ((win * width + 16, 3 * channels), full),
        ((win, width, 2 * channels), half),
        ((rows, 2 * width, 2 * channels), half),
    ]
    queries, first_kv_t, first_expo, first_grad_probs, taps, wkv = on_device(
        first_kernel,
        [
            (image.shape, half),
            ((win, 2 * channels, width), half),
            ((rows, BAND * width, width), full),
            ((rows, BAND * width, width), full),
            ((3 * channels, 3 * channels), half),
            ((channels, 2 * channels), half),
        ],
        conv_scratch,
        1_000_000,
        scalars,
        image,
        first_slab,
        within,
        between,
        conv_weight,
        q_weight,
        k_weight,
        v_weight,
        grad_attended[0],
    )
    second_within = swap_within(
        jnp.where(odd_row, second_slab[:halo], second_slab[rows - halo :])
    )
    margins = ((2 * MARGIN, width, channels), half)
    weights = ((rows, 2 * BAND * width, width), half)
    for_within, second_edges, first_edges, center, probs, grad_scores, kv_t = on_device(
        second_kernel,
        [
            ((2 * MARGIN, width, channels), half),
            margins,
            margins,
            ((2, rows, width, channels), full),
            weights,
            weights,
            ((win, 2 * channels, width), half),
        ],
        conv_scratch + [((2, win, width, 2 * channels), full)],
        1_500_000_000,
        scalars,
        queries,
        grad_attended[0],
        second_slab,
        second_within,
        second_between,
        taps,
        wkv,
        first_expo,
        first_grad_probs,
    )
    within = swap_within(for_within)

    def spread(part, onto_first):
        part = part.astype(full)
        none = jnp.zeros((rows - 2 * MARGIN, width, channels), full)
        return jnp.concatenate(
            [jnp.where(onto_first, part, 0.0), none, jnp.where(onto_first, 0.0, part)], axis=0
        )

    second = (center[0] + spread(within[:MARGIN], odd_row)).astype(half)
    from_second = routed(second, -2, 2)
    second_edges, first_edges, _ = lax.optimization_barrier((second_edges, first_edges, second))
    second_between = across(
        jnp.where(odd_row, second_edges[MARGIN:], second_edges[:MARGIN]), -2, 2
    )
    first_between = swap_between(
        jnp.where(odd_row, first_edges[MARGIN:], first_edges[:MARGIN])
    )
    attended, grad_own = on_device(
        third_kernel,
        [(image.shape, half), (image.shape, full)],
        [],
        1_000_000,
        scalars,
        probs,
        grad_scores,
        kv_t,
        first_kv_t,
        q_weight,
    )
    first = center[1] + spread(within[MARGIN:], odd_row) + spread(first_between, even_row)
    first = first.astype(half)
    from_first = routed(first, 2, -2)
    from_second, second_between, _ = lax.optimization_barrier(
        (from_second, second_between, first)
    )
    from_second = from_second.astype(full) + spread(second_between, even_row)
    for_pair = jnp.where(first_near, first.astype(full), 0.0) + jnp.where(
        second_near, from_second, 0.0
    )
    from_pair = routed(for_pair.astype(half), 1, -1)
    summed = grad_own + from_pair.astype(full)
    summed = summed + jnp.where(second_near, 0.0, from_second)
    summed = summed + jnp.where(first_near_back, 0.0, from_first.astype(full))
    return (attended[None], summed.astype(half)[None])


def solution(mesh):
    placed = (
        P("cam", "row", None, None),
        P(),
        P(),
        P(),
        P(),
        P(),
        P(),
        P("cam", "row", None, None),
        P("cam", "row", None, None),
    )
    return jax.shard_map(
        local,
        mesh=mesh,
        in_specs=placed,
        out_specs=(P("cam", "row", None, None), P("cam", "row", None, None)),
        check_vma=False,
    )
```

```python
import jax
import jax.numpy as jnp
import numpy as np
from jax import lax
from jax.experimental import pallas as pl
from jax.experimental.pallas import tpu as pltpu
from jax.sharding import PartitionSpec as P

MARGIN = 2
BAND = 3
LOG2E = 1.4426950408889634


def swap_within(value):
    pairs = [(i, i + 1) for i in range(0, lax.axis_size("row") - 1, 2)]
    return lax.ppermute(value, "row", pairs + [(j, i) for i, j in pairs])


def swap_between(value):
    pairs = [(i, i + 1) for i in range(1, lax.axis_size("row") - 1, 2)]
    return lax.ppermute(value, "row", pairs + [(j, i) for i, j in pairs])


def parity_split(to_next, to_previous, odd):
    return jnp.where(odd, to_next, to_previous), jnp.where(odd, to_previous, to_next)


def margins_of(odd, between, within):
    return jnp.where(odd, within, between), jnp.where(odd, between, within)


def dot_nn(a, b):
    return lax.dot_general(a, b, (((1,), (0,)), ((), ())), preferred_element_type=jnp.float32)


def dot_nt(a, b):
    return lax.dot_general(a, b, (((1,), (1,)), ((), ())), preferred_element_type=jnp.float32)


def stacked_taps(conv_weight):
    return jnp.concatenate(
        [jnp.concatenate([conv_weight[i, j] for j in range(3)], axis=1) for i in range(3)], axis=0
    )


def conv_rows(image, work, out_rows, width, taps):
    count = out_rows * width
    channels = taps.shape[1] // 3
    stacked = jnp.concatenate([image[i * width : i * width + count, :] for i in range(3)], axis=1)
    work[8 : 8 + count, :] = dot_nn(stacked, taps)
    none = jnp.zeros((1, channels), jnp.float32)
    for i in range(out_rows + 1):
        work[7 + i * width : 8 + i * width, :channels] = none
        work[8 + i * width : 9 + i * width, 2 * channels :] = none
    total = work[8 : 8 + count, channels : 2 * channels]
    total = total + work[7 : 7 + count, :channels]
    total = total + work[9 : 9 + count, 2 * channels :]
    return total.astype(jnp.bfloat16)


def side_keys(slab, odd, between, within, image, work, taps, wkv, kv, kv_t):
    rows, width, channels = slab.shape
    halo = MARGIN + 1
    win = rows + 2 * MARGIN
    above, below = margins_of(odd, between[0:halo], within[0:halo])
    image[0 : halo * width, :] = above.reshape(halo * width, channels)
    image[halo * width : (halo + rows) * width, :] = slab.reshape(rows * width, channels)
    image[(halo + rows) * width :, :] = below.reshape(halo * width, channels)
    hidden = conv_rows(image, work, win, width, taps)
    kv[...] = dot_nn(hidden, wkv).astype(jnp.bfloat16).reshape(win, width, 2 * channels)
    turned = dot_nt(wkv.T, hidden).astype(jnp.bfloat16)
    for r in range(win):
        kv_t[r] = turned[:, r * width : (r + 1) * width]


def places_of(scalars, rows, b, side):
    return [
        (
            scalars[1 + (b * 2 + side) * BAND + s],
            scalars[1 + rows * 2 * BAND + side * BAND + s] == 1,
        )
        for s in range(BAND)
    ]


def side_scores(places, kv, pair_b, width, channels):
    keys = jnp.concatenate([kv[at] for at, _ in places], axis=0)
    both = dot_nt(keys, pair_b)
    expo = jnp.exp2(both[:, :width] * (channels**-0.5 * LOG2E))
    expo = jnp.concatenate(
        [
            jnp.where(live, expo[i * width : (i + 1) * width], 0.0)
            for i, (_, live) in enumerate(places)
        ],
        axis=0,
    )
    return expo, both[:, width:]


def squared(queries_b, cotangent_b, square):
    width, channels = queries_b.shape
    square[...] = jnp.zeros_like(square)
    square[:width, :channels] = queries_b
    square[width:, channels:] = cotangent_b


def first_kernel(
    scalars,
    own,
    slab,
    within,
    between,
    conv_weight,
    q_weight,
    k_weight,
    v_weight,
    cotangent,
    queries,
    kv_t,
    expo,
    grad_probs,
    taps,
    wkv,
    image,
    work,
    kv,
    square,
):
    rows, width, channels = own.shape
    halo = MARGIN + 1
    odd = scalars[0] == 1
    taps[...] = stacked_taps(conv_weight)
    wkv[...] = jnp.concatenate([k_weight[...], v_weight[...]], axis=1)

    above, below = margins_of(odd, between[halo], within[halo])
    image[0:width, :] = above
    image[width : (rows + 1) * width, :] = own[...].reshape(rows * width, channels)
    image[(rows + 1) * width : (rows + 2) * width, :] = below
    hidden = conv_rows(image, work, rows, width, taps[...])
    queries[...] = (
        dot_nn(hidden, q_weight[...]).astype(jnp.bfloat16).reshape(rows, width, channels)
    )

    side_keys(slab[...], odd, between, within, image, work, taps[...], wkv[...], kv, kv_t)
    for b in range(rows):
        squared(queries[b], cotangent[b], square.at[b])
        expo[b], grad_probs[b] = side_scores(
            places_of(scalars, rows, b, 1), kv, square[b], width, channels
        )


def second_kernel(
    scalars,
    queries,
    cotangent,
    slab,
    within,
    between,
    taps,
    wkv,
    first_expo,
    first_grad_probs,
    for_within,
    second_edges,
    first_edges,
    center,
    probs_out,
    grad_scores_out,
    kv_t,
    image,
    work,
    kv,
    square,
    acc,
):
    rows, width, channels = slab.shape
    odd = scalars[0] == 1
    acc[...] = jnp.zeros_like(acc)
    side_keys(slab[...], odd, between, within, image, work, taps[...], wkv[...], kv, kv_t)

    for b in range(rows):
        squared(queries[b], cotangent[b], square.at[b])
        places = [places_of(scalars, rows, b, side) for side in range(2)]
        expo, grad_probs = side_scores(places[0], kv, square[b], width, channels)
        expo = jnp.concatenate([expo, first_expo[b]], axis=0)
        grad_probs = jnp.concatenate([grad_probs, first_grad_probs[b]], axis=0)
        probs = expo * (1.0 / jnp.sum(expo, axis=0, keepdims=True))
        probs_bf = probs.astype(jnp.bfloat16)
        delta = jnp.sum(probs * grad_probs, axis=0, keepdims=True)
        grad_scores = (probs * (grad_probs - delta)).astype(jnp.bfloat16)
        probs_out[b] = probs_bf
        grad_scores_out[b] = grad_scores
        terms = dot_nn(jnp.concatenate([grad_scores, probs_bf], axis=1), square[b])
        for side in range(2):
            for s, (at, _) in enumerate(places[side]):
                i = side * BAND + s
                acc[side, at] += terms[i * width : (i + 1) * width]

    for side, edges in enumerate((second_edges, first_edges)):
        back = back_projected(acc[side], wkv[...])
        top, bottom = back[:MARGIN], back[MARGIN + rows :]
        span = slice(side * MARGIN, (side + 1) * MARGIN)
        for_within[span] = jnp.where(odd, top, bottom).astype(jnp.bfloat16)
        edges[:MARGIN] = top.astype(jnp.bfloat16)
        edges[MARGIN:] = bottom.astype(jnp.bfloat16)
        center[side] = back[MARGIN : MARGIN + rows]


def back_projected(grads, wkv):
    rows, width, both = grads.shape
    channels = both // 2
    grads = jnp.concatenate(
        [grads[:, :, :channels] * channels**-0.5, grads[:, :, channels:]], axis=2
    ).astype(jnp.bfloat16)
    return dot_nt(grads.reshape(rows * width, both), wkv).reshape(rows, width, channels)


def third_kernel(
    scalars,
    probs,
    grad_scores,
    kv_t,
    first_kv_t,
    q_weight,
    attended,
    grad_own,
):
    rows, width, channels = attended.shape
    grad_q = []
    for b in range(rows):
        places = [places_of(scalars, rows, b, side) for side in range(2)]
        keys_t = jnp.concatenate(
            [kv_t[at] for at, _ in places[0]] + [first_kv_t[at] for at, _ in places[1]], axis=1
        )
        attended[b] = dot_nn(keys_t[channels:], probs[b]).T.astype(jnp.bfloat16)
        grad_q.append(dot_nn(keys_t[:channels], grad_scores[b]))
    grad_q = jnp.concatenate(grad_q, axis=1) * channels**-0.5
    turned = dot_nn(q_weight[...], grad_q.astype(jnp.bfloat16))
    for b in range(rows):
        grad_own[b] = turned[:, b * width : (b + 1) * width].T


def on_device(kernel, out_shape, scratch, flops, *arrays):
    smem = pl.BlockSpec(memory_space=pltpu.SMEM)
    vmem = pl.BlockSpec(memory_space=pltpu.VMEM)
    return pl.pallas_call(
        kernel,
        out_shape=tuple(jax.ShapeDtypeStruct(*one) for one in out_shape),
        in_specs=[smem if one.dtype == jnp.int32 else vmem for one in arrays],
        out_specs=tuple(smem if one[1] == jnp.int32 else vmem for one in out_shape),
        scratch_shapes=[pltpu.VMEM(*one) for one in scratch],
        compiler_params=pltpu.CompilerParams(vmem_limit_bytes=14 * 1024 * 1024),
        cost_estimate=pl.CostEstimate(
            flops=flops, bytes_accessed=flops // 1000, transcendentals=0
        ),
    )(*arrays)


def local(
    features_in,
    conv_weight,
    q_weight,
    k_weight,
    v_weight,
    partners,
    band_widths,
    bands,
    grad_attended,
):
    image = features_in[0]
    rows, width, channels = image.shape
    halo = MARGIN + 1
    win = rows + 2 * MARGIN
    half, full = jnp.bfloat16, jnp.float32
    views = lax.axis_size("cam")
    samples = views // min(16, views)
    ring = views // samples
    count = lax.axis_size("row")

    def routed(value, evens, odds):
        pairs = []
        for c in range(views):
            step = odds if (c // samples) % 2 else evens
            pairs.append((c, (c // samples + step) % ring * samples + c % samples))
        return lax.ppermute(value, "cam", pairs)

    camera = lax.axis_index("cam")
    slab = lax.axis_index("row")
    odd_place = (camera if samples == 1 else lax.div(camera, samples)) & 1
    odd_row = (slab & 1) == 1
    even_row = (slab & 1) == 0
    on = (2 - 4 * odd_place) * samples

    def around(place):
        return place & (views - 1) if views & (views - 1) == 0 else lax.rem(place + views, views)

    near_partner = np.arange(views)[:, None] + samples * np.array([[-1, 1]])
    near = (partners == np.mod(near_partner, views).astype(np.int32)).astype(full)
    near = jnp.broadcast_to(near.reshape(2 * views, 1), (2 * views, channels))
    near = lax.optimization_barrier(near)

    def is_near(other, side):
        place = (2 * other + side, jnp.int32(0))
        row = lax.dynamic_slice(near, place, (1, channels), allow_negative_indices=False)
        return row[None] > 0.5

    def across(value, evens, odds):
        pairs = []
        for c in range(views):
            step = odds if (c // samples) % 2 else evens
            to = (c // samples + step) % ring * samples + c % samples
            for r in range(1, count - 1, 2):
                pairs += [(c * count + r, to * count + r + 1), (c * count + r + 1, to * count + r)]
        return lax.ppermute(value, ("cam", "row"), pairs)

    second_near = is_near(around(camera + on), odd_place)
    first_near = is_near(camera, odd_place ^ 1)
    first_near_back = is_near(around(camera - on), odd_place ^ 1)
    pair_slab = routed(image, 1, -1)
    far_slab = routed(image, -2, 2)
    passed_on = jnp.where(second_near, pair_slab, image)
    second_slab = routed(passed_on, 2, -2)
    far_slab, _ = lax.optimization_barrier((far_slab, passed_on))
    first_slab = jnp.where(~first_near, far_slab, pair_slab)
    to_next = jnp.concatenate([first_slab[rows - halo :], image[rows - 1 :]])
    to_previous = jnp.concatenate([first_slab[:halo], image[:1]])
    for_between, for_within = parity_split(to_next, to_previous, odd_row)
    between, within = swap_between(for_between), swap_within(for_within)
    _, bands, band_widths, even_row, edge = lax.optimization_barrier(
        (for_between, bands, band_widths, even_row, passed_on)
    )
    second_between = across(jnp.where(odd_row, edge[rows - halo :], edge[:halo]), 2, -2)

    widths_here = lax.dynamic_slice(
        band_widths, (camera, 0), (1, 2), allow_negative_indices=False
    )[0]
    live = jnp.arange(BAND, dtype=jnp.int32)[None, :] < widths_here[:, None]
    places = jnp.clip(bands[0] - (slab * rows - MARGIN), 0, win - 1)
    live = jnp.where(odd_place == 1, live[::-1], live)
    places = jnp.where(odd_place == 1, places[:, ::-1], places)
    scalars = jnp.concatenate(
        [
            odd_row.astype(jnp.int32).reshape(1),
            places.reshape(-1),
            live.reshape(-1).astype(jnp.int32),
        ]
    )

    conv_scratch = [
        (((win + 2) * width, channels), half),
        ((win * width + 16, 3 * channels), full),
        ((win, width, 2 * channels), half),
        ((rows, 2 * width, 2 * channels), half),
    ]
    queries, first_kv_t, first_expo, first_grad_probs, taps, wkv = on_device(
        first_kernel,
        [
            (image.shape, half),
            ((win, 2 * channels, width), half),
            ((rows, BAND * width, width), full),
            ((rows, BAND * width, width), full),
            ((3 * channels, 3 * channels), half),
            ((channels, 2 * channels), half),
        ],
        conv_scratch,
        1_000_000,
        scalars,
        image,
        first_slab,
        within,
        between,
        conv_weight,
        q_weight,
        k_weight,
        v_weight,
        grad_attended[0],
    )
    second_within = swap_within(
        jnp.where(odd_row, second_slab[:halo], second_slab[rows - halo :])
    )
    margins = ((2 * MARGIN, width, channels), half)
    weights = ((rows, 2 * BAND * width, width), half)
    for_within, second_edges, first_edges, center, probs, grad_scores, kv_t = on_device(
        second_kernel,
        [
            ((2 * MARGIN, width, channels), half),
            margins,
            margins,
            ((2, rows, width, channels), full),
            weights,
            weights,
            ((win, 2 * channels, width), half),
        ],
        conv_scratch + [((2, win, width, 2 * channels), full)],
        1_500_000_000,
        scalars,
        queries,
        grad_attended[0],
        second_slab,
        second_within,
        second_between,
        taps,
        wkv,
        first_expo,
        first_grad_probs,
    )
    within = swap_within(for_within)

    def spread(part, onto_first):
        part = part.astype(full)
        none = jnp.zeros((rows - 2 * MARGIN, width, channels), full)
        return jnp.concatenate(
            [jnp.where(onto_first, part, 0.0), none, jnp.where(onto_first, 0.0, part)], axis=0
        )

    second = (center[0] + spread(within[:MARGIN], odd_row)).astype(half)
    from_second = routed(second, -2, 2)
    second_edges, first_edges, _ = lax.optimization_barrier((second_edges, first_edges, second))
    second_between = across(
        jnp.where(odd_row, second_edges[MARGIN:], second_edges[:MARGIN]), -2, 2
    )
    first_between = swap_between(
        jnp.where(odd_row, first_edges[MARGIN:], first_edges[:MARGIN])
    )
    attended, grad_own = on_device(
        third_kernel,
        [(image.shape, half), (image.shape, full)],
        [],
        1_000_000,
        scalars,
        probs,
        grad_scores,
        kv_t,
        first_kv_t,
        q_weight,
    )
    first = center[1] + spread(within[MARGIN:], odd_row) + spread(first_between, even_row)
    first = first.astype(half)
    from_first = routed(first, 2, -2)
    from_second, second_between, _ = lax.optimization_barrier(
        (from_second, second_between, first)
    )
    from_second = from_second.astype(full) + spread(second_between, even_row)
    for_pair = jnp.where(first_near, first.astype(full), 0.0) + jnp.where(
        second_near, from_second, 0.0
    )
    from_pair = routed(for_pair.astype(half), 1, -1)
    summed = grad_own + from_pair.astype(full)
    summed = summed + jnp.where(second_near, 0.0, from_second)
    summed = summed + jnp.where(first_near_back, 0.0, from_first.astype(full))
    return (attended[None], summed.astype(half)[None])


def solution(mesh):
    placed = (
        P("cam", "row", None, None),
        P(),
        P(),
        P(),
        P(),
        P(),
        P(),
        P("cam", "row", None, None),
        P("cam", "row", None, None),
    )
    return jax.shard_map(
        local,
        mesh=mesh,
        in_specs=placed,
        out_specs=(P("cam", "row", None, None), P("cam", "row", None, None)),
        check_vma=False,
    )
```

```python
import jax
import jax.numpy as jnp
import numpy as np
from jax import lax
from jax.experimental import pallas as pl
from jax.experimental.pallas import tpu as pltpu
from jax.sharding import PartitionSpec as P

MARGIN = 2
BAND = 3
LOG2E = 1.4426950408889634


def swap_within(value):
    pairs = [(i, i + 1) for i in range(0, lax.axis_size("row") - 1, 2)]
    return lax.ppermute(value, "row", pairs + [(j, i) for i, j in pairs])


def swap_between(value):
    pairs = [(i, i + 1) for i in range(1, lax.axis_size("row") - 1, 2)]
    return lax.ppermute(value, "row", pairs + [(j, i) for i, j in pairs])


def parity_split(to_next, to_previous, odd):
    return jnp.where(odd, to_next, to_previous), jnp.where(odd, to_previous, to_next)


def margins_of(odd, between, within):
    return jnp.where(odd, within, between), jnp.where(odd, between, within)


def dot_nn(a, b):
    return lax.dot_general(a, b, (((1,), (0,)), ((), ())), preferred_element_type=jnp.float32)


def dot_nt(a, b):
    return lax.dot_general(a, b, (((1,), (1,)), ((), ())), preferred_element_type=jnp.float32)


def stacked_taps(conv_weight):
    return jnp.concatenate(
        [jnp.concatenate([conv_weight[i, j] for j in range(3)], axis=1) for i in range(3)], axis=0
    )


def conv_rows(image, work, out_rows, width, taps):
    count = out_rows * width
    channels = taps.shape[1] // 3
    stacked = jnp.concatenate([image[i * width : i * width + count, :] for i in range(3)], axis=1)
    work[8 : 8 + count, :] = dot_nn(stacked, taps)
    none = jnp.zeros((1, channels), jnp.float32)
    for i in range(out_rows + 1):
        work[7 + i * width : 8 + i * width, :channels] = none
        work[8 + i * width : 9 + i * width, 2 * channels :] = none
    total = work[8 : 8 + count, channels : 2 * channels]
    total = total + work[7 : 7 + count, :channels]
    total = total + work[9 : 9 + count, 2 * channels :]
    return total.astype(jnp.bfloat16)


def side_keys(slab, odd, between, within, image, work, taps, wkv, kv, kv_t):
    rows, width, channels = slab.shape
    halo = MARGIN + 1
    win = rows + 2 * MARGIN
    above, below = margins_of(odd, between[0:halo], within[0:halo])
    image[0 : halo * width, :] = above.reshape(halo * width, channels)
    image[halo * width : (halo + rows) * width, :] = slab.reshape(rows * width, channels)
    image[(halo + rows) * width :, :] = below.reshape(halo * width, channels)
    hidden = conv_rows(image, work, win, width, taps)
    kv[...] = dot_nn(hidden, wkv).astype(jnp.bfloat16).reshape(win, width, 2 * channels)
    turned = dot_nt(wkv.T, hidden).astype(jnp.bfloat16)
    for r in range(win):
        kv_t[r] = turned[:, r * width : (r + 1) * width]


def places_of(scalars, rows, b, side):
    return [
        (
            scalars[1 + (b * 2 + side) * BAND + s],
            scalars[1 + rows * 2 * BAND + side * BAND + s] == 1,
        )
        for s in range(BAND)
    ]


def side_scores(places, kv, pair_b, width, channels):
    keys = jnp.concatenate([kv[at] for at, _ in places], axis=0)
    both = dot_nt(keys, pair_b)
    expo = jnp.exp2(both[:, :width] * (channels**-0.5 * LOG2E))
    expo = jnp.concatenate(
        [
            jnp.where(live, expo[i * width : (i + 1) * width], 0.0)
            for i, (_, live) in enumerate(places)
        ],
        axis=0,
    )
    return expo, both[:, width:]


def squared(queries_b, cotangent_b, square):
    width, channels = queries_b.shape
    square[...] = jnp.zeros_like(square)
    square[:width, :channels] = queries_b
    square[width:, channels:] = cotangent_b


def first_kernel(
    scalars,
    own,
    slab,
    within,
    between,
    conv_weight,
    q_weight,
    k_weight,
    v_weight,
    cotangent,
    queries,
    kv_t,
    expo,
    grad_probs,
    taps,
    wkv,
    image,
    work,
    kv,
    square,
):
    rows, width, channels = own.shape
    halo = MARGIN + 1
    odd = scalars[0] == 1
    taps[...] = stacked_taps(conv_weight)
    wkv[...] = jnp.concatenate([k_weight[...], v_weight[...]], axis=1)

    above, below = margins_of(odd, between[halo], within[halo])
    image[0:width, :] = above
    image[width : (rows + 1) * width, :] = own[...].reshape(rows * width, channels)
    image[(rows + 1) * width : (rows + 2) * width, :] = below
    hidden = conv_rows(image, work, rows, width, taps[...])
    queries[...] = (
        dot_nn(hidden, q_weight[...]).astype(jnp.bfloat16).reshape(rows, width, channels)
    )

    side_keys(slab[...], odd, between, within, image, work, taps[...], wkv[...], kv, kv_t)
    for b in range(rows):
        squared(queries[b], cotangent[b], square.at[b])
        expo[b], grad_probs[b] = side_scores(
            places_of(scalars, rows, b, 1), kv, square[b], width, channels
        )


def second_kernel(
    scalars,
    queries,
    cotangent,
    slab,
    within,
    between,
    taps,
    wkv,
    first_expo,
    first_grad_probs,
    for_within,
    second_edges,
    first_edges,
    center,
    probs_out,
    grad_scores_out,
    kv_t,
    image,
    work,
    kv,
    square,
    acc,
):
    rows, width, channels = slab.shape
    odd = scalars[0] == 1
    acc[...] = jnp.zeros_like(acc)
    side_keys(slab[...], odd, between, within, image, work, taps[...], wkv[...], kv, kv_t)

    for b in range(rows):
        squared(queries[b], cotangent[b], square.at[b])
        places = [places_of(scalars, rows, b, side) for side in range(2)]
        expo, grad_probs = side_scores(places[0], kv, square[b], width, channels)
        expo = jnp.concatenate([expo, first_expo[b]], axis=0)
        grad_probs = jnp.concatenate([grad_probs, first_grad_probs[b]], axis=0)
        probs = expo * (1.0 / jnp.sum(expo, axis=0, keepdims=True))
        probs_bf = probs.astype(jnp.bfloat16)
        delta = jnp.sum(probs * grad_probs, axis=0, keepdims=True)
        grad_scores = (probs * (grad_probs - delta)).astype(jnp.bfloat16)
        probs_out[b] = probs_bf
        grad_scores_out[b] = grad_scores
        terms = dot_nn(jnp.concatenate([grad_scores, probs_bf], axis=1), square[b])
        for side in range(2):
            for s, (at, _) in enumerate(places[side]):
                i = side * BAND + s
                acc[side, at] += terms[i * width : (i + 1) * width]

    for side, edges in enumerate((second_edges, first_edges)):
        back = back_projected(acc[side], wkv[...])
        top, bottom = back[:MARGIN], back[MARGIN + rows :]
        span = slice(side * MARGIN, (side + 1) * MARGIN)
        for_within[span] = jnp.where(odd, top, bottom).astype(jnp.bfloat16)
        edges[:MARGIN] = top.astype(jnp.bfloat16)
        edges[MARGIN:] = bottom.astype(jnp.bfloat16)
        center[side] = back[MARGIN : MARGIN + rows]


def back_projected(grads, wkv):
    rows, width, both = grads.shape
    channels = both // 2
    grads = jnp.concatenate(
        [grads[:, :, :channels] * channels**-0.5, grads[:, :, channels:]], axis=2
    ).astype(jnp.bfloat16)
    return dot_nt(grads.reshape(rows * width, both), wkv).reshape(rows, width, channels)


def third_kernel(
    scalars,
    probs,
    grad_scores,
    kv_t,
    first_kv_t,
    q_weight,
    attended,
    grad_own,
):
    rows, width, channels = attended.shape
    grad_q = []
    for b in range(rows):
        places = [places_of(scalars, rows, b, side) for side in range(2)]
        keys_t = jnp.concatenate(
            [kv_t[at] for at, _ in places[0]] + [first_kv_t[at] for at, _ in places[1]], axis=1
        )
        attended[b] = dot_nn(keys_t[channels:], probs[b]).T.astype(jnp.bfloat16)
        grad_q.append(dot_nn(keys_t[:channels], grad_scores[b]))
    grad_q = jnp.concatenate(grad_q, axis=1) * channels**-0.5
    turned = dot_nn(q_weight[...], grad_q.astype(jnp.bfloat16))
    for b in range(rows):
        grad_own[b] = turned[:, b * width : (b + 1) * width].T


def on_device(kernel, out_shape, scratch, flops, *arrays):
    smem = pl.BlockSpec(memory_space=pltpu.SMEM)
    vmem = pl.BlockSpec(memory_space=pltpu.VMEM)
    return pl.pallas_call(
        kernel,
        out_shape=tuple(jax.ShapeDtypeStruct(*one) for one in out_shape),
        in_specs=[smem if one.dtype == jnp.int32 else vmem for one in arrays],
        out_specs=tuple(smem if one[1] == jnp.int32 else vmem for one in out_shape),
        scratch_shapes=[pltpu.VMEM(*one) for one in scratch],
        compiler_params=pltpu.CompilerParams(vmem_limit_bytes=14 * 1024 * 1024),
        cost_estimate=pl.CostEstimate(
            flops=flops, bytes_accessed=flops // 1000, transcendentals=0
        ),
    )(*arrays)


def local(
    features_in,
    conv_weight,
    q_weight,
    k_weight,
    v_weight,
    partners,
    band_widths,
    bands,
    grad_attended,
):
    image = features_in[0]
    rows, width, channels = image.shape
    halo = MARGIN + 1
    win = rows + 2 * MARGIN
    half, full = jnp.bfloat16, jnp.float32
    views = lax.axis_size("cam")
    samples = views // min(16, views)
    ring = views // samples
    count = lax.axis_size("row")

    def routed(value, evens, odds):
        pairs = []
        for c in range(views):
            step = odds if (c // samples) % 2 else evens
            pairs.append((c, (c // samples + step) % ring * samples + c % samples))
        return lax.ppermute(value, "cam", pairs)

    camera = lax.axis_index("cam")
    slab = lax.axis_index("row")
    odd_place = (camera if samples == 1 else lax.div(camera, samples)) & 1
    odd_row = (slab & 1) == 1
    even_row = (slab & 1) == 0
    on = (2 - 4 * odd_place) * samples

    def around(place):
        return place & (views - 1) if views & (views - 1) == 0 else lax.rem(place + views, views)

    near_partner = np.arange(views)[:, None] + samples * np.array([[-1, 1]])
    near = (partners == np.mod(near_partner, views).astype(np.int32)).astype(full)
    near = jnp.broadcast_to(near.reshape(2 * views, 1), (2 * views, channels))
    near = lax.optimization_barrier(near)

    def is_near(other, side):
        place = (2 * other + side, jnp.int32(0))
        row = lax.dynamic_slice(near, place, (1, channels), allow_negative_indices=False)
        return row[None] > 0.5

    def across(value, evens, odds):
        pairs = []
        for c in range(views):
            step = odds if (c // samples) % 2 else evens
            to = (c // samples + step) % ring * samples + c % samples
            for r in range(1, count - 1, 2):
                pairs += [(c * count + r, to * count + r + 1), (c * count + r + 1, to * count + r)]
        return lax.ppermute(value, ("cam", "row"), pairs)

    second_near = is_near(around(camera + on), odd_place)
    first_near = is_near(camera, odd_place ^ 1)
    first_near_back = is_near(around(camera - on), odd_place ^ 1)
    pair_slab = routed(image, 1, -1)
    far_slab = routed(image, -2, 2)
    passed_on = jnp.where(second_near, pair_slab, image)
    second_slab = routed(passed_on, 2, -2)
    second_between = across(
        jnp.where(odd_row, passed_on[rows - halo :], passed_on[:halo]), 2, -2
    )
    far_slab, _ = lax.optimization_barrier((far_slab, passed_on))
    first_slab = jnp.where(~first_near, far_slab, pair_slab)
    to_next = jnp.concatenate([first_slab[rows - halo :], image[rows - 1 :]])
    to_previous = jnp.concatenate([first_slab[:halo], image[:1]])
    for_between, for_within = parity_split(to_next, to_previous, odd_row)
    between, within = swap_between(for_between), swap_within(for_within)
    bands, band_widths, even_row, _ = lax.optimization_barrier(
        (bands, band_widths, even_row, for_between)
    )

    widths_here = lax.dynamic_slice(
        band_widths, (camera, 0), (1, 2), allow_negative_indices=False
    )[0]
    live = jnp.arange(BAND, dtype=jnp.int32)[None, :] < widths_here[:, None]
    places = jnp.clip(bands[0] - (slab * rows - MARGIN), 0, win - 1)
    live = jnp.where(odd_place == 1, live[::-1], live)
    places = jnp.where(odd_place == 1, places[:, ::-1], places)
    scalars = jnp.concatenate(
        [
            odd_row.astype(jnp.int32).reshape(1),
            places.reshape(-1),
            live.reshape(-1).astype(jnp.int32),
        ]
    )

    conv_scratch = [
        (((win + 2) * width, channels), half),
        ((win * width + 16, 3 * channels), full),
        ((win, width, 2 * channels), half),
        ((rows, 2 * width, 2 * channels), half),
    ]
    queries, first_kv_t, first_expo, first_grad_probs, taps, wkv = on_device(
        first_kernel,
        [
            (image.shape, half),
            ((win, 2 * channels, width), half),
            ((rows, BAND * width, width), full),
            ((rows, BAND * width, width), full),
            ((3 * channels, 3 * channels), half),
            ((channels, 2 * channels), half),
        ],
        conv_scratch,
        1_000_000,
        scalars,
        image,
        first_slab,
        within,
        between,
        conv_weight,
        q_weight,
        k_weight,
        v_weight,
        grad_attended[0],
    )
    second_within = swap_within(
        jnp.where(odd_row, second_slab[:halo], second_slab[rows - halo :])
    )
    margins = ((2 * MARGIN, width, channels), half)
    weights = ((rows, 2 * BAND * width, width), half)
    for_within, second_edges, first_edges, center, probs, grad_scores, kv_t = on_device(
        second_kernel,
        [
            ((2 * MARGIN, width, channels), half),
            margins,
            margins,
            ((2, rows, width, channels), full),
            weights,
            weights,
            ((win, 2 * channels, width), half),
        ],
        conv_scratch + [((2, win, width, 2 * channels), full)],
        1_500_000_000,
        scalars,
        queries,
        grad_attended[0],
        second_slab,
        second_within,
        second_between,
        taps,
        wkv,
        first_expo,
        first_grad_probs,
    )
    within = swap_within(for_within)

    def spread(part, onto_first):
        part = part.astype(full)
        none = jnp.zeros((rows - 2 * MARGIN, width, channels), full)
        return jnp.concatenate(
            [jnp.where(onto_first, part, 0.0), none, jnp.where(onto_first, 0.0, part)], axis=0
        )

    second = (center[0] + spread(within[:MARGIN], odd_row)).astype(half)
    from_second = routed(second, -2, 2)
    second_edges, first_edges, _ = lax.optimization_barrier((second_edges, first_edges, second))
    second_between = across(
        jnp.where(odd_row, second_edges[MARGIN:], second_edges[:MARGIN]), -2, 2
    )
    first_between = swap_between(
        jnp.where(odd_row, first_edges[MARGIN:], first_edges[:MARGIN])
    )
    attended, grad_own = on_device(
        third_kernel,
        [(image.shape, half), (image.shape, full)],
        [],
        1_000_000,
        scalars,
        probs,
        grad_scores,
        kv_t,
        first_kv_t,
        q_weight,
    )
    from_second, second_between = lax.optimization_barrier((from_second, second_between))
    from_second = from_second.astype(full) + spread(second_between, even_row)
    first_between, _ = lax.optimization_barrier((first_between, from_second))
    first = center[1] + spread(within[MARGIN:], odd_row) + spread(first_between, even_row)
    first = first.astype(half)
    from_first = routed(first, 2, -2)
    for_pair = jnp.where(second_near, from_second, 0.0) + jnp.where(
        first_near, first.astype(full), 0.0
    )
    from_pair = routed(for_pair.astype(half), 1, -1)
    summed = grad_own + from_pair.astype(full)
    summed = summed + jnp.where(second_near, 0.0, from_second)
    summed = summed + jnp.where(first_near_back, 0.0, from_first.astype(full))
    return (attended[None], summed.astype(half)[None])


def solution(mesh):
    placed = (
        P("cam", "row", None, None),
        P(),
        P(),
        P(),
        P(),
        P(),
        P(),
        P("cam", "row", None, None),
        P("cam", "row", None, None),
    )
    return jax.shard_map(
        local,
        mesh=mesh,
        in_specs=placed,
        out_specs=(P("cam", "row", None, None), P("cam", "row", None, None)),
        check_vma=False,
    )
```

```python
import jax
import jax.numpy as jnp
import numpy as np
from jax import lax
from jax.experimental import pallas as pl
from jax.experimental.pallas import tpu as pltpu
from jax.sharding import PartitionSpec as P

MARGIN = 2
BAND = 3
LOG2E = 1.4426950408889634


def swap_within(value):
    pairs = [(i, i + 1) for i in range(0, lax.axis_size("row") - 1, 2)]
    return lax.ppermute(value, "row", pairs + [(j, i) for i, j in pairs])


def swap_between(value):
    pairs = [(i, i + 1) for i in range(1, lax.axis_size("row") - 1, 2)]
    return lax.ppermute(value, "row", pairs + [(j, i) for i, j in pairs])


def parity_split(to_next, to_previous, odd):
    return jnp.where(odd, to_next, to_previous), jnp.where(odd, to_previous, to_next)


def margins_of(odd, between, within):
    return jnp.where(odd, within, between), jnp.where(odd, between, within)


def dot_nn(a, b):
    return lax.dot_general(a, b, (((1,), (0,)), ((), ())), preferred_element_type=jnp.float32)


def dot_nt(a, b):
    return lax.dot_general(a, b, (((1,), (1,)), ((), ())), preferred_element_type=jnp.float32)


def stacked_taps(conv_weight):
    return jnp.concatenate(
        [jnp.concatenate([conv_weight[i, j] for j in range(3)], axis=1) for i in range(3)], axis=0
    )


def conv_rows(image, out_rows, width, taps):
    count = out_rows * width
    channels = taps.shape[1] // 3
    stacked = jnp.concatenate([image[i * width : i * width + count, :] for i in range(3)], axis=1)
    parts = dot_nn(stacked, taps)
    left, middle, right = (parts[:, i * channels : (i + 1) * channels] for i in range(3))
    column = lax.broadcasted_iota(jnp.int32, (count, channels), 0) & (width - 1)
    total = middle + jnp.where(column == 0, 0.0, pltpu.roll(left, 1, 0))
    total = total + jnp.where(column == width - 1, 0.0, pltpu.roll(right, count - 1, 0))
    return total.astype(jnp.bfloat16)


def side_keys(slab, odd, between, within, image, taps, wkv, kv, kv_t):
    rows, width, channels = slab.shape
    halo = MARGIN + 1
    win = rows + 2 * MARGIN
    above, below = margins_of(odd, between[0:halo], within[0:halo])
    image[0 : halo * width, :] = above.reshape(halo * width, channels)
    image[halo * width : (halo + rows) * width, :] = slab.reshape(rows * width, channels)
    image[(halo + rows) * width :, :] = below.reshape(halo * width, channels)
    hidden = conv_rows(image, win, width, taps)
    kv[...] = dot_nn(hidden, wkv).astype(jnp.bfloat16).reshape(win, width, 2 * channels)
    turned = dot_nt(wkv.T, hidden).astype(jnp.bfloat16)
    for r in range(win):
        kv_t[r] = turned[:, r * width : (r + 1) * width]


def places_of(scalars, rows, b, side):
    return [
        (
            scalars[1 + (b * 2 + side) * BAND + s],
            scalars[1 + rows * 2 * BAND + side * BAND + s] == 1,
        )
        for s in range(BAND)
    ]


def side_scores(places, kv, pair_b, width, channels):
    keys = jnp.concatenate([kv[at] for at, _ in places], axis=0)
    both = dot_nt(keys, pair_b)
    expo = jnp.exp2(both[:, :width] * (channels**-0.5 * LOG2E))
    expo = jnp.concatenate(
        [
            jnp.where(live, expo[i * width : (i + 1) * width], 0.0)
            for i, (_, live) in enumerate(places)
        ],
        axis=0,
    )
    return expo, both[:, width:]


def squared(queries_b, cotangent_b, square):
    width, channels = queries_b.shape
    square[...] = jnp.zeros_like(square)
    square[:width, :channels] = queries_b
    square[width:, channels:] = cotangent_b


def first_kernel(
    scalars,
    own,
    slab,
    within,
    between,
    conv_weight,
    q_weight,
    k_weight,
    v_weight,
    cotangent,
    queries,
    kv_t,
    expo,
    grad_probs,
    taps,
    wkv,
    image,
    kv,
    square,
):
    rows, width, channels = own.shape
    halo = MARGIN + 1
    odd = scalars[0] == 1
    taps[...] = stacked_taps(conv_weight)
    wkv[...] = jnp.concatenate([k_weight[...], v_weight[...]], axis=1)

    above, below = margins_of(odd, between[halo], within[halo])
    image[0:width, :] = above
    image[width : (rows + 1) * width, :] = own[...].reshape(rows * width, channels)
    image[(rows + 1) * width : (rows + 2) * width, :] = below
    hidden = conv_rows(image, rows, width, taps[...])
    queries[...] = (
        dot_nn(hidden, q_weight[...]).astype(jnp.bfloat16).reshape(rows, width, channels)
    )

    side_keys(slab[...], odd, between, within, image, taps[...], wkv[...], kv, kv_t)
    for b in range(rows):
        squared(queries[b], cotangent[b], square.at[b])
        expo[b], grad_probs[b] = side_scores(
            places_of(scalars, rows, b, 1), kv, square[b], width, channels
        )


def second_kernel(
    scalars,
    queries,
    cotangent,
    slab,
    within,
    between,
    taps,
    wkv,
    first_expo,
    first_grad_probs,
    for_within,
    second_edges,
    first_edges,
    center,
    probs_out,
    grad_scores_out,
    kv_t,
    image,
    kv,
    square,
    acc,
):
    rows, width, channels = slab.shape
    odd = scalars[0] == 1
    acc[...] = jnp.zeros_like(acc)
    side_keys(slab[...], odd, between, within, image, taps[...], wkv[...], kv, kv_t)

    for b in range(rows):
        squared(queries[b], cotangent[b], square.at[b])
        places = [places_of(scalars, rows, b, side) for side in range(2)]
        expo, grad_probs = side_scores(places[0], kv, square[b], width, channels)
        expo = jnp.concatenate([expo, first_expo[b]], axis=0)
        grad_probs = jnp.concatenate([grad_probs, first_grad_probs[b]], axis=0)
        probs = expo * (1.0 / jnp.sum(expo, axis=0, keepdims=True))
        probs_bf = probs.astype(jnp.bfloat16)
        delta = jnp.sum(probs * grad_probs, axis=0, keepdims=True)
        grad_scores = (probs * (grad_probs - delta)).astype(jnp.bfloat16)
        probs_out[b] = probs_bf
        grad_scores_out[b] = grad_scores
        terms = dot_nn(jnp.concatenate([grad_scores, probs_bf], axis=1), square[b])
        for side in range(2):
            for s, (at, _) in enumerate(places[side]):
                i = side * BAND + s
                acc[side, at] += terms[i * width : (i + 1) * width]

    for side, edges in enumerate((second_edges, first_edges)):
        back = back_projected(acc[side], wkv[...])
        top, bottom = back[:MARGIN], back[MARGIN + rows :]
        span = slice(side * MARGIN, (side + 1) * MARGIN)
        for_within[span] = jnp.where(odd, top, bottom).astype(jnp.bfloat16)
        edges[:MARGIN] = top.astype(jnp.bfloat16)
        edges[MARGIN:] = bottom.astype(jnp.bfloat16)
        center[side] = back[MARGIN : MARGIN + rows]


def back_projected(grads, wkv):
    rows, width, both = grads.shape
    channels = both // 2
    grads = jnp.concatenate(
        [grads[:, :, :channels] * channels**-0.5, grads[:, :, channels:]], axis=2
    ).astype(jnp.bfloat16)
    return dot_nt(grads.reshape(rows * width, both), wkv).reshape(rows, width, channels)


def third_kernel(
    scalars,
    probs,
    grad_scores,
    kv_t,
    first_kv_t,
    q_weight,
    attended,
    grad_own,
):
    rows, width, channels = attended.shape
    grad_q = []
    for b in range(rows):
        places = [places_of(scalars, rows, b, side) for side in range(2)]
        keys_t = jnp.concatenate(
            [kv_t[at] for at, _ in places[0]] + [first_kv_t[at] for at, _ in places[1]], axis=1
        )
        attended[b] = dot_nn(keys_t[channels:], probs[b]).T.astype(jnp.bfloat16)
        grad_q.append(dot_nn(keys_t[:channels], grad_scores[b]))
    grad_q = jnp.concatenate(grad_q, axis=1) * channels**-0.5
    turned = dot_nn(q_weight[...], grad_q.astype(jnp.bfloat16))
    for b in range(rows):
        grad_own[b] = turned[:, b * width : (b + 1) * width].T


def on_device(kernel, out_shape, scratch, flops, *arrays):
    smem = pl.BlockSpec(memory_space=pltpu.SMEM)
    vmem = pl.BlockSpec(memory_space=pltpu.VMEM)
    return pl.pallas_call(
        kernel,
        out_shape=tuple(jax.ShapeDtypeStruct(*one) for one in out_shape),
        in_specs=[smem if one.dtype == jnp.int32 else vmem for one in arrays],
        out_specs=tuple(smem if one[1] == jnp.int32 else vmem for one in out_shape),
        scratch_shapes=[pltpu.VMEM(*one) for one in scratch],
        compiler_params=pltpu.CompilerParams(vmem_limit_bytes=14 * 1024 * 1024),
        cost_estimate=pl.CostEstimate(
            flops=flops, bytes_accessed=flops // 1000, transcendentals=0
        ),
    )(*arrays)


def local(
    features_in,
    conv_weight,
    q_weight,
    k_weight,
    v_weight,
    partners,
    band_widths,
    bands,
    grad_attended,
):
    image = features_in[0]
    rows, width, channels = image.shape
    halo = MARGIN + 1
    win = rows + 2 * MARGIN
    half, full = jnp.bfloat16, jnp.float32
    views = lax.axis_size("cam")
    samples = views // min(16, views)
    ring = views // samples
    count = lax.axis_size("row")

    def routed(value, evens, odds):
        pairs = []
        for c in range(views):
            step = odds if (c // samples) % 2 else evens
            pairs.append((c, (c // samples + step) % ring * samples + c % samples))
        return lax.ppermute(value, "cam", pairs)

    camera = lax.axis_index("cam")
    slab = lax.axis_index("row")
    odd_place = (camera if samples == 1 else lax.div(camera, samples)) & 1
    odd_row = (slab & 1) == 1
    even_row = (slab & 1) == 0
    on = (2 - 4 * odd_place) * samples

    def around(place):
        return place & (views - 1) if views & (views - 1) == 0 else lax.rem(place + views, views)

    near_partner = np.arange(views)[:, None] + samples * np.array([[-1, 1]])
    near = (partners == np.mod(near_partner, views).astype(np.int32)).astype(full)
    near = jnp.broadcast_to(near.reshape(2 * views, 1), (2 * views, channels))
    near = lax.optimization_barrier(near)

    def is_near(other, side):
        place = (2 * other + side, jnp.int32(0))
        row = lax.dynamic_slice(near, place, (1, channels), allow_negative_indices=False)
        return row[None] > 0.5

    def across(value, evens, odds):
        pairs = []
        for c in range(views):
            step = odds if (c // samples) % 2 else evens
            to = (c // samples + step) % ring * samples + c % samples
            for r in range(1, count - 1, 2):
                pairs += [(c * count + r, to * count + r + 1), (c * count + r + 1, to * count + r)]
        return lax.ppermute(value, ("cam", "row"), pairs)

    second_near = is_near(around(camera + on), odd_place)
    first_near = is_near(camera, odd_place ^ 1)
    first_near_back = is_near(around(camera - on), odd_place ^ 1)
    pair_slab = routed(image, 1, -1)
    far_slab = routed(image, -2, 2)
    passed_on = jnp.where(second_near, pair_slab, image)
    second_slab = routed(passed_on, 2, -2)
    second_between = across(
        jnp.where(odd_row, passed_on[rows - halo :], passed_on[:halo]), 2, -2
    )
    far_slab, _ = lax.optimization_barrier((far_slab, passed_on))
    first_slab = jnp.where(~first_near, far_slab, pair_slab)
    to_next = jnp.concatenate([first_slab[rows - halo :], image[rows - 1 :]])
    to_previous = jnp.concatenate([first_slab[:halo], image[:1]])
    for_between, for_within = parity_split(to_next, to_previous, odd_row)
    between, within = swap_between(for_between), swap_within(for_within)
    bands, band_widths, even_row, _ = lax.optimization_barrier(
        (bands, band_widths, even_row, for_between)
    )

    widths_here = lax.dynamic_slice(
        band_widths, (camera, 0), (1, 2), allow_negative_indices=False
    )[0]
    live = jnp.arange(BAND, dtype=jnp.int32)[None, :] < widths_here[:, None]
    places = jnp.clip(bands[0] - (slab * rows - MARGIN), 0, win - 1)
    live = jnp.where(odd_place == 1, live[::-1], live)
    places = jnp.where(odd_place == 1, places[:, ::-1], places)
    scalars = jnp.concatenate(
        [
            odd_row.astype(jnp.int32).reshape(1),
            places.reshape(-1),
            live.reshape(-1).astype(jnp.int32),
        ]
    )

    conv_scratch = [
        (((win + 2) * width, channels), half),
        ((win, width, 2 * channels), half),
        ((rows, 2 * width, 2 * channels), half),
    ]
    queries, first_kv_t, first_expo, first_grad_probs, taps, wkv = on_device(
        first_kernel,
        [
            (image.shape, half),
            ((win, 2 * channels, width), half),
            ((rows, BAND * width, width), full),
            ((rows, BAND * width, width), full),
            ((3 * channels, 3 * channels), half),
            ((channels, 2 * channels), half),
        ],
        conv_scratch,
        1_000_000,
        scalars,
        image,
        first_slab,
        within,
        between,
        conv_weight,
        q_weight,
        k_weight,
        v_weight,
        grad_attended[0],
    )
    second_within = swap_within(
        jnp.where(odd_row, second_slab[:halo], second_slab[rows - halo :])
    )
    margins = ((2 * MARGIN, width, channels), half)
    weights = ((rows, 2 * BAND * width, width), half)
    for_within, second_edges, first_edges, center, probs, grad_scores, kv_t = on_device(
        second_kernel,
        [
            ((2 * MARGIN, width, channels), half),
            margins,
            margins,
            ((2, rows, width, channels), full),
            weights,
            weights,
            ((win, 2 * channels, width), half),
        ],
        conv_scratch + [((2, win, width, 2 * channels), full)],
        1_500_000_000,
        scalars,
        queries,
        grad_attended[0],
        second_slab,
        second_within,
        second_between,
        taps,
        wkv,
        first_expo,
        first_grad_probs,
    )
    within = swap_within(for_within)

    def spread(part, onto_first):
        part = part.astype(full)
        none = jnp.zeros((rows - 2 * MARGIN, width, channels), full)
        return jnp.concatenate(
            [jnp.where(onto_first, part, 0.0), none, jnp.where(onto_first, 0.0, part)], axis=0
        )

    second = (center[0] + spread(within[:MARGIN], odd_row)).astype(half)
    from_second = routed(second, -2, 2)
    second_edges, first_edges, _ = lax.optimization_barrier((second_edges, first_edges, second))
    second_between = across(
        jnp.where(odd_row, second_edges[MARGIN:], second_edges[:MARGIN]), -2, 2
    )
    first_between = swap_between(
        jnp.where(odd_row, first_edges[MARGIN:], first_edges[:MARGIN])
    )
    attended, grad_own = on_device(
        third_kernel,
        [(image.shape, half), (image.shape, full)],
        [],
        1_000_000,
        scalars,
        probs,
        grad_scores,
        kv_t,
        first_kv_t,
        q_weight,
    )
    first = center[1] + spread(within[MARGIN:], odd_row) + spread(first_between, even_row)
    first = first.astype(half)
    from_first = routed(first, 2, -2)
    from_second, second_between, _ = lax.optimization_barrier(
        (from_second, second_between, first)
    )
    from_second = from_second.astype(full) + spread(second_between, even_row)
    for_pair = jnp.where(first_near, first.astype(full), 0.0) + jnp.where(
        second_near, from_second, 0.0
    )
    from_pair = routed(for_pair.astype(half), 1, -1)
    summed = grad_own + from_pair.astype(full)
    summed = summed + jnp.where(second_near, 0.0, from_second)
    summed = summed + jnp.where(first_near_back, 0.0, from_first.astype(full))
    return (attended[None], summed.astype(half)[None])


def solution(mesh):
    placed = (
        P("cam", "row", None, None),
        P(),
        P(),
        P(),
        P(),
        P(),
        P(),
        P("cam", "row", None, None),
        P("cam", "row", None, None),
    )
    return jax.shard_map(
        local,
        mesh=mesh,
        in_specs=placed,
        out_specs=(P("cam", "row", None, None), P("cam", "row", None, None)),
        check_vma=False,
    )
```

```python
import jax
import jax.numpy as jnp
from jax import lax
from jax.experimental import pallas as pl
from jax.experimental.pallas import tpu as pltpu
from jax.sharding import PartitionSpec as P

MARGIN = 2
BAND = 3
LOG2E = 1.4426950408889634


def swap_within(value):
    pairs = [(i, i + 1) for i in range(0, lax.axis_size("row") - 1, 2)]
    return lax.ppermute(value, "row", pairs + [(j, i) for i, j in pairs])


def swap_between(value):
    pairs = [(i, i + 1) for i in range(1, lax.axis_size("row") - 1, 2)]
    return lax.ppermute(value, "row", pairs + [(j, i) for i, j in pairs])


def parity_split(to_next, to_previous, odd):
    return jnp.where(odd, to_next, to_previous), jnp.where(odd, to_previous, to_next)


def margins_of(odd, between, within):
    return jnp.where(odd, within, between), jnp.where(odd, between, within)


def dot_nn(a, b):
    return lax.dot_general(a, b, (((1,), (0,)), ((), ())), preferred_element_type=jnp.float32)


def dot_nt(a, b):
    return lax.dot_general(a, b, (((1,), (1,)), ((), ())), preferred_element_type=jnp.float32)


def stacked_taps(conv_weight):
    return jnp.concatenate(
        [jnp.concatenate([conv_weight[i, j] for j in range(3)], axis=1) for i in range(3)], axis=0
    )


def conv_rows(image, work, out_rows, width, taps):
    count = out_rows * width
    channels = taps.shape[1] // 3
    stacked = jnp.concatenate([image[i * width : i * width + count, :] for i in range(3)], axis=1)
    work[8 : 8 + count, :] = dot_nn(stacked, taps)
    none = jnp.zeros((1, channels), jnp.float32)
    for i in range(out_rows + 1):
        work[7 + i * width : 8 + i * width, :channels] = none
        work[8 + i * width : 9 + i * width, 2 * channels :] = none
    total = work[8 : 8 + count, channels : 2 * channels]
    total = total + work[7 : 7 + count, :channels]
    total = total + work[9 : 9 + count, 2 * channels :]
    return total.astype(jnp.bfloat16)


def side_keys(slab, odd, between, within, image, work, taps, wkv, kv, kv_t):
    rows, width, channels = slab.shape
    halo = MARGIN + 1
    win = rows + 2 * MARGIN
    above, below = margins_of(odd, between[0:halo], within[0:halo])
    image[0 : halo * width, :] = above.reshape(halo * width, channels)
    image[halo * width : (halo + rows) * width, :] = slab.reshape(rows * width, channels)
    image[(halo + rows) * width :, :] = below.reshape(halo * width, channels)
    hidden = conv_rows(image, work, win, width, taps)
    kv[...] = dot_nn(hidden, wkv).astype(jnp.bfloat16).reshape(win, width, 2 * channels)
    turned = dot_nt(wkv.T, hidden).astype(jnp.bfloat16)
    for r in range(win):
        kv_t[r] = turned[:, r * width : (r + 1) * width]


def places_of(scalars, rows, b, side):
    return [
        (
            scalars[1 + (b * 2 + side) * BAND + s],
            scalars[1 + rows * 2 * BAND + side * BAND + s] == 1,
        )
        for s in range(BAND)
    ]


def side_scores(places, kv, pair_b, width, channels):
    keys = jnp.concatenate([kv[at] for at, _ in places], axis=0)
    both = dot_nt(keys, pair_b)
    expo = jnp.exp2(both[:, :width] * (channels**-0.5 * LOG2E))
    expo = jnp.concatenate(
        [
            jnp.where(live, expo[i * width : (i + 1) * width], 0.0)
            for i, (_, live) in enumerate(places)
        ],
        axis=0,
    )
    return expo, both[:, width:]


def squared(queries_b, cotangent_b, square):
    width, channels = queries_b.shape
    square[...] = jnp.zeros_like(square)
    square[:width, :channels] = queries_b
    square[width:, channels:] = cotangent_b


def first_kernel(
    scalars,
    own,
    slab,
    within,
    between,
    conv_weight,
    q_weight,
    k_weight,
    v_weight,
    cotangent,
    queries,
    kv_t,
    expo,
    grad_probs,
    taps,
    wkv,
    image,
    work,
    kv,
    square,
):
    rows, width, channels = own.shape
    halo = MARGIN + 1
    odd = scalars[0] == 1
    taps[...] = stacked_taps(conv_weight)
    wkv[...] = jnp.concatenate([k_weight[...], v_weight[...]], axis=1)

    above, below = margins_of(odd, between[halo], within[halo])
    image[0:width, :] = above
    image[width : (rows + 1) * width, :] = own[...].reshape(rows * width, channels)
    image[(rows + 1) * width : (rows + 2) * width, :] = below
    hidden = conv_rows(image, work, rows, width, taps[...])
    queries[...] = (
        dot_nn(hidden, q_weight[...]).astype(jnp.bfloat16).reshape(rows, width, channels)
    )

    side_keys(slab[...], odd, between, within, image, work, taps[...], wkv[...], kv, kv_t)
    for b in range(rows):
        squared(queries[b], cotangent[b], square.at[b])
        expo[b], grad_probs[b] = side_scores(
            places_of(scalars, rows, b, 1), kv, square[b], width, channels
        )


def second_kernel(
    scalars,
    queries,
    cotangent,
    slab,
    within,
    between,
    taps,
    wkv,
    first_expo,
    first_grad_probs,
    for_within,
    second_edges,
    first_edges,
    center,
    probs_out,
    grad_scores_out,
    kv_t,
    image,
    work,
    kv,
    square,
    acc,
):
    rows, width, channels = slab.shape
    odd = scalars[0] == 1
    acc[...] = jnp.zeros_like(acc)
    side_keys(slab[...], odd, between, within, image, work, taps[...], wkv[...], kv, kv_t)

    for b in range(rows):
        squared(queries[b], cotangent[b], square.at[b])
        places = [places_of(scalars, rows, b, side) for side in range(2)]
        expo, grad_probs = side_scores(places[0], kv, square[b], width, channels)
        expo = jnp.concatenate([expo, first_expo[b]], axis=0)
        grad_probs = jnp.concatenate([grad_probs, first_grad_probs[b]], axis=0)
        probs = expo * (1.0 / jnp.sum(expo, axis=0, keepdims=True))
        probs_bf = probs.astype(jnp.bfloat16)
        delta = jnp.sum(probs * grad_probs, axis=0, keepdims=True)
        grad_scores = (probs * (grad_probs - delta)).astype(jnp.bfloat16)
        probs_out[b] = probs_bf
        grad_scores_out[b] = grad_scores
        terms = dot_nn(jnp.concatenate([grad_scores, probs_bf], axis=1), square[b])
        for side in range(2):
            for s, (at, _) in enumerate(places[side]):
                i = side * BAND + s
                acc[side, at] += terms[i * width : (i + 1) * width]

    for side, edges in enumerate((second_edges, first_edges)):
        back = back_projected(acc[side], wkv[...])
        top, bottom = back[:MARGIN], back[MARGIN + rows :]
        span = slice(side * MARGIN, (side + 1) * MARGIN)
        for_within[span] = jnp.where(odd, top, bottom).astype(jnp.bfloat16)
        edges[:MARGIN] = top.astype(jnp.bfloat16)
        edges[MARGIN:] = bottom.astype(jnp.bfloat16)
        center[side] = back[MARGIN : MARGIN + rows]


def back_projected(grads, wkv):
    rows, width, both = grads.shape
    channels = both // 2
    grads = jnp.concatenate(
        [grads[:, :, :channels] * channels**-0.5, grads[:, :, channels:]], axis=2
    ).astype(jnp.bfloat16)
    return dot_nt(grads.reshape(rows * width, both), wkv).reshape(rows, width, channels)


def third_kernel(
    scalars,
    probs,
    grad_scores,
    kv_t,
    first_kv_t,
    q_weight,
    attended,
    grad_own,
):
    rows, width, channels = attended.shape
    grad_q = []
    for b in range(rows):
        places = [places_of(scalars, rows, b, side) for side in range(2)]
        keys_t = jnp.concatenate(
            [kv_t[at] for at, _ in places[0]] + [first_kv_t[at] for at, _ in places[1]], axis=1
        )
        attended[b] = dot_nn(keys_t[channels:], probs[b]).T.astype(jnp.bfloat16)
        grad_q.append(dot_nn(keys_t[:channels], grad_scores[b]))
    grad_q = jnp.concatenate(grad_q, axis=1) * channels**-0.5
    turned = dot_nn(q_weight[...], grad_q.astype(jnp.bfloat16))
    for b in range(rows):
        grad_own[b] = turned[:, b * width : (b + 1) * width].T


def on_device(kernel, out_shape, scratch, flops, *arrays):
    smem = pl.BlockSpec(memory_space=pltpu.SMEM)
    vmem = pl.BlockSpec(memory_space=pltpu.VMEM)
    return pl.pallas_call(
        kernel,
        out_shape=tuple(jax.ShapeDtypeStruct(*one) for one in out_shape),
        in_specs=[smem if one.dtype == jnp.int32 else vmem for one in arrays],
        out_specs=tuple(smem if one[1] == jnp.int32 else vmem for one in out_shape),
        scratch_shapes=[pltpu.VMEM(*one) for one in scratch],
        compiler_params=pltpu.CompilerParams(vmem_limit_bytes=14 * 1024 * 1024),
        cost_estimate=pl.CostEstimate(
            flops=flops, bytes_accessed=flops // 1000, transcendentals=0
        ),
    )(*arrays)


def local(
    features_in,
    conv_weight,
    q_weight,
    k_weight,
    v_weight,
    partners,
    band_widths,
    bands,
    grad_attended,
):
    image = features_in[0]
    rows, width, channels = image.shape
    halo = MARGIN + 1
    win = rows + 2 * MARGIN
    half, full = jnp.bfloat16, jnp.float32
    views = lax.axis_size("cam")
    samples = views // min(16, views)
    ring = views // samples
    count = lax.axis_size("row")

    def routed(value, evens, odds):
        pairs = []
        for c in range(views):
            step = odds if (c // samples) % 2 else evens
            pairs.append((c, (c // samples + step) % ring * samples + c % samples))
        return lax.ppermute(value, "cam", pairs)

    camera = lax.axis_index("cam")
    slab = lax.axis_index("row")
    odd_place = (camera if samples == 1 else lax.div(camera, samples)) & 1
    odd_row = (slab & 1) == 1
    even_row = (slab & 1) == 0
    on = (2 - 4 * odd_place) * samples

    def around(place):
        return place & (views - 1) if views & (views - 1) == 0 else lax.rem(place + views, views)

    place, side = (lax.broadcasted_iota(jnp.int32, (views, 2), dim) for dim in range(2))
    near = (partners == around(place + (2 * side - 1) * samples)).astype(full)
    near = jnp.broadcast_to(near.reshape(2 * views, 1), (2 * views, channels))
    near = lax.optimization_barrier(near)

    def is_near(other, side):
        place = (2 * other + side, jnp.int32(0))
        row = lax.dynamic_slice(near, place, (1, channels), allow_negative_indices=False)
        return row[None] > 0.5

    def across(value, evens, odds):
        pairs = []
        for c in range(views):
            step = odds if (c // samples) % 2 else evens
            to = (c // samples + step) % ring * samples + c % samples
            for r in range(1, count - 1, 2):
                pairs += [(c * count + r, to * count + r + 1), (c * count + r + 1, to * count + r)]
        return lax.ppermute(value, ("cam", "row"), pairs)

    second_near = is_near(around(camera + on), odd_place)
    first_near = is_near(camera, odd_place ^ 1)
    first_near_back = is_near(around(camera - on), odd_place ^ 1)
    pair_slab = routed(image, 1, -1)
    far_slab = routed(image, -2, 2)
    passed_on = jnp.where(second_near, pair_slab, image)
    second_slab = routed(passed_on, 2, -2)
    second_between = across(
        jnp.where(odd_row, passed_on[rows - halo :], passed_on[:halo]), 2, -2
    )
    far_slab, _ = lax.optimization_barrier((far_slab, passed_on))
    first_slab = jnp.where(~first_near, far_slab, pair_slab)
    to_next = jnp.concatenate([first_slab[rows - halo :], image[rows - 1 :]])
    to_previous = jnp.concatenate([first_slab[:halo], image[:1]])
    for_between, for_within = parity_split(to_next, to_previous, odd_row)
    between, within = swap_between(for_between), swap_within(for_within)
    bands, band_widths, even_row, _ = lax.optimization_barrier(
        (bands, band_widths, even_row, for_between)
    )

    widths_here = lax.dynamic_slice(
        band_widths, (camera, 0), (1, 2), allow_negative_indices=False
    )[0]
    live = jnp.arange(BAND, dtype=jnp.int32)[None, :] < widths_here[:, None]
    places = jnp.clip(bands[0] - (slab * rows - MARGIN), 0, win - 1)
    live = jnp.where(odd_place == 1, live[::-1], live)
    places = jnp.where(odd_place == 1, places[:, ::-1], places)
    scalars = jnp.concatenate(
        [
            odd_row.astype(jnp.int32).reshape(1),
            places.reshape(-1),
            live.reshape(-1).astype(jnp.int32),
        ]
    )

    conv_scratch = [
        (((win + 2) * width, channels), half),
        ((win * width + 16, 3 * channels), full),
        ((win, width, 2 * channels), half),
        ((rows, 2 * width, 2 * channels), half),
    ]
    queries, first_kv_t, first_expo, first_grad_probs, taps, wkv = on_device(
        first_kernel,
        [
            (image.shape, half),
            ((win, 2 * channels, width), half),
            ((rows, BAND * width, width), full),
            ((rows, BAND * width, width), full),
            ((3 * channels, 3 * channels), half),
            ((channels, 2 * channels), half),
        ],
        conv_scratch,
        1_000_000,
        scalars,
        image,
        first_slab,
        within,
        between,
        conv_weight,
        q_weight,
        k_weight,
        v_weight,
        grad_attended[0],
    )
    second_within = swap_within(
        jnp.where(odd_row, second_slab[:halo], second_slab[rows - halo :])
    )
    margins = ((2 * MARGIN, width, channels), half)
    weights = ((rows, 2 * BAND * width, width), half)
    for_within, second_edges, first_edges, center, probs, grad_scores, kv_t = on_device(
        second_kernel,
        [
            ((2 * MARGIN, width, channels), half),
            margins,
            margins,
            ((2, rows, width, channels), full),
            weights,
            weights,
            ((win, 2 * channels, width), half),
        ],
        conv_scratch + [((2, win, width, 2 * channels), full)],
        1_500_000_000,
        scalars,
        queries,
        grad_attended[0],
        second_slab,
        second_within,
        second_between,
        taps,
        wkv,
        first_expo,
        first_grad_probs,
    )
    within = swap_within(for_within)

    def spread(part, onto_first):
        part = part.astype(full)
        none = jnp.zeros((rows - 2 * MARGIN, width, channels), full)
        return jnp.concatenate(
            [jnp.where(onto_first, part, 0.0), none, jnp.where(onto_first, 0.0, part)], axis=0
        )

    second = (center[0] + spread(within[:MARGIN], odd_row)).astype(half)
    from_second = routed(second, -2, 2)
    second_edges, first_edges, _ = lax.optimization_barrier((second_edges, first_edges, second))
    second_between = across(
        jnp.where(odd_row, second_edges[MARGIN:], second_edges[:MARGIN]), -2, 2
    )
    first_between = swap_between(
        jnp.where(odd_row, first_edges[MARGIN:], first_edges[:MARGIN])
    )
    attended, grad_own = on_device(
        third_kernel,
        [(image.shape, half), (image.shape, full)],
        [],
        1_000_000,
        scalars,
        probs,
        grad_scores,
        kv_t,
        first_kv_t,
        q_weight,
    )
    first = center[1] + spread(within[MARGIN:], odd_row) + spread(first_between, even_row)
    first = first.astype(half)
    from_first = routed(first, 2, -2)
    from_second, second_between, _ = lax.optimization_barrier(
        (from_second, second_between, first)
    )
    from_second = from_second.astype(full) + spread(second_between, even_row)
    for_pair = jnp.where(first_near, first.astype(full), 0.0) + jnp.where(
        second_near, from_second, 0.0
    )
    from_pair = routed(for_pair.astype(half), 1, -1)
    summed = grad_own + from_pair.astype(full)
    summed = summed + jnp.where(second_near, 0.0, from_second)
    summed = summed + jnp.where(first_near_back, 0.0, from_first.astype(full))
    return (attended[None], summed.astype(half)[None])


def solution(mesh):
    placed = (
        P("cam", "row", None, None),
        P(),
        P(),
        P(),
        P(),
        P(),
        P(),
        P("cam", "row", None, None),
        P("cam", "row", None, None),
    )
    return jax.shard_map(
        local,
        mesh=mesh,
        in_specs=placed,
        out_specs=(P("cam", "row", None, None), P("cam", "row", None, None)),
        check_vma=False,
    )
```

```python
import jax
import jax.numpy as jnp
from jax import lax
from jax.experimental import pallas as pl
from jax.experimental.pallas import tpu as pltpu
from jax.sharding import PartitionSpec as P

MARGIN = 2
BAND = 3
LOG2E = 1.4426950408889634


def swap_within(value):
    pairs = [(i, i + 1) for i in range(0, lax.axis_size("row") - 1, 2)]
    return lax.ppermute(value, "row", pairs + [(j, i) for i, j in pairs])


def swap_between(value):
    pairs = [(i, i + 1) for i in range(1, lax.axis_size("row") - 1, 2)]
    return lax.ppermute(value, "row", pairs + [(j, i) for i, j in pairs])


def parity_split(to_next, to_previous, odd):
    return jnp.where(odd, to_next, to_previous), jnp.where(odd, to_previous, to_next)


def margins_of(odd, between, within):
    return jnp.where(odd, within, between), jnp.where(odd, between, within)


def dot_nn(a, b):
    return lax.dot_general(a, b, (((1,), (0,)), ((), ())), preferred_element_type=jnp.float32)


def dot_nt(a, b):
    return lax.dot_general(a, b, (((1,), (1,)), ((), ())), preferred_element_type=jnp.float32)


def stacked_taps(conv_weight):
    return jnp.concatenate(
        [jnp.concatenate([conv_weight[i, j] for j in range(3)], axis=1) for i in range(3)], axis=0
    )


def conv_rows(image, work, out_rows, width, taps):
    count = out_rows * width
    channels = taps.shape[1] // 3
    stacked = jnp.concatenate([image[i * width : i * width + count, :] for i in range(3)], axis=1)
    work[8 : 8 + count, :] = dot_nn(stacked, taps)
    none = jnp.zeros((1, channels), jnp.float32)
    for i in range(out_rows + 1):
        work[7 + i * width : 8 + i * width, :channels] = none
        work[8 + i * width : 9 + i * width, 2 * channels :] = none
    total = work[8 : 8 + count, channels : 2 * channels]
    total = total + work[7 : 7 + count, :channels]
    total = total + work[9 : 9 + count, 2 * channels :]
    return total.astype(jnp.bfloat16)


def side_keys(slab, odd, between, within, image, work, taps, wkv, kv, kv_t):
    rows, width, channels = slab.shape
    halo = MARGIN + 1
    win = rows + 2 * MARGIN
    above, below = margins_of(odd, between[0:halo], within[0:halo])
    image[0 : halo * width, :] = above.reshape(halo * width, channels)
    image[halo * width : (halo + rows) * width, :] = slab.reshape(rows * width, channels)
    image[(halo + rows) * width :, :] = below.reshape(halo * width, channels)
    hidden = conv_rows(image, work, win, width, taps)
    kv[...] = dot_nn(hidden, wkv).astype(jnp.bfloat16).reshape(win, width, 2 * channels)
    turned = dot_nt(wkv.T, hidden).astype(jnp.bfloat16)
    for r in range(win):
        kv_t[r] = turned[:, r * width : (r + 1) * width]


def places_of(scalars, rows, b, side):
    return [
        (
            scalars[1 + (b * 2 + side) * BAND + s],
            scalars[1 + rows * 2 * BAND + side * BAND + s] == 1,
        )
        for s in range(BAND)
    ]


def side_scores(places, kv, pair_b, width, channels):
    keys = jnp.concatenate([kv[at] for at, _ in places], axis=0)
    both = dot_nt(keys, pair_b)
    expo = jnp.exp2(both[:, :width] * (channels**-0.5 * LOG2E))
    expo = jnp.concatenate(
        [
            jnp.where(live, expo[i * width : (i + 1) * width], 0.0)
            for i, (_, live) in enumerate(places)
        ],
        axis=0,
    )
    return expo, both[:, width:]


def squared(queries_b, cotangent_b, square):
    width, channels = queries_b.shape
    square[...] = jnp.zeros_like(square)
    square[:width, :channels] = queries_b
    square[width:, channels:] = cotangent_b


def first_kernel(
    scalars,
    own,
    slab,
    within,
    between,
    conv_weight,
    q_weight,
    k_weight,
    v_weight,
    cotangent,
    queries,
    kv_t,
    expo,
    grad_probs,
    taps,
    wkv,
    image,
    work,
    kv,
    square,
):
    rows, width, channels = own.shape
    halo = MARGIN + 1
    odd = scalars[0] == 1
    taps[...] = stacked_taps(conv_weight)
    wkv[...] = jnp.concatenate([k_weight[...], v_weight[...]], axis=1)

    above, below = margins_of(odd, between[halo], within[halo])
    image[0:width, :] = above
    image[width : (rows + 1) * width, :] = own[...].reshape(rows * width, channels)
    image[(rows + 1) * width : (rows + 2) * width, :] = below
    hidden = conv_rows(image, work, rows, width, taps[...])
    queries[...] = (
        dot_nn(hidden, q_weight[...]).astype(jnp.bfloat16).reshape(rows, width, channels)
    )

    side_keys(slab[...], odd, between, within, image, work, taps[...], wkv[...], kv, kv_t)
    for b in range(rows):
        squared(queries[b], cotangent[b], square.at[b])
        expo[b], grad_probs[b] = side_scores(
            places_of(scalars, rows, b, 1), kv, square[b], width, channels
        )


def second_kernel(
    scalars,
    queries,
    cotangent,
    slab,
    within,
    between,
    taps,
    wkv,
    first_expo,
    first_grad_probs,
    for_within,
    second_edges,
    first_edges,
    center,
    probs_out,
    grad_scores_out,
    kv_t,
    image,
    work,
    kv,
    square,
    acc,
):
    rows, width, channels = slab.shape
    odd = scalars[0] == 1
    acc[...] = jnp.zeros_like(acc)
    side_keys(slab[...], odd, between, within, image, work, taps[...], wkv[...], kv, kv_t)

    for b in range(rows):
        squared(queries[b], cotangent[b], square.at[b])
        places = [places_of(scalars, rows, b, side) for side in range(2)]
        expo, grad_probs = side_scores(places[0], kv, square[b], width, channels)
        expo = jnp.concatenate([expo, first_expo[b]], axis=0)
        grad_probs = jnp.concatenate([grad_probs, first_grad_probs[b]], axis=0)
        probs = expo * (1.0 / jnp.sum(expo, axis=0, keepdims=True))
        probs_bf = probs.astype(jnp.bfloat16)
        delta = jnp.sum(probs * grad_probs, axis=0, keepdims=True)
        grad_scores = (probs * (grad_probs - delta)).astype(jnp.bfloat16)
        probs_out[b] = probs_bf
        grad_scores_out[b] = grad_scores
        terms = dot_nn(jnp.concatenate([grad_scores, probs_bf], axis=1), square[b])
        for side in range(2):
            for s, (at, _) in enumerate(places[side]):
                i = side * BAND + s
                acc[side, at] += terms[i * width : (i + 1) * width]

    for side, edges in enumerate((second_edges, first_edges)):
        back = back_projected(acc[side], wkv[...])
        top, bottom = back[:MARGIN], back[MARGIN + rows :]
        span = slice(side * MARGIN, (side + 1) * MARGIN)
        for_within[span] = jnp.where(odd, top, bottom).astype(jnp.bfloat16)
        edges[:MARGIN] = top.astype(jnp.bfloat16)
        edges[MARGIN:] = bottom.astype(jnp.bfloat16)
        center[side] = back[MARGIN : MARGIN + rows]


def back_projected(grads, wkv):
    rows, width, both = grads.shape
    channels = both // 2
    grads = jnp.concatenate(
        [grads[:, :, :channels] * channels**-0.5, grads[:, :, channels:]], axis=2
    ).astype(jnp.bfloat16)
    return dot_nt(grads.reshape(rows * width, both), wkv).reshape(rows, width, channels)


def third_kernel(
    scalars,
    probs,
    grad_scores,
    kv_t,
    first_kv_t,
    q_weight,
    attended,
    grad_own,
):
    rows, width, channels = attended.shape
    grad_q = []
    for b in range(rows):
        places = [places_of(scalars, rows, b, side) for side in range(2)]
        keys_t = jnp.concatenate(
            [kv_t[at] for at, _ in places[0]] + [first_kv_t[at] for at, _ in places[1]], axis=1
        )
        attended[b] = dot_nn(keys_t[channels:], probs[b]).T.astype(jnp.bfloat16)
        grad_q.append(dot_nn(keys_t[:channels], grad_scores[b]))
    grad_q = jnp.concatenate(grad_q, axis=1) * channels**-0.5
    turned = dot_nn(q_weight[...], grad_q.astype(jnp.bfloat16))
    for b in range(rows):
        grad_own[b] = turned[:, b * width : (b + 1) * width].T


def on_device(kernel, out_shape, scratch, flops, *arrays):
    smem = pl.BlockSpec(memory_space=pltpu.SMEM)
    vmem = pl.BlockSpec(memory_space=pltpu.VMEM)
    return pl.pallas_call(
        kernel,
        out_shape=tuple(jax.ShapeDtypeStruct(*one) for one in out_shape),
        in_specs=[smem if one.dtype == jnp.int32 else vmem for one in arrays],
        out_specs=tuple(smem if one[1] == jnp.int32 else vmem for one in out_shape),
        scratch_shapes=[pltpu.VMEM(*one) for one in scratch],
        compiler_params=pltpu.CompilerParams(vmem_limit_bytes=14 * 1024 * 1024),
        cost_estimate=pl.CostEstimate(
            flops=flops, bytes_accessed=flops // 1000, transcendentals=0
        ),
    )(*arrays)


def local(
    features_in,
    conv_weight,
    q_weight,
    k_weight,
    v_weight,
    partners,
    band_widths,
    bands,
    grad_attended,
):
    image = features_in[0]
    rows, width, channels = image.shape
    halo = MARGIN + 1
    win = rows + 2 * MARGIN
    half, full = jnp.bfloat16, jnp.float32
    views = lax.axis_size("cam")
    samples = views // min(16, views)
    ring = views // samples
    count = lax.axis_size("row")

    def routed(value, evens, odds):
        pairs = []
        for c in range(views):
            step = odds if (c // samples) % 2 else evens
            pairs.append((c, (c // samples + step) % ring * samples + c % samples))
        return lax.ppermute(value, "cam", pairs)

    camera = lax.axis_index("cam")
    slab = lax.axis_index("row")
    odd_place = (camera if samples == 1 else lax.div(camera, samples)) & 1
    odd_row = (slab & 1) == 1
    even_row = (slab & 1) == 0
    on = (2 - 4 * odd_place) * samples

    def around(place):
        return place & (views - 1) if views & (views - 1) == 0 else lax.rem(place + views, views)

    place, side = (lax.broadcasted_iota(jnp.int32, (views, 2), dim) for dim in range(2))
    near = (partners == around(place + (2 * side - 1) * samples)).astype(full)
    near = jnp.broadcast_to(near.reshape(2 * views, 1), (2 * views, channels))
    near = lax.optimization_barrier(near)

    def is_near(other, side):
        place = (2 * other + side, jnp.int32(0))
        row = lax.dynamic_slice(near, place, (1, channels), allow_negative_indices=False)
        return row[None] > 0.5

    def across(value, evens, odds):
        pairs = []
        for c in range(views):
            step = odds if (c // samples) % 2 else evens
            to = (c // samples + step) % ring * samples + c % samples
            for r in range(1, count - 1, 2):
                pairs += [(c * count + r, to * count + r + 1), (c * count + r + 1, to * count + r)]
        return lax.ppermute(value, ("cam", "row"), pairs)

    second_near = is_near(around(camera + on), odd_place)
    first_near = is_near(camera, odd_place ^ 1)
    first_near_back = is_near(around(camera - on), odd_place ^ 1)
    pair_slab = routed(image, 1, -1)
    far_slab = routed(image, -2, 2)
    passed_on = jnp.where(second_near, pair_slab, image)
    second_slab = routed(passed_on, 2, -2)
    second_between = across(
        jnp.where(odd_row, passed_on[rows - halo :], passed_on[:halo]), 2, -2
    )
    far_slab, _ = lax.optimization_barrier((far_slab, passed_on))
    first_slab = jnp.where(~first_near, far_slab, pair_slab)
    to_next = jnp.concatenate([first_slab[rows - halo :], image[rows - 1 :]])
    to_previous = jnp.concatenate([first_slab[:halo], image[:1]])
    for_between, for_within = parity_split(to_next, to_previous, odd_row)
    between, within = swap_between(for_between), swap_within(for_within)
    bands, band_widths, even_row, _ = lax.optimization_barrier(
        (bands, band_widths, even_row, for_between)
    )

    widths_here = lax.dynamic_slice(
        band_widths, (camera, 0), (1, 2), allow_negative_indices=False
    )[0]
    live = jnp.arange(BAND, dtype=jnp.int32)[None, :] < widths_here[:, None]
    places = jnp.clip(bands[0] - (slab * rows - MARGIN), 0, win - 1)
    live = jnp.where(odd_place == 1, live[::-1], live)
    places = jnp.where(odd_place == 1, places[:, ::-1], places)
    scalars = jnp.concatenate(
        [
            odd_row.astype(jnp.int32).reshape(1),
            places.reshape(-1),
            live.reshape(-1).astype(jnp.int32),
        ]
    )

    conv_scratch = [
        (((win + 2) * width, channels), half),
        ((win * width + 16, 3 * channels), full),
        ((win, width, 2 * channels), half),
        ((rows, 2 * width, 2 * channels), half),
    ]
    queries, first_kv_t, first_expo, first_grad_probs, taps, wkv = on_device(
        first_kernel,
        [
            (image.shape, half),
            ((win, 2 * channels, width), half),
            ((rows, BAND * width, width), full),
            ((rows, BAND * width, width), full),
            ((3 * channels, 3 * channels), half),
            ((channels, 2 * channels), half),
        ],
        conv_scratch,
        1_000_000,
        scalars,
        image,
        first_slab,
        within,
        between,
        conv_weight,
        q_weight,
        k_weight,
        v_weight,
        grad_attended[0],
    )
    second_within = swap_within(
        jnp.where(odd_row, second_slab[:halo], second_slab[rows - halo :])
    )
    margins = ((2 * MARGIN, width, channels), half)
    weights = ((rows, 2 * BAND * width, width), half)
    for_within, second_edges, first_edges, center, probs, grad_scores, kv_t = on_device(
        second_kernel,
        [
            ((2 * MARGIN, width, channels), half),
            margins,
            margins,
            ((2, rows, width, channels), full),
            weights,
            weights,
            ((win, 2 * channels, width), half),
        ],
        conv_scratch + [((2, win, width, 2 * channels), full)],
        1_500_000_000,
        scalars,
        queries,
        grad_attended[0],
        second_slab,
        second_within,
        second_between,
        taps,
        wkv,
        first_expo,
        first_grad_probs,
    )
    within = swap_within(for_within)

    def spread(part, onto_first):
        part = part.astype(full)
        none = jnp.zeros((rows - 2 * MARGIN, width, channels), full)
        return jnp.concatenate(
            [jnp.where(onto_first, part, 0.0), none, jnp.where(onto_first, 0.0, part)], axis=0
        )

    second = (center[0] + spread(within[:MARGIN], odd_row)).astype(half)
    from_second = routed(second, -2, 2)
    second_edges, first_edges, _ = lax.optimization_barrier((second_edges, first_edges, second))
    second_between = across(
        jnp.where(odd_row, second_edges[MARGIN:], second_edges[:MARGIN]), -2, 2
    )
    first_between = swap_between(
        jnp.where(odd_row, first_edges[MARGIN:], first_edges[:MARGIN])
    )
    attended, grad_own = on_device(
        third_kernel,
        [(image.shape, half), (image.shape, full)],
        [],
        1_000_000,
        scalars,
        probs,
        grad_scores,
        kv_t,
        first_kv_t,
        q_weight,
    )
    first = center[1] + spread(within[MARGIN:], odd_row) + spread(first_between, even_row)
    first = first.astype(half)
    from_first = routed(first, 2, -2)
    from_second, second_between, _, grad_own = lax.optimization_barrier(
        (from_second, second_between, first, grad_own)
    )
    from_second = from_second.astype(full) + spread(second_between, even_row)
    for_pair = jnp.where(first_near, first.astype(full), 0.0) + jnp.where(
        second_near, from_second, 0.0
    )
    from_pair = routed(for_pair.astype(half), 1, -1)
    summed = grad_own + from_pair.astype(full)
    summed = summed + jnp.where(second_near, 0.0, from_second)
    summed = summed + jnp.where(first_near_back, 0.0, from_first.astype(full))
    return (attended[None], summed.astype(half)[None])


def solution(mesh):
    placed = (
        P("cam", "row", None, None),
        P(),
        P(),
        P(),
        P(),
        P(),
        P(),
        P("cam", "row", None, None),
        P("cam", "row", None, None),
    )
    return jax.shard_map(
        local,
        mesh=mesh,
        in_specs=placed,
        out_specs=(P("cam", "row", None, None), P("cam", "row", None, None)),
        check_vma=False,
    )
```
